128 devices in a mesh: role: 4 (over y), dp: 32 (over x, z, core).
Axes of the slice: x: 4, y: 4, z: 4, core: 2. Of those that a mesh axis runs over, the one named last changes fastest.
Arguments:
- embedding_table: bfloat16 [131072, 128], P('dp'), may hold values from -0.796875 to 0.796875
- touched_blocks: int32 [32, 384, 16], P('dp', 'role'), may hold values from 0 to 511
- bag_index: int32 [32, 49152, 16], P('dp', 'role'), may hold values from 0 to 127
- bag_count: int32 [32, 49152, 16], P('dp', 'role'), may hold values from 0 to 3
- feature_map: int32 [32], replicated, may hold values from 0 to 31, each once
- labels: int32 [49152], P(('role', 'dp')), may hold values 0 or 1
- v_weight: bfloat16 [4096, 256], replicated, may hold values from -0.09375 to 0.09375
- u_weight: bfloat16 [256, 4096], replicated, may hold values from -0.375 to 0.375
- cross_bias: float32 [4096], replicated, may hold values from -3 to 3
- hidden_weight: bfloat16 [4096, 512], replicated, may hold values from -0.09375 to 0.09375
- hidden_bias: float32 [512], replicated, may hold values from -3 to 3
- out_weight: bfloat16 [512], replicated, may hold values from -0.25 to 0.25
Outputs:
- table_grad: float32 [131072, 128], P('dp')
- grad_v_weight: float32 [4096, 256], P(('role', 'dp'))
- grad_u_weight: float32 [256, 4096], P(None, ('role', 'dp'))
- grad_cross_bias: float32 [4096], P(('role', 'dp'))
- grad_hidden_weight: float32 [4096, 512], P(('role', 'dp'))
- grad_hidden_bias: float32 [512], P(('role', 'dp'))
- grad_out_weight: float32 [512], P(('role', 'dp'))
The draws below stay inside these ranges and needn't reach their ends.
All inputs are finite; a program needn't handle non-finite values. No bound on the sum of `labels` on one device may be relied on, other than what follows from the above.
Results may differ from the reference program's by a relative error of at most 0.015.
Values may be sent and summed in bfloat16 or wider, within the bound.
No kernel may reach another device: no remote copies, remote signals or barrier semaphores. Data moves between devices by JAX's collectives and lax.ppermute only.
A program may use at most 128 MiB of HBM per device.

```python
import jax
import jax.numpy as jnp
from jax import lax

E = 128
RANK = 256
H1 = 512
B_DEV = 384
ROWS_DEV = 4096
HOT = 16
ST = 128
TBLK = 16
BLK = 8
FEATURES = 32
INTER = 4096
SAMPLES = 49152
TILES = 384
TILE_ROWS = 128
N_ROLE = 4
N_DP = 32


def place_ends(entries, rng, low, top_value):
    shape = entries.shape
    spot = [jax.random.randint(jax.random.fold_in(rng, axis), (), 0, shape[axis]) for axis in range(len(shape))]
    entries = entries.at[tuple(spot)].set(low)
    longest = shape.index(max(shape))
    spot[longest] = (spot[longest] + 1) % shape[longest]
    return entries.at[tuple(spot)].set(top_value)


def levels(stream_key, extent, cuts, least, top_value):
    def one(dim, blocks):
        draws = jax.random.uniform(jax.random.fold_in(jax.random.fold_in(stream_key, 6), dim), (blocks,), jnp.float32, least / len(cuts), top_value / len(cuts))
        return jnp.repeat(jnp.exp(draws), extent[dim] // blocks).reshape((-1,) + (1,) * (len(extent) - dim - 1))

    loudness = one(*cuts[0])
    for cut in cuts[1:]:
        loudness = loudness * one(*cut)
    return loudness


def scatter_about(rng, dims, spread, limit, cuts=(), kind=jnp.bfloat16):
    array = spread * jax.random.normal(rng, dims, jnp.float32)
    if cuts:
        array = array * levels(rng, dims, cuts, -0.22, 0.18)
    return jnp.clip(array, -limit, limit).astype(kind)


def setup_inputs(seed: int = 0) -> dict:
    arg_keys = jax.random.split(jax.random.key(seed), 13)
    return {
        "embedding_table": scatter_about(arg_keys[0], (FEATURES * ROWS_DEV, E), 0.13, 0.796875, ((0, 32),)),
        "touched_blocks": place_ends(jax.random.randint(arg_keys[1], (FEATURES, TILES, TBLK), 0, ROWS_DEV // BLK), jax.random.fold_in(arg_keys[1], 1), 0, (ROWS_DEV // BLK) - 1).astype(jnp.int32),
        "bag_index": place_ends(jax.random.randint(arg_keys[2], (FEATURES, SAMPLES, HOT), 0, TILE_ROWS), jax.random.fold_in(arg_keys[2], 1), 0, TILE_ROWS - 1).astype(jnp.int32),
        "bag_count": place_ends(jax.random.randint(arg_keys[3], (FEATURES, SAMPLES, HOT), 0, 4), jax.random.fold_in(arg_keys[3], 1), 0, 3).astype(jnp.int32),
        "feature_map": jax.random.permutation(arg_keys[4], FEATURES).astype(jnp.int32),
        "labels": place_ends((jax.random.randint(arg_keys[5], (SAMPLES,), 0, 4) < 1).astype(jnp.int32), jax.random.fold_in(arg_keys[5], 1), 0, 1),
        "v_weight": scatter_about(arg_keys[6], (INTER, RANK), INTER ** -0.5, 0.09375),
        "u_weight": scatter_about(arg_keys[7], (RANK, INTER), RANK ** -0.5, 0.375),
        "cross_bias": scatter_about(arg_keys[8], (INTER,), 0.5, 3.0, (), jnp.float32),
        "hidden_weight": scatter_about(arg_keys[9], (INTER, H1), INTER ** -0.5, 0.09375),
        "hidden_bias": scatter_about(arg_keys[10], (H1,), 0.5, 3.0, (), jnp.float32),
        "out_weight": scatter_about(arg_keys[11], (H1,), H1 ** -0.5, 0.25),
    }


LOSS_SCALE = 65536.0


def incidence(index, count):
    columns = jnp.arange(TBLK * BLK, dtype=jnp.int32)
    hits = jnp.where(index[:, :, None] == columns[None, None, :], count[:, :, None], 0)
    return jnp.sum(hits, axis=1).astype(jnp.float32)


def pool_feature(pieces):
    shard_rows, touched, index, count = pieces
    tile_count = touched.shape[0]
    row_ids = (touched[:, :, None] * BLK + jnp.arange(BLK, dtype=jnp.int32)[None, None, :]).reshape(tile_count, TBLK * BLK)
    picked = shard_rows[row_ids].astype(jnp.float32)
    weights = incidence(index, count).reshape(tile_count, ST, TBLK * BLK)
    pooled = jnp.einsum("tnc,tce->tne", weights, picked).astype(jnp.bfloat16)
    return pooled.reshape(tile_count * ST, E), row_ids, weights


def dense_pass(interaction, label, params, total):
    v_weight, u_weight, cross_bias, hidden_weight, hidden_bias, out_weight = params
    low_rank = jnp.dot(interaction, v_weight, preferred_element_type=jnp.float32).astype(jnp.bfloat16)
    projected = jnp.dot(low_rank, u_weight, preferred_element_type=jnp.float32) + cross_bias
    inter_float = interaction.astype(jnp.float32)
    crossed = (inter_float * projected + inter_float).astype(jnp.bfloat16)
    hidden_pre = jnp.dot(crossed, hidden_weight, preferred_element_type=jnp.float32) + hidden_bias
    hidden_act = jax.nn.silu(hidden_pre).astype(jnp.bfloat16)
    logit = jnp.dot(hidden_act, out_weight, preferred_element_type=jnp.float32)
    d_logit = ((LOSS_SCALE / total) * (jax.nn.sigmoid(logit) - label.astype(jnp.float32))).astype(jnp.bfloat16)
    grad_out = jnp.dot(d_logit, hidden_act, preferred_element_type=jnp.float32)
    gate_sig = jax.nn.sigmoid(hidden_pre)
    slope_factor = gate_sig * (1.0 + hidden_pre * (1.0 - gate_sig))
    d_hidden = (d_logit.astype(jnp.float32)[:, None] * out_weight.astype(jnp.float32)[None, :] * slope_factor).astype(jnp.bfloat16)
    grad_hw = jnp.dot(crossed.T, d_hidden, preferred_element_type=jnp.float32)
    grad_hb = jnp.sum(d_hidden.astype(jnp.float32), axis=0)
    d_crossed = jnp.dot(d_hidden, hidden_weight.T, preferred_element_type=jnp.float32)
    d_proj = d_crossed * inter_float
    grad_cb = jnp.sum(d_proj, axis=0)
    d_proj_low = d_proj.astype(jnp.bfloat16)
    grad_u = jnp.dot(low_rank.T, d_proj_low, preferred_element_type=jnp.float32)
    low_grad = jnp.dot(d_proj_low, u_weight.T, preferred_element_type=jnp.float32).astype(jnp.bfloat16)
    grad_v = jnp.dot(interaction.T, low_grad, preferred_element_type=jnp.float32)
    d_inter = (d_crossed * (projected + 1.0) + jnp.dot(low_grad, v_weight.T, preferred_element_type=jnp.float32)).astype(jnp.bfloat16)
    return (grad_v, grad_u, grad_cb, grad_hw, grad_hb, grad_out), d_inter


def add_rows(shard_grad, row_ids, values):
    return shard_grad.at[row_ids.reshape(-1)].add(values.reshape(-1, E))


def reference(embedding_table, touched_blocks, bag_index, bag_count, feature_map, labels, v_weight, u_weight, cross_bias, hidden_weight, hidden_bias, out_weight):
    params = (v_weight, u_weight, cross_bias, hidden_weight, hidden_bias, out_weight)
    group_samples = N_DP * B_DEV
    group_tiles = group_samples // ST
    total = N_ROLE * group_samples
    shards = embedding_table.reshape(FEATURES, ROWS_DEV, E)
    slot_of = jnp.zeros((FEATURES,), jnp.int32).at[feature_map].set(jnp.arange(FEATURES, dtype=jnp.int32))
    table_grad = jnp.zeros((FEATURES, ROWS_DEV, E), jnp.float32)
    sums = None
    for member in range(N_ROLE):
        touched = touched_blocks[:, member * group_tiles:(member + 1) * group_tiles]
        index = bag_index[:, member * group_samples:(member + 1) * group_samples]
        count = bag_count[:, member * group_samples:(member + 1) * group_samples]
        pooled, row_ids, weights = lax.map(pool_feature, (shards, touched, index, count))
        interaction = jnp.transpose(pooled[slot_of], (1, 0, 2)).reshape(group_samples, INTER)
        label = labels[member * group_samples:(member + 1) * group_samples]
        grads, d_inter = dense_pass(interaction, label, params, total)
        sums = grads if sums is None else tuple(a + b for a, b in zip(sums, grads))
        d_pooled = jnp.transpose(d_inter.reshape(group_samples, FEATURES, E), (1, 0, 2))[feature_map]
        d_tiles = d_pooled.astype(jnp.float32).reshape(FEATURES, group_tiles, ST, E)
        tile_grad = jnp.einsum("ftnc,ftne->ftce", weights, d_tiles)
        table_grad = jax.vmap(add_rows)(table_grad, row_ids, tile_grad)
    return (table_grad.reshape(FEATURES * ROWS_DEV, E), sums[0], sums[1], sums[2], sums[3], sums[4], sums[5])
```

```python
import functools

import jax
import jax.numpy as jnp
from jax import lax
from jax.experimental import pallas as pl
from jax.experimental.pallas import tpu as pltpu
from jax.sharding import Mesh
from jax.sharding import PartitionSpec as P

BLK = 8
LOSS_SCALE = 65536.0
STEP_TILES = 8
WIDE = 512
EXTRA = 16

BF = jnp.bfloat16
F32 = jnp.float32


def nt(left, right):
    return lax.dot_general(left, right, (((1,), (1,)), ((), ())), preferred_element_type=F32)


def pool_kernel(touched, table, index, count, pooled, incidence, rows32):
    step = pl.program_id(0)
    tile = incidence.shape[1]

    @pl.when(step == 0)
    def _():
        rows32[...] = table[...].astype(F32)

    listed = lax.broadcasted_iota(jnp.int32, (tile, tile), 0).astype(BF)
    for i in range(STEP_TILES):
        t = step * STEP_TILES + i
        idx = index[:, i * tile : (i + 1) * tile].astype(BF)
        cnt = count[:, i * tile : (i + 1) * tile].astype(BF)
        total = jnp.zeros((tile, tile), BF)
        for j in range(index.shape[0]):
            total += jnp.where(idx[j : j + 1] == listed, cnt[j : j + 1], jnp.zeros((), BF))
        incidence[i] = total
        blocks = [
            rows32[pl.ds(pl.multiple_of(touched[k, t] * BLK, BLK), BLK), :]
            for k in range(touched.shape[0])
        ]
        picked = jnp.concatenate(blocks, axis=0).astype(BF)
        pooled[pl.ds(i * tile, tile), :] = lax.dot_general(
            total, picked, (((0,), (0,)), ((), ())), preferred_element_type=F32
        ).astype(BF)


def pool(touched, table, index, count, tile):
    hot, samples = index.shape
    tiles = samples // tile
    width = table.shape[1]
    span = STEP_TILES * tile
    return pl.pallas_call(
        pool_kernel,
        name="pool",
        grid_spec=pltpu.PrefetchScalarGridSpec(
            num_scalar_prefetch=1,
            grid=(tiles // STEP_TILES,),
            in_specs=[
                pl.BlockSpec(table.shape, lambda s, _: (0, 0)),
                pl.BlockSpec((hot, span), lambda s, _: (0, s)),
                pl.BlockSpec((hot, span), lambda s, _: (0, s)),
            ],
            out_specs=[
                pl.BlockSpec((span, width), lambda s, _: (s, 0)),
                pl.BlockSpec((STEP_TILES, tile, tile), lambda s, _: (s, 0, 0)),
            ],
            scratch_shapes=[pltpu.VMEM(table.shape, F32)],
        ),
        out_shape=[
            jax.ShapeDtypeStruct((samples, width), BF),
            jax.ShapeDtypeStruct((tiles, tile, tile), BF),
        ],
        compiler_params=pltpu.CompilerParams(vmem_limit_bytes=24 << 20),
    )(touched, table, index, count)


def scatter_kernel(touched, incidence, grad, out, *sums):
    step = pl.program_id(0)
    tile = incidence.shape[1]

    @pl.when(step == 0)
    def _():
        for acc in sums:
            acc[...] = jnp.zeros_like(acc)

    for i in range(STEP_TILES):
        t = step * STEP_TILES + i
        product = jnp.dot(
            incidence[i], grad[pl.ds(i * tile, tile), :], preferred_element_type=F32
        )
        for k in range(touched.shape[0]):
            acc = sums[k % len(sums)]
            rows = pl.ds(pl.multiple_of(touched[k, t] * BLK, BLK), BLK)
            acc[rows, :] += product[k * BLK : (k + 1) * BLK]

    @pl.when(step == pl.num_programs(0) - 1)
    def _():
        total = sums[0][...]
        for acc in sums[1:]:
            total = total + acc[...]
        out[...] = total.astype(out.dtype)


def scatter(touched, incidence, grad, rows):
    tiles, tile, _ = incidence.shape
    width = grad.shape[1]
    span = STEP_TILES * tile
    return pl.pallas_call(
        scatter_kernel,
        name="scatter",
        grid_spec=pltpu.PrefetchScalarGridSpec(
            num_scalar_prefetch=1,
            grid=(tiles // STEP_TILES,),
            in_specs=[
                pl.BlockSpec((STEP_TILES, tile, tile), lambda s, _: (s, 0, 0)),
                pl.BlockSpec((span, width), lambda s, _: (s, 0)),
            ],
            out_specs=pl.BlockSpec((rows, width), lambda s, _: (0, 0)),
            scratch_shapes=[pltpu.VMEM((rows, width), F32)] * 4,
        ),
        out_shape=jax.ShapeDtypeStruct((rows, width), BF),
        compiler_params=pltpu.CompilerParams(vmem_limit_bytes=24 << 20),
    )(touched, incidence, grad)


def dense_kernel(
    scale,
    fmap,
    received,
    labels,
    v_hbm,
    u_hbm,
    cross_bias,
    h_hbm,
    hidden_bias,
    out_weight,
    back,
    inter_out,
    crossed_out,
    proj_out,
    low_out,
    low_grad_out,
    d_hidden_out,
    cross_bias_grad,
    hidden_bias_grad,
    out_weight_grad,
    inter,
    crossed,
    proj_low,
    held,
    d_inter,
    v,
    u,
    h,
    hidden,
    low_sum,
    slot_of,
    in_sems,
    weight_sems,
    out_sems,
    back_sems,
):
    features, batch, width = received.shape
    total_width = features * width
    blocks = total_width // WIDE
    per_block = WIDE // width

    loads = []
    for s in range(features):
        cols = pl.ds(pl.multiple_of(fmap[s] * width, width), width)
        copy = pltpu.make_async_copy(received.at[s], inter.at[:, cols], in_sems.at[s])
        copy.start()
        loads.append(copy)
    weights = [
        pltpu.make_async_copy(source, target, weight_sems.at[i])
        for i, (source, target) in enumerate(((v_hbm, v), (u_hbm, u), (h_hbm, h)))
    ]
    for copy in weights:
        copy.start()
    for s in range(features):
        slot_of[fmap[s]] = s
    low_sum[...] = jnp.zeros_like(low_sum)
    hidden[...] = jnp.broadcast_to(hidden_bias[...], hidden.shape)
    for copy in loads:
        copy.wait()
    inter_copy = pltpu.make_async_copy(inter, inter_out, out_sems.at[0])
    inter_copy.start()
    weights[0].wait()

    @pl.loop(0, blocks)
    def _(b):
        cols = pl.ds(pl.multiple_of(b * WIDE, WIDE), WIDE)
        low_sum[...] += jnp.dot(inter[:, cols], v[cols, :], preferred_element_type=F32)

    low_out[...] = low_sum[...].astype(BF)
    weights[1].wait()
    weights[2].wait()

    @pl.loop(0, blocks)
    def _(b):
        cols = pl.ds(pl.multiple_of(b * WIDE, WIDE), WIDE)
        projected = (
            jnp.dot(low_out[...], u[:, cols], preferred_element_type=F32) + cross_bias[:, cols]
        )
        held[:, cols] = projected
        x = inter[:, cols].astype(F32)
        product = (x * projected + x).astype(BF)
        crossed[:, cols] = product
        hidden[...] += jnp.dot(product, h[cols, :], preferred_element_type=F32)

    crossed_copy = pltpu.make_async_copy(crossed, crossed_out, out_sems.at[1])
    crossed_copy.start()
    hidden_bias_grad[...] = jnp.zeros_like(hidden_bias_grad)
    out_weight_grad[...] = jnp.zeros_like(out_weight_grad)
    chunk = 64

    @pl.loop(0, batch // chunk)
    def _(r):
        rows = pl.ds(pl.multiple_of(r * chunk, chunk), chunk)
        pre = hidden[rows, :]
        gate = jax.nn.sigmoid(pre)
        act = (pre * gate).astype(BF).astype(F32)
        weight = out_weight[...].astype(F32)
        logit = jnp.sum(act * weight, axis=1, keepdims=True)
        d_logit = (scale * (jax.nn.sigmoid(logit) - labels[rows, :].astype(F32))).astype(BF)
        d_logit = d_logit.astype(F32)
        d_hidden = (d_logit * weight * (gate * (1.0 + pre * (1.0 - gate)))).astype(BF)
        d_hidden_out[rows, :] = d_hidden
        hidden_bias_grad[...] += jnp.sum(d_hidden.astype(F32), axis=0, keepdims=True)
        out_weight_grad[...] += jnp.sum(d_logit * act, axis=0, keepdims=True)

    low_sum[...] = jnp.zeros_like(low_sum)

    @pl.loop(0, blocks)
    def _(b):
        cols = pl.ds(pl.multiple_of(b * WIDE, WIDE), WIDE)
        d_crossed = nt(d_hidden_out[...], h[cols, :])
        d_proj = d_crossed * inter[:, cols].astype(F32)
        cross_bias_grad[:, cols] = jnp.sum(d_proj, axis=0, keepdims=True)
        rounded = d_proj.astype(BF)
        proj_low[:, cols] = rounded
        low_sum[...] += nt(rounded, u[:, cols])
        held[:, cols] = d_crossed * (held[:, cols] + 1.0)

    proj_copy = pltpu.make_async_copy(proj_low, proj_out, out_sems.at[2])
    proj_copy.start()
    low_grad_out[...] = low_sum[...].astype(BF)
    stores = []
    for b in range(blocks):
        cols = pl.ds(b * WIDE, WIDE)
        d_inter[:, cols] = (held[:, cols] + nt(low_grad_out[...], v[cols, :])).astype(BF)
        for i in range(per_block):
            f = b * per_block + i
            copy = pltpu.make_async_copy(
                d_inter.at[:, pl.ds(f * width, width)], back.at[slot_of[f]], back_sems.at[f]
            )
            copy.start()
            stores.append(copy)
    for copy in stores:
        copy.wait()
    inter_copy.wait()
    crossed_copy.wait()
    proj_copy.wait()


def dense(fmap, received, labels, v, u, cross_bias, h, hidden_bias, out_weight, scale):
    features, batch, width = received.shape
    total_width = features * width
    rank = v.shape[1]
    units = h.shape[1]
    vmem = pl.BlockSpec(memory_space=pltpu.VMEM)
    smem = pl.BlockSpec(memory_space=pltpu.SMEM)
    hbm = pl.BlockSpec(memory_space=pl.ANY)
    wide = jax.ShapeDtypeStruct((batch, total_width), BF)
    return pl.pallas_call(
        functools.partial(dense_kernel, scale),
        name="dense",
        in_specs=[smem, hbm, vmem, hbm, hbm, vmem, hbm, vmem, vmem],
        out_specs=[hbm, hbm, hbm, hbm, vmem, vmem, vmem, vmem, vmem, vmem],
        out_shape=[
            jax.ShapeDtypeStruct(received.shape, BF),
            wide,
            wide,
            wide,
            jax.ShapeDtypeStruct((batch, rank), BF),
            jax.ShapeDtypeStruct((batch, rank), BF),
            jax.ShapeDtypeStruct((batch, units), BF),
            jax.ShapeDtypeStruct((1, total_width), F32),
            jax.ShapeDtypeStruct((1, units), F32),
            jax.ShapeDtypeStruct((1, units), F32),
        ],
        scratch_shapes=[
            pltpu.VMEM((batch, total_width), BF),
            pltpu.VMEM((batch, total_width), BF),
            pltpu.VMEM((batch, total_width), BF),
            pltpu.VMEM((batch, total_width), F32),
            pltpu.VMEM((batch, total_width), BF),
            pltpu.VMEM(v.shape, BF),
            pltpu.VMEM(u.shape, BF),
            pltpu.VMEM(h.shape, BF),
            pltpu.VMEM((batch, units), F32),
            pltpu.VMEM((batch, rank), F32),
            pltpu.SMEM((features,), jnp.int32),
            pltpu.SemaphoreType.DMA((features,)),
            pltpu.SemaphoreType.DMA((3,)),
            pltpu.SemaphoreType.DMA((3,)),
            pltpu.SemaphoreType.DMA((features,)),
        ],
        compiler_params=pltpu.CompilerParams(vmem_limit_bytes=48 << 20),
    )(fmap, received, labels, v, u, cross_bias, h, hidden_bias, out_weight)


def gradients_kernel(
    core, inter, crossed, proj, low, low_grad, d_hidden, extra, keep, send, low_t, low_grad_t, d_hidden_t
):
    @pl.when(pl.program_id(0) == 0)
    def _():
        low_t[...] = low[...].astype(F32).T.astype(BF)
        low_grad_t[...] = low_grad[...].astype(F32).T.astype(BF)
        d_hidden_t[...] = d_hidden[...].astype(F32).T.astype(BF)

    first = core[0] == 0
    rank = low_t.shape[0]
    features, _, _, width = keep.shape
    of_v = jnp.dot(low_grad_t[...], inter[...], preferred_element_type=F32).astype(BF)
    of_u = jnp.dot(low_t[...], proj[...], preferred_element_type=F32).astype(BF)
    of_h = jnp.dot(d_hidden_t[...], crossed[...], preferred_element_type=F32).astype(BF)
    nothing = jnp.zeros((EXTRA, width), BF)

    def fill(one, other):
        for i in range(features):
            lanes = slice(i * width, (i + 1) * width)
            one[i, 0, pl.ds(0, rank), :] = of_v[:, lanes]
            one[i, 0, pl.ds(rank, EXTRA), :] = extra[i]
            one[i, 1, pl.ds(0, rank), :] = of_u[:, lanes]
            one[i, 1, pl.ds(rank, EXTRA), :] = nothing
            other[i, 0, pl.ds(0, rank), :] = of_h[:rank, lanes]
            other[i, 0, pl.ds(rank, EXTRA), :] = nothing
            other[i, 1, pl.ds(0, rank), :] = of_h[rank:, lanes]
            other[i, 1, pl.ds(rank, EXTRA), :] = nothing

    @pl.when(first)
    def _():
        fill(keep, send)

    @pl.when(jnp.logical_not(first))
    def _():
        fill(send, keep)


def gradients(core, inter, crossed, proj, low, low_grad, d_hidden, extra, width):
    batch, total_width = inter.shape
    rank, units = low.shape[1], d_hidden.shape[1]
    features = total_width // width
    pair = 2
    wide = pl.BlockSpec((batch, pair * width), lambda s, _: (0, s))
    half = jax.ShapeDtypeStruct((features, 2, rank + EXTRA, width), BF)
    half_spec = pl.BlockSpec((pair, 2, rank + EXTRA, width), lambda s, _: (s, 0, 0, 0))
    return pl.pallas_call(
        gradients_kernel,
        name="gradients",
        grid_spec=pltpu.PrefetchScalarGridSpec(
            num_scalar_prefetch=1,
            grid=(features // pair,),
            in_specs=[
                wide,
                wide,
                wide,
                pl.BlockSpec((batch, rank), lambda s, _: (0, 0)),
                pl.BlockSpec((batch, rank), lambda s, _: (0, 0)),
                pl.BlockSpec((batch, units), lambda s, _: (0, 0)),
                pl.BlockSpec((pair, EXTRA, width), lambda s, _: (s, 0, 0)),
            ],
            out_specs=[half_spec, half_spec],
            scratch_shapes=[
                pltpu.VMEM((rank, batch), BF),
                pltpu.VMEM((rank, batch), BF),
                pltpu.VMEM((units, batch), BF),
            ],
        ),
        out_shape=[half, half],
        compiler_params=pltpu.CompilerParams(vmem_limit_bytes=24 << 20),
        cost_estimate=pl.CostEstimate(
            flops=2 * batch * total_width * (2 * rank + units),
            bytes_accessed=18 << 20,
            transcendentals=0,
        ),
    )(core, inter, crossed, proj, low, low_grad, d_hidden, extra)


def body(
    embedding_table,
    touched_blocks,
    bag_index,
    bag_count,
    feature_map,
    labels,
    v_weight,
    u_weight,
    cross_bias,
    hidden_weight,
    hidden_bias,
    out_weight,
):
    dp = ("x", "zh", "zl", "core")
    features = feature_map.shape[0]
    rows, width = embedding_table.shape
    samples = bag_index.shape[1]
    tile = samples // touched_blocks.shape[1]
    batch = labels.shape[0]
    rank = v_weight.shape[1]
    units = hidden_weight.shape[1]
    roles = lax.axis_size("role")
    total = roles * lax.axis_size(dp) * batch
    core = lax.axis_index("core")

    touched = touched_blocks[0].T
    pooled, incidence = pool(touched, embedding_table, bag_index[0].T, bag_count[0].T, tile)
    received = lax.all_to_all(
        pooled.reshape(features, batch, width), dp, split_axis=0, concat_axis=0, tiled=True
    )
    back, inter, crossed, proj, low, low_grad, d_hidden, cross_g, hidden_g, out_g = dense(
        feature_map,
        received,
        labels.reshape(batch, 1),
        v_weight,
        u_weight,
        cross_bias.reshape(1, -1),
        hidden_weight,
        hidden_bias.reshape(1, -1),
        out_weight.reshape(1, -1),
        LOSS_SCALE / total,
    )
    returned = lax.all_to_all(back, dp, split_axis=0, concat_axis=0, tiled=True)

    quarters = 4
    share = width // quarters
    per = units // (features * quarters)

    def spread(values):
        values = values.reshape(features, quarters, per)
        return jnp.pad(values, ((0, 0), (0, 0), (0, share - per))).reshape(features, 1, width)

    extra = jnp.concatenate(
        [cross_g.reshape(features, 1, width), spread(hidden_g), spread(out_g)], axis=1
    )
    extra = jnp.pad(extra, ((0, 0), (0, EXTRA - 3), (0, 0))).astype(BF)
    keep, send = gradients(
        core.reshape(1), inter, crossed, proj, low, low_grad, d_hidden, extra, width
    )
    other = lax.ppermute(send, "core", [(0, 1), (1, 0)])
    chip_sum = (keep.astype(F32) + other.astype(F32)).astype(BF)
    role_sum = lax.psum_scatter(chip_sum, "role", scatter_dimension=0, tiled=True)
    pieces = lax.all_to_all(
        role_sum.reshape(features // roles * 2, rank + EXTRA, width),
        ("x", "zh", "zl"),
        split_axis=0,
        concat_axis=0,
        tiled=True,
    )
    piece = jnp.sum(pieces.astype(F32), axis=0)
    shares = lax.all_to_all(piece.T, ("zl", "core"), split_axis=0, concat_axis=0, tiled=True)
    shares = shares.reshape(quarters, share, rank + EXTRA)
    grad_v = shares[0, :, :rank]
    grad_u = shares[2, :, :rank].T
    grad_h = jnp.concatenate([shares[1, :, :rank], shares[3, :, :rank]], axis=1)
    grad_cb = shares[0, :, rank]
    grad_hb = shares[0, :per, rank + 1]
    grad_ow = shares[0, :per, rank + 2]

    local = scatter(touched, incidence, returned.reshape(samples, width), rows)
    parts = lax.all_to_all(
        local.reshape(roles, rows // roles, width), "role", split_axis=0, concat_axis=0, tiled=True
    )
    part = jnp.sum(parts.astype(F32), axis=0).astype(BF)
    table_grad = lax.all_gather(part, "role", axis=0, tiled=True).astype(F32)
    return (table_grad, grad_v, grad_u, grad_cb, grad_h, grad_hb, grad_ow)


def solution(mesh):
    fine = Mesh(mesh.devices.reshape(4, 4, 2, 2, 2), ("role", "x", "zh", "zl", "core"))
    dp = ("x", "zh", "zl", "core")
    everywhere = ("role",) + dp
    return jax.shard_map(
        body,
        mesh=fine,
        in_specs=(
            P(dp, None),
            P(dp, "role", None),
            P(dp, "role", None),
            P(dp, "role", None),
            P(),
            P(everywhere),
            P(),
            P(),
            P(),
            P(),
            P(),
            P(),
        ),
        out_specs=(
            P(dp, None),
            P(everywhere, None),
            P(None, everywhere),
            P(everywhere),
            P(everywhere, None),
            P(everywhere),
            P(everywhere),
        ),
        check_vma=False,
    )
```

```python
import functools

import jax
import jax.numpy as jnp
from jax import lax
from jax.experimental import pallas as pl
from jax.experimental.pallas import tpu as pltpu
from jax.sharding import Mesh
from jax.sharding import PartitionSpec as P

BLK = 8
LOSS_SCALE = 65536.0
STEP_TILES = 8
WIDE = 512
EXTRA = 16
ORDER = (2, 1, 3, 0)
VMEM = 60 << 20

BF = jnp.bfloat16
F32 = jnp.float32


def nt(left, right):
    return lax.dot_general(left, right, (((1,), (1,)), ((), ())), preferred_element_type=F32)


def pool_kernel(touched, table, index, count, pooled, incidence, rows32):
    step = pl.program_id(0)
    tile = incidence.shape[1]

    @pl.when(step == 0)
    def _():
        rows32[...] = table[...].astype(F32)

    listed = lax.broadcasted_iota(jnp.int32, (tile, tile), 0).astype(BF)
    for i in range(STEP_TILES):
        t = step * STEP_TILES + i
        idx = index[:, i * tile : (i + 1) * tile].astype(BF)
        cnt = count[:, i * tile : (i + 1) * tile].astype(BF)
        total = jnp.zeros((tile, tile), BF)
        for j in range(index.shape[0]):
            total += jnp.where(idx[j : j + 1] == listed, cnt[j : j + 1], jnp.zeros((), BF))
        incidence[i] = total
        blocks = [
            rows32[pl.ds(pl.multiple_of(touched[k, t] * BLK, BLK), BLK), :]
            for k in range(touched.shape[0])
        ]
        picked = jnp.concatenate(blocks, axis=0).astype(BF)
        pooled[pl.ds(i * tile, tile), :] = lax.dot_general(
            total, picked, (((0,), (0,)), ((), ())), preferred_element_type=F32
        ).astype(BF)


def pool(touched, table, index, count, tile):
    hot, samples = index.shape
    tiles = samples // tile
    width = table.shape[1]
    span = STEP_TILES * tile
    return pl.pallas_call(
        pool_kernel,
        name="pool",
        grid_spec=pltpu.PrefetchScalarGridSpec(
            num_scalar_prefetch=1,
            grid=(tiles // STEP_TILES,),
            in_specs=[
                pl.BlockSpec(table.shape, lambda s, _: (0, 0)),
                pl.BlockSpec((hot, span), lambda s, _: (0, s)),
                pl.BlockSpec((hot, span), lambda s, _: (0, s)),
            ],
            out_specs=[
                pl.BlockSpec((span, width), lambda s, _: (s, 0)),
                pl.BlockSpec((STEP_TILES, tile, tile), lambda s, _: (s, 0, 0)),
            ],
            scratch_shapes=[pltpu.VMEM(table.shape, F32)],
        ),
        out_shape=[
            jax.ShapeDtypeStruct((samples, width), BF),
            jax.ShapeDtypeStruct((tiles, tile, tile), BF),
        ],
        compiler_params=pltpu.CompilerParams(vmem_limit_bytes=VMEM),
    )(touched, table, index, count)


def scatter_kernel(touched, role, incidence, grad, out, *scratch):
    sums, (tiles_in, grads_in, tile_sems, grad_sems) = scratch[:-4], scratch[-4:]
    tiles, tile, _ = incidence.shape
    chunks, rows, _ = out.shape
    steps = tiles // STEP_TILES

    def loads(step):
        part = pl.ds(step * STEP_TILES, STEP_TILES)
        span = pl.ds(step * STEP_TILES * tile, STEP_TILES * tile)
        return (
            pltpu.make_async_copy(incidence.at[part], tiles_in.at[part], tile_sems.at[step]),
            pltpu.make_async_copy(grad.at[span], grads_in.at[span], grad_sems.at[step]),
        )

    for step in range(steps):
        for copy in loads(step):
            copy.start()
    for acc in sums:
        acc[...] = jnp.zeros_like(acc)

    @pl.loop(0, steps)
    def _(step):
        for copy in loads(step):
            copy.wait()
        for i in range(STEP_TILES):
            t = step * STEP_TILES + i
            product = jnp.dot(
                tiles_in[t], grads_in[pl.ds(t * tile, tile), :], preferred_element_type=F32
            )
            for k in range(touched.shape[0]):
                acc = sums[k % len(sums)]
                place = pl.ds(pl.multiple_of(touched[k, t] * BLK, BLK), BLK)
                acc[place, :] += product[k * BLK : (k + 1) * BLK]

    for i, offset in enumerate(ORDER):
        first = lax.rem(role[0] + offset, chunks) * rows
        place = pl.ds(pl.multiple_of(first, rows), rows)
        total = sums[0][place, :]
        for acc in sums[1:]:
            total = total + acc[place, :]
        out[i] = total.astype(out.dtype)


def scatter(touched, role, incidence, grad, rows, chunks):
    tiles, tile, _ = incidence.shape
    width = grad.shape[1]
    steps = tiles // STEP_TILES
    smem = pl.BlockSpec(memory_space=pltpu.SMEM)
    hbm = pl.BlockSpec(memory_space=pltpu.HBM)
    return pl.pallas_call(
        scatter_kernel,
        name="scatter",
        in_specs=[smem, smem, hbm, hbm],
        out_specs=pl.BlockSpec(memory_space=pltpu.VMEM),
        out_shape=jax.ShapeDtypeStruct((chunks, rows // chunks, width), BF),
        scratch_shapes=[pltpu.VMEM((rows, width), F32)] * 4
        + [
            pltpu.VMEM(incidence.shape, BF),
            pltpu.VMEM(grad.shape, BF),
            pltpu.SemaphoreType.DMA((steps,)),
            pltpu.SemaphoreType.DMA((steps,)),
        ],
        compiler_params=pltpu.CompilerParams(vmem_limit_bytes=VMEM),
        cost_estimate=pl.CostEstimate(flops=1 << 33, bytes_accessed=8 << 20, transcendentals=0),
    )(touched, role, incidence, grad)


def spread_kernel(role, own, following, opposite_a, opposite_b, preceding, out):
    rows = own.shape[0]
    half = rows // 2
    chunks = out.shape[0] // rows

    def place(offset, size, piece):
        first = lax.rem(role[0] + offset, chunks) * rows
        out[pl.ds(pl.multiple_of(first, rows) + size, piece.shape[0]), :] = piece[...].astype(F32)

    place(0, 0, own)
    place(1, 0, following)
    place(2, 0, opposite_a)
    place(2, half, opposite_b)
    place(3, 0, preceding)


def spread_rows(role, pieces, chunks):
    rows, width = pieces[0].shape
    vmem = pl.BlockSpec(memory_space=pltpu.VMEM)
    return pl.pallas_call(
        spread_kernel,
        name="spread_rows",
        in_specs=[pl.BlockSpec(memory_space=pltpu.SMEM)] + [vmem] * 5,
        out_specs=vmem,
        out_shape=jax.ShapeDtypeStruct((chunks * rows, width), F32),
        compiler_params=pltpu.CompilerParams(vmem_limit_bytes=16 << 20),
    )(role, *pieces)


def dense_kernel(
    scale,
    fmap,
    received,
    labels,
    v_hbm,
    u_hbm,
    cross_bias,
    h_hbm,
    hidden_bias,
    out_weight,
    back,
    crossed_out,
    proj_out,
    low_out,
    low_grad_out,
    d_hidden_out,
    cross_bias_grad,
    hidden_bias_grad,
    out_weight_grad,
    slot_of,
    inter,
    crossed,
    proj_low,
    held,
    d_inter,
    v,
    u,
    h,
    hidden,
    low_sum,
    in_sems,
    weight_sems,
    crossed_sems,
    proj_sems,
    back_sems,
):
    features, batch, width = received.shape
    total_width = features * width
    blocks = total_width // WIDE
    per_block = WIDE // width

    loads = []
    for s in range(features):
        cols = pl.ds(pl.multiple_of(fmap[s] * width, width), width)
        copy = pltpu.make_async_copy(received.at[s], inter.at[:, cols], in_sems.at[s])
        copy.start()
        loads.append(copy)
    weights = [
        pltpu.make_async_copy(source, target, weight_sems.at[i])
        for i, (source, target) in enumerate(((v_hbm, v), (u_hbm, u), (h_hbm, h)))
    ]
    for copy in weights:
        copy.start()
    for s in range(features):
        slot_of[fmap[s]] = s
    low_sum[...] = jnp.zeros_like(low_sum)
    hidden[...] = jnp.broadcast_to(hidden_bias[...], hidden.shape)
    for copy in loads:
        copy.wait()
    weights[0].wait()

    @pl.loop(0, blocks)
    def _(b):
        cols = pl.ds(pl.multiple_of(b * WIDE, WIDE), WIDE)
        low_sum[...] += jnp.dot(inter[:, cols], v[cols, :], preferred_element_type=F32)

    low_out[...] = low_sum[...].astype(BF)
    weights[1].wait()
    weights[2].wait()

    @pl.loop(0, blocks)
    def _(b):
        cols = pl.ds(pl.multiple_of(b * WIDE, WIDE), WIDE)
        projected = (
            jnp.dot(low_out[...], u[:, cols], preferred_element_type=F32) + cross_bias[:, cols]
        )
        held[:, cols] = projected
        x = inter[:, cols].astype(F32)
        product = (x * projected + x).astype(BF)
        crossed[:, cols] = product
        hidden[...] += jnp.dot(product, h[cols, :], preferred_element_type=F32)

    stores = []

    def store(source, f, target, sem):
        copy = pltpu.make_async_copy(source.at[:, pl.ds(f * width, width)], target, sem)
        copy.start()
        stores.append(copy)

    for f in range(features):
        store(crossed, f, crossed_out.at[f], crossed_sems.at[f])
    hidden_bias_grad[...] = jnp.zeros_like(hidden_bias_grad)
    out_weight_grad[...] = jnp.zeros_like(out_weight_grad)
    chunk = 64

    @pl.loop(0, batch // chunk)
    def _(r):
        rows = pl.ds(pl.multiple_of(r * chunk, chunk), chunk)
        pre = hidden[rows, :]
        gate = jax.nn.sigmoid(pre)
        act = (pre * gate).astype(BF).astype(F32)
        weight = out_weight[...].astype(F32)
        logit = jnp.sum(act * weight, axis=1, keepdims=True)
        d_logit = (scale * (jax.nn.sigmoid(logit) - labels[rows, :].astype(F32))).astype(BF)
        d_logit = d_logit.astype(F32)
        d_hidden = (d_logit * weight * (gate * (1.0 + pre * (1.0 - gate)))).astype(BF)
        d_hidden_out[rows, :] = d_hidden
        hidden_bias_grad[...] += jnp.sum(d_hidden.astype(F32), axis=0, keepdims=True)
        out_weight_grad[...] += jnp.sum(d_logit * act, axis=0, keepdims=True)

    low_sum[...] = jnp.zeros_like(low_sum)

    @pl.loop(0, blocks)
    def _(b):
        cols = pl.ds(pl.multiple_of(b * WIDE, WIDE), WIDE)
        d_crossed = nt(d_hidden_out[...], h[cols, :])
        d_proj = d_crossed * inter[:, cols].astype(F32)
        cross_bias_grad[:, cols] = jnp.sum(d_proj, axis=0, keepdims=True)
        rounded = d_proj.astype(BF)
        proj_low[:, cols] = rounded
        low_sum[...] += nt(rounded, u[:, cols])
        held[:, cols] = d_crossed * (held[:, cols] + 1.0)

    for f in range(features):
        store(proj_low, f, proj_out.at[f], proj_sems.at[f])
    low_grad_out[...] = low_sum[...].astype(BF)
    for b in range(blocks):
        cols = pl.ds(b * WIDE, WIDE)
        d_inter[:, cols] = (held[:, cols] + nt(low_grad_out[...], v[cols, :])).astype(BF)
        for i in range(per_block):
            f = b * per_block + i
            store(d_inter, f, back.at[slot_of[f]], back_sems.at[f])
    for copy in stores:
        copy.wait()


def dense(fmap, received, labels, v, u, cross_bias, h, hidden_bias, out_weight, scale):
    features, batch, width = received.shape
    total_width = features * width
    rank = v.shape[1]
    units = h.shape[1]
    vmem = pl.BlockSpec(memory_space=pltpu.VMEM)
    smem = pl.BlockSpec(memory_space=pltpu.SMEM)
    hbm = pl.BlockSpec(memory_space=pltpu.HBM)
    return pl.pallas_call(
        functools.partial(dense_kernel, scale),
        name="dense",
        in_specs=[smem, hbm, vmem, hbm, hbm, vmem, hbm, vmem, vmem],
        out_specs=[hbm, hbm, hbm, vmem, vmem, vmem, vmem, vmem, vmem, smem],
        out_shape=[
            jax.ShapeDtypeStruct(received.shape, BF),
            jax.ShapeDtypeStruct(received.shape, BF),
            jax.ShapeDtypeStruct(received.shape, BF),
            jax.ShapeDtypeStruct((batch, rank), BF),
            jax.ShapeDtypeStruct((batch, rank), BF),
            jax.ShapeDtypeStruct((batch, units), BF),
            jax.ShapeDtypeStruct((1, total_width), F32),
            jax.ShapeDtypeStruct((1, units), F32),
            jax.ShapeDtypeStruct((1, units), F32),
            jax.ShapeDtypeStruct((features,), jnp.int32),
        ],
        scratch_shapes=[
            pltpu.VMEM((batch, total_width), BF),
            pltpu.VMEM((batch, total_width), BF),
            pltpu.VMEM((batch, total_width), BF),
            pltpu.VMEM((batch, total_width), F32),
            pltpu.VMEM((batch, total_width), BF),
            pltpu.VMEM(v.shape, BF),
            pltpu.VMEM(u.shape, BF),
            pltpu.VMEM(h.shape, BF),
            pltpu.VMEM((batch, units), F32),
            pltpu.VMEM((batch, rank), F32),
            pltpu.SemaphoreType.DMA((features,)),
            pltpu.SemaphoreType.DMA((3,)),
            pltpu.SemaphoreType.DMA((features,)),
            pltpu.SemaphoreType.DMA((features,)),
            pltpu.SemaphoreType.DMA((features,)),
        ],
        compiler_params=pltpu.CompilerParams(vmem_limit_bytes=VMEM),
    )(fmap, received, labels, v, u, cross_bias, h, hidden_bias, out_weight)


def gradients_kernel(
    place,
    slot_of,
    inter_a,
    inter_b,
    crossed,
    proj,
    low,
    low_grad,
    d_hidden,
    extra,
    *rest,
):
    outs, (low_t, low_grad_t, d_hidden_t) = rest[:-3], rest[-3:]
    parts = len(ORDER)
    @pl.when(pl.program_id(0) == 0)
    def _():
        low_t[...] = low[...].astype(F32).T.astype(BF)
        low_grad_t[...] = low_grad[...].astype(F32).T.astype(BF)
        d_hidden_t[...] = d_hidden[...].astype(F32).T.astype(BF)

    rank = low_t.shape[0]
    features, _, _, width = outs[0].shape
    x = jnp.concatenate([inter_a[0], inter_b[0]], axis=1)
    c = jnp.concatenate([crossed[0], crossed[1]], axis=1)
    p = jnp.concatenate([proj[0], proj[1]], axis=1)
    of_v = jnp.dot(low_grad_t[...], x, preferred_element_type=F32).astype(BF)
    of_u = jnp.dot(low_t[...], p, preferred_element_type=F32).astype(BF)
    of_h = jnp.dot(d_hidden_t[...], c, preferred_element_type=F32).astype(BF)
    nothing = jnp.zeros((EXTRA, width), BF)

    def fill(one, other):
        for i in range(features):
            lanes = slice(i * width, (i + 1) * width)
            one[i, 0, pl.ds(0, rank), :] = of_v[:, lanes]
            one[i, 0, pl.ds(rank, EXTRA), :] = extra[i]
            one[i, 1, pl.ds(0, rank), :] = of_u[:, lanes]
            one[i, 1, pl.ds(rank, EXTRA), :] = nothing
            other[i, 0, pl.ds(0, rank), :] = of_h[:rank, lanes]
            other[i, 0, pl.ds(rank, EXTRA), :] = nothing
            other[i, 1, pl.ds(0, rank), :] = of_h[rank:, lanes]
            other[i, 1, pl.ds(rank, EXTRA), :] = nothing

    share = pl.num_programs(0) // parts
    first = place[0] == 0
    for part in range(parts):
        now = pl.program_id(0) // share == part

        @pl.when(jnp.logical_and(now, first))
        def _(part=part):
            fill(outs[part], outs[parts + part])

        @pl.when(jnp.logical_and(now, jnp.logical_not(first)))
        def _(part=part):
            fill(outs[parts + part], outs[part])


def gradients(place, slot_of, received, crossed, proj, low, low_grad, d_hidden, extra):
    features, batch, width = received.shape
    rank, units = low.shape[1], d_hidden.shape[1]
    pair = 2
    pairs = features // pair
    share = pairs // len(ORDER)

    def pair_of(s, place):
        part = s // share
        offset = jnp.where(part == 0, ORDER[0], jnp.where(part == 1, ORDER[1], 0))
        offset = jnp.where(part == 2, ORDER[2], offset)
        return lax.rem(place[1] + offset, len(ORDER)) * share + lax.rem(s, share)

    one = pl.BlockSpec((1, batch, width), lambda s, a, m: (m[pair_of(s, a) * pair], 0, 0))
    two = pl.BlockSpec((1, batch, width), lambda s, a, m: (m[pair_of(s, a) * pair + 1], 0, 0))
    both = pl.BlockSpec((pair, batch, width), lambda s, a, m: (pair_of(s, a), 0, 0))
    part = jax.ShapeDtypeStruct((features // len(ORDER), 2, rank + EXTRA, width), BF)

    def part_spec(i):
        return pl.BlockSpec(
            (pair, 2, rank + EXTRA, width),
            lambda s, a, m: (jnp.clip(s - i * share, 0, share - 1), 0, 0, 0),
        )

    specs = [part_spec(i) for i in range(len(ORDER))] * 2
    outs = pl.pallas_call(
        gradients_kernel,
        name="gradients",
        grid_spec=pltpu.PrefetchScalarGridSpec(
            num_scalar_prefetch=2,
            grid=(pairs,),
            in_specs=[
                one,
                two,
                both,
                both,
                pl.BlockSpec((batch, rank), lambda s, a, m: (0, 0)),
                pl.BlockSpec((batch, rank), lambda s, a, m: (0, 0)),
                pl.BlockSpec((batch, units), lambda s, a, m: (0, 0)),
                pl.BlockSpec((pair, EXTRA, width), lambda s, a, m: (pair_of(s, a), 0, 0)),
            ],
            out_specs=specs,
            scratch_shapes=[
                pltpu.VMEM((rank, batch), BF),
                pltpu.VMEM((rank, batch), BF),
                pltpu.VMEM((units, batch), BF),
            ],
        ),
        out_shape=[part] * len(specs),
        compiler_params=pltpu.CompilerParams(vmem_limit_bytes=VMEM),
        cost_estimate=pl.CostEstimate(
            flops=2 * batch * features * width * (2 * rank + units),
            bytes_accessed=18 << 20,
            transcendentals=0,
        ),
    )(place, slot_of, received, received, crossed, proj, low, low_grad, d_hidden, extra)
    return outs[: len(ORDER)], outs[len(ORDER) :]


def neighbours(axis):
    size = lax.axis_size(axis)
    up = [(i, (i + 1) % size) for i in range(size)]
    down = [(i, (i - 1) % size) for i in range(size)]
    return (
        lambda value: lax.ppermute(value, axis, up),
        lambda value: lax.ppermute(value, axis, down),
    )


def add(*terms):
    total = terms[0].astype(F32)
    for term in terms[1:]:
        total = total + term.astype(F32)
    return total.astype(BF)


def ring_sum(axis, opposite, following, preceding, own, between=lambda value: value):
    up, down = neighbours(axis)
    passed_down, passed_up = down(opposite[0]), up(opposite[1])
    direct_down, direct_up = down(preceding[1]), up(following[0])
    passed_down, passed_up = between((passed_down, passed_up))
    last_down = down(add(preceding[0], passed_down))
    last_up = up(add(following[1], passed_up))
    return add(own[0], direct_up, last_down), add(own[1], last_up, direct_down)


def ring_spread(axis, own):
    up, down = neighbours(axis)
    preceding, following = up(own), down(own)
    half = own.shape[0] // 2
    return own, following, down(following[:half]), up(preceding[half:]), preceding


def body(
    embedding_table,
    touched_blocks,
    bag_index,
    bag_count,
    feature_map,
    labels,
    v_weight,
    u_weight,
    cross_bias,
    hidden_weight,
    hidden_bias,
    out_weight,
):
    dp = ("x", "zh", "zl", "core")
    features = feature_map.shape[0]
    rows, width = embedding_table.shape
    samples = bag_index.shape[1]
    tile = samples // touched_blocks.shape[1]
    batch = labels.shape[0]
    rank = v_weight.shape[1]
    units = hidden_weight.shape[1]
    roles = lax.axis_size("role")
    total = roles * lax.axis_size(dp) * batch
    core = lax.axis_index("core")
    role = lax.axis_index("role")

    touched = touched_blocks[0].T
    pooled, incidence = pool(touched, embedding_table, bag_index[0].T, bag_count[0].T, tile)
    received = lax.all_to_all(
        pooled.reshape(features, batch, width), dp, split_axis=0, concat_axis=0, tiled=True
    )
    back, crossed, proj, low, low_grad, d_hidden, cross_g, hidden_g, out_g, slot_of = dense(
        feature_map,
        received,
        labels.reshape(batch, 1),
        v_weight,
        u_weight,
        cross_bias.reshape(1, -1),
        hidden_weight,
        hidden_bias.reshape(1, -1),
        out_weight.reshape(1, -1),
        LOSS_SCALE / total,
    )
    returned = lax.all_to_all(back, dp, split_axis=0, concat_axis=0, tiled=True)

    quarters = 4
    share = width // quarters
    per = units // (features * quarters)

    def spread(values):
        values = values.reshape(features, quarters, per)
        return jnp.pad(values, ((0, 0), (0, 0), (0, share - per))).reshape(features, 1, width)

    extra = jnp.concatenate(
        [cross_g.reshape(features, 1, width), spread(hidden_g), spread(out_g)], axis=1
    )
    extra = jnp.pad(extra, ((0, 0), (0, EXTRA - 3), (0, 0)))
    swap = [(0, 1), (1, 0)]
    extra = jnp.where(core == 0, extra + lax.ppermute(extra, "core", swap), 0.0).astype(BF)
    keep, send = gradients(
        jnp.stack([core, role]), slot_of, received, crossed, proj, low, low_grad, d_hidden, extra
    )
    each = features // roles
    halves = []
    for mine, sent in zip(keep, send):
        other = lax.ppermute(sent, "core", swap)
        cuts = (slice(0, each // 2), slice(each // 2, each))
        halves.append([add(mine[cut], other[cut]) for cut in cuts])

    def after_return(values):
        nonlocal returned
        values, returned = lax.optimization_barrier((values, returned))
        return values

    role_sum = jnp.concatenate(ring_sum("role", *halves, after_return), axis=0)
    pieces = lax.all_to_all(
        role_sum.reshape(each * 2, rank + EXTRA, width),
        ("x", "zh", "zl"),
        split_axis=0,
        concat_axis=0,
        tiled=True,
    )
    piece = jnp.sum(pieces.astype(F32), axis=0)
    shares = lax.all_to_all(piece.T, ("zl", "core"), split_axis=0, concat_axis=0, tiled=True)
    shares = shares.reshape(quarters, share, rank + EXTRA)
    grad_v = shares[0, :, :rank]
    grad_u = shares[2, :, :rank].T
    grad_h = jnp.concatenate([shares[1, :, :rank], shares[3, :, :rank]], axis=1)
    grad_cb = shares[0, :, rank]
    grad_hb = shares[0, :per, rank + 1]
    grad_ow = shares[0, :per, rank + 2]

    where = role.reshape(1)
    local = scatter(touched, where, incidence, returned.reshape(samples, width), rows, roles)
    middle = rows // roles // 2
    halves = [[local[i, :middle], local[i, middle:]] for i in range(roles)]
    part = jnp.concatenate(ring_sum("role", *halves), axis=0)
    table_grad = spread_rows(where, ring_spread("role", part), roles)
    return (table_grad, grad_v, grad_u, grad_cb, grad_h, grad_hb, grad_ow)


def solution(mesh):
    fine = Mesh(mesh.devices.reshape(4, 4, 2, 2, 2), ("role", "x", "zh", "zl", "core"))
    dp = ("x", "zh", "zl", "core")
    everywhere = ("role",) + dp
    return jax.shard_map(
        body,
        mesh=fine,
        in_specs=(
            P(dp, None),
            P(dp, "role", None),
            P(dp, "role", None),
            P(dp, "role", None),
            P(),
            P(everywhere),
            P(),
            P(),
            P(),
            P(),
            P(),
            P(),
        ),
        out_specs=(
            P(dp, None),
            P(everywhere, None),
            P(None, everywhere),
            P(everywhere),
            P(everywhere, None),
            P(everywhere),
            P(everywhere),
        ),
        check_vma=False,
    )
```

```python
import functools

import jax
import jax.numpy as jnp
from jax import lax
from jax.experimental import pallas as pl
from jax.experimental.pallas import tpu as pltpu
from jax.sharding import Mesh
from jax.sharding import PartitionSpec as P

BLK = 8
LOSS_SCALE = 65536.0
STEP_TILES = 8
WIDE = 2048
EXTRA = 16
ORDER = (2, 1, 3, 0)
VMEM = 60 << 20
POOL_VMEM = VMEM
DENSE_VMEM = VMEM
GRADIENTS_VMEM = VMEM
SCATTER_VMEM = VMEM

BF = jnp.bfloat16
F32 = jnp.float32


def nt(left, right):
    return lax.dot_general(left, right, (((1,), (1,)), ((), ())), preferred_element_type=F32)


def pool_kernel(touched, table, index, count, pooled, incidence, *scratch):
    rows16, rows32, index_in, count_in, held, tiles_held, table_sem, in_sems, out_sems = scratch
    tiles, tile, _ = incidence.shape
    steps = tiles // STEP_TILES
    span = STEP_TILES * tile

    def loads(step):
        part = pl.ds(pl.multiple_of(step * span, span), span)
        return (
            pltpu.make_async_copy(index.at[:, part], index_in.at[:, part], in_sems.at[0, step]),
            pltpu.make_async_copy(count.at[:, part], count_in.at[:, part], in_sems.at[1, step]),
        )

    def stores(step):
        part = pl.ds(pl.multiple_of(step * span, span), span)
        some = pl.ds(step * STEP_TILES, STEP_TILES)
        return (
            pltpu.make_async_copy(held.at[part], pooled.at[part], out_sems.at[0, step]),
            pltpu.make_async_copy(tiles_held.at[some], incidence.at[some], out_sems.at[1, step]),
        )

    whole = pltpu.make_async_copy(table, rows16, table_sem)
    whole.start()
    for step in range(steps):
        for copy in loads(step):
            copy.start()
    whole.wait()
    rows32[...] = rows16[...].astype(F32)
    listed = lax.broadcasted_iota(jnp.int32, (tile, tile), 0).astype(BF)

    @pl.loop(0, steps)
    def _(step):
        for copy in loads(step):
            copy.wait()
        for i in range(STEP_TILES):
            t = step * STEP_TILES + i
            part = pl.ds(pl.multiple_of(t * tile, tile), tile)
            idx = index_in[:, part].astype(BF)
            cnt = count_in[:, part].astype(BF)
            total = jnp.zeros((tile, tile), BF)
            for j in range(index.shape[0]):
                total += jnp.where(idx[j : j + 1] == listed, cnt[j : j + 1], jnp.zeros((), BF))
            tiles_held[t] = total
            blocks = [
                rows32[pl.ds(pl.multiple_of(touched[k, t] * BLK, BLK), BLK), :]
                for k in range(touched.shape[0])
            ]
            picked = jnp.concatenate(blocks, axis=0).astype(BF)
            held[part, :] = lax.dot_general(
                total, picked, (((0,), (0,)), ((), ())), preferred_element_type=F32
            ).astype(BF)
        for copy in stores(step):
            copy.start()

    for step in range(steps):
        for copy in stores(step):
            copy.wait()


def pool(touched, table, index, count, tile):
    hot, samples = index.shape
    tiles = samples // tile
    width = table.shape[1]
    steps = tiles // STEP_TILES
    hbm = pl.BlockSpec(memory_space=pltpu.HBM)
    return pl.pallas_call(
        pool_kernel,
        name="pool",
        in_specs=[pl.BlockSpec(memory_space=pltpu.SMEM), hbm, hbm, hbm],
        out_specs=[hbm, hbm],
        out_shape=[
            jax.ShapeDtypeStruct((samples, width), BF),
            jax.ShapeDtypeStruct((tiles, tile, tile), BF),
        ],
        scratch_shapes=[
            pltpu.VMEM(table.shape, BF),
            pltpu.VMEM(table.shape, F32),
            pltpu.VMEM(index.shape, jnp.int32),
            pltpu.VMEM(count.shape, jnp.int32),
            pltpu.VMEM((samples, width), BF),
            pltpu.VMEM((tiles, tile, tile), BF),
            pltpu.SemaphoreType.DMA,
            pltpu.SemaphoreType.DMA((2, steps)),
            pltpu.SemaphoreType.DMA((2, steps)),
        ],
        compiler_params=pltpu.CompilerParams(vmem_limit_bytes=POOL_VMEM),
    )(touched, table, index, count)


def scatter_kernel(touched, incidence, grad, out, *scratch):
    sums, (tiles_in, grads_in, sems) = scratch[:-3], scratch[-3:]
    tiles, tile, _ = incidence.shape
    chunks, rows, _ = out.shape
    steps = tiles // STEP_TILES

    def loads(step):
        part = pl.ds(step * STEP_TILES, STEP_TILES)
        span = pl.ds(step * STEP_TILES * tile, STEP_TILES * tile)
        return (
            pltpu.make_async_copy(incidence.at[part], tiles_in.at[part], sems.at[0, step]),
            pltpu.make_async_copy(grad.at[span], grads_in.at[span], sems.at[1, step]),
        )

    for step in range(steps):
        for copy in loads(step):
            copy.start()
    for acc in sums:
        acc[...] = jnp.zeros_like(acc)

    @pl.loop(0, steps)
    def _(step):
        for copy in loads(step):
            copy.wait()
        for i in range(STEP_TILES):
            t = step * STEP_TILES + i
            product = jnp.dot(
                tiles_in[t], grads_in[pl.ds(t * tile, tile), :], preferred_element_type=F32
            )
            for k in range(touched.shape[0]):
                acc = sums[k % len(sums)]
                place = pl.ds(pl.multiple_of(touched[k, t] * BLK, BLK), BLK)
                acc[place, :] += product[k * BLK : (k + 1) * BLK]

    for i in range(chunks):
        place = pl.ds(i * rows, rows)
        total = sums[0][place, :]
        for acc in sums[1:]:
            total = total + acc[place, :]
        out[i] = total.astype(out.dtype)


def scatter(touched, incidence, grad, rows, chunks):
    tiles, tile, _ = incidence.shape
    width = grad.shape[1]
    steps = tiles // STEP_TILES
    smem = pl.BlockSpec(memory_space=pltpu.SMEM)
    hbm = pl.BlockSpec(memory_space=pltpu.HBM)
    vmem = pl.BlockSpec(memory_space=pltpu.VMEM)
    return pl.pallas_call(
        scatter_kernel,
        name="scatter",
        in_specs=[smem, hbm, hbm],
        out_specs=vmem,
        out_shape=jax.ShapeDtypeStruct((chunks, rows // chunks, width), BF),
        scratch_shapes=[pltpu.VMEM((rows, width), F32)] * 4
        + [
            pltpu.VMEM(incidence.shape, BF),
            pltpu.VMEM(grad.shape, BF),
            pltpu.SemaphoreType.DMA((2, steps)),
        ],
        compiler_params=pltpu.CompilerParams(vmem_limit_bytes=SCATTER_VMEM),
        cost_estimate=pl.CostEstimate(flops=1 << 33, bytes_accessed=8 << 20, transcendentals=0),
    )(touched, incidence, grad)


def spread_kernel(role, own, following, opposite_a, opposite_b, preceding, out):
    rows = own.shape[0]
    half = rows // 2
    chunks = out.shape[0] // rows

    def place(offset, size, piece):
        first = lax.rem(role[0] + offset, chunks) * rows
        out[pl.ds(pl.multiple_of(first, rows) + size, piece.shape[0]), :] = piece[...].astype(F32)

    place(0, 0, own)
    place(1, 0, following)
    place(2, 0, opposite_a)
    place(2, half, opposite_b)
    place(3, 0, preceding)


def spread_rows(role, pieces, chunks):
    rows, width = pieces[0].shape
    vmem = pl.BlockSpec(memory_space=pltpu.VMEM)
    return pl.pallas_call(
        spread_kernel,
        name="spread_rows",
        in_specs=[pl.BlockSpec(memory_space=pltpu.SMEM)] + [vmem] * 5,
        out_specs=vmem,
        out_shape=jax.ShapeDtypeStruct((chunks * rows, width), F32),
        compiler_params=pltpu.CompilerParams(vmem_limit_bytes=VMEM),
    )(role, *pieces)


def dense_kernel(
    scale,
    fmap,
    received,
    labels,
    v_hbm,
    u_hbm,
    cross_bias,
    h_hbm,
    hidden_bias,
    out_weight,
    back,
    crossed_hbm,
    proj_hbm,
    low_hbm,
    low_grad_hbm,
    d_hidden_hbm,
    cross_bias_grad,
    hidden_bias_grad,
    out_weight_grad,
    inter,
    crossed,
    proj_low,
    held,
    d_inter,
    v,
    u,
    h,
    low_out,
    low_grad_out,
    d_hidden_out,
    hidden,
    low_sum,
    in_sems,
    weight_sems,
    small_sems,
    wide_sems,
    back_sems,
):
    features, batch, width = received.shape
    total_width = features * width
    blocks = total_width // WIDE
    per_block = WIDE // width

    def load(s):
        cols = pl.ds(pl.multiple_of(fmap[s] * width, width), width)
        return pltpu.make_async_copy(received.at[s], inter.at[:, cols], in_sems.at[s])

    weights = [
        pltpu.make_async_copy(source, target, weight_sems.at[i])
        for i, (source, target) in enumerate(((v_hbm, v), (u_hbm, u), (h_hbm, h)))
    ]
    weights[0].start()
    loads = [load(s) for s in range(features)]
    for copy in loads:
        copy.start()
    weights[1].start()
    weights[2].start()

    def store(row, source, target, f):
        cols = pl.ds(pl.multiple_of(f * width, width), width)
        return pltpu.make_async_copy(source.at[:, cols], target.at[f], wide_sems.at[row, f])

    small = [
        pltpu.make_async_copy(source, target, small_sems.at[i])
        for i, (source, target) in enumerate(
            ((low_out, low_hbm), (low_grad_out, low_grad_hbm), (d_hidden_out, d_hidden_hbm))
        )
    ]
    low_sum[...] = jnp.zeros_like(low_sum)
    hidden[...] = jnp.broadcast_to(hidden_bias[...], hidden.shape)
    hidden_bias_grad[...] = jnp.zeros_like(hidden_bias_grad)
    out_weight_grad[...] = jnp.zeros_like(out_weight_grad)
    weights[0].wait()
    for b in range(blocks):
        places = []
        for s in range(b * per_block, (b + 1) * per_block):
            loads[s].wait()
            places.append(pl.ds(pl.multiple_of(fmap[s] * width, width), width))
        left = jnp.concatenate([inter[:, place] for place in places], axis=1)
        right = jnp.concatenate([v[place, :] for place in places], axis=0)
        low_sum[...] += jnp.dot(left, right, preferred_element_type=F32)

    low_out[...] = low_sum[...].astype(BF)
    small[0].start()
    weights[1].wait()
    weights[2].wait()

    @pl.loop(0, blocks)
    def _(b):
        cols = pl.ds(pl.multiple_of(b * WIDE, WIDE), WIDE)
        projected = (
            jnp.dot(low_out[...], u[:, cols], preferred_element_type=F32) + cross_bias[:, cols]
        )
        held[:, cols] = projected
        x = inter[:, cols].astype(F32)
        product = (x * projected + x).astype(BF)
        crossed[:, cols] = product
        hidden[...] += jnp.dot(product, h[cols, :], preferred_element_type=F32)
        for i in range(per_block):
            store(0, crossed, crossed_hbm, b * per_block + i).start()

    chunk = 64

    @pl.loop(0, batch // chunk)
    def _(r):
        rows = pl.ds(pl.multiple_of(r * chunk, chunk), chunk)
        pre = hidden[rows, :]
        gate = jax.nn.sigmoid(pre)
        act = (pre * gate).astype(BF).astype(F32)
        weight = out_weight[...].astype(F32)
        logit = jnp.sum(act * weight, axis=1, keepdims=True)
        d_logit = (scale * (jax.nn.sigmoid(logit) - labels[rows, :].astype(F32))).astype(BF)
        d_logit = d_logit.astype(F32)
        d_hidden = (d_logit * weight * (gate * (1.0 + pre * (1.0 - gate)))).astype(BF)
        d_hidden_out[rows, :] = d_hidden
        hidden_bias_grad[...] += jnp.sum(d_hidden.astype(F32), axis=0, keepdims=True)
        out_weight_grad[...] += jnp.sum(d_logit * act, axis=0, keepdims=True)

    small[2].start()
    low_sum[...] = jnp.zeros_like(low_sum)

    @pl.loop(0, blocks)
    def _(b):
        cols = pl.ds(pl.multiple_of(b * WIDE, WIDE), WIDE)
        d_crossed = nt(d_hidden_out[...], h[cols, :])
        d_proj = d_crossed * inter[:, cols].astype(F32)
        cross_bias_grad[:, cols] = jnp.sum(d_proj, axis=0, keepdims=True)
        rounded = d_proj.astype(BF)
        proj_low[:, cols] = rounded
        low_sum[...] += nt(rounded, u[:, cols])
        held[:, cols] = d_crossed * (held[:, cols] + 1.0)
        for i in range(per_block):
            store(1, proj_low, proj_hbm, b * per_block + i).start()

    low_grad_out[...] = low_sum[...].astype(BF)
    small[1].start()
    stores = list(small)
    for f in range(features):
        stores += [store(0, crossed, crossed_hbm, f), store(1, proj_low, proj_hbm, f)]
    for b in range(blocks):
        slots = range(b * per_block, (b + 1) * per_block)
        places = [pl.ds(pl.multiple_of(fmap[s] * width, width), width) for s in slots]
        kept = jnp.concatenate([held[:, place] for place in places], axis=1)
        right = jnp.concatenate([v[place, :] for place in places], axis=0)
        result = (kept + nt(low_grad_out[...], right)).astype(BF)
        for i, s in enumerate(slots):
            d_inter[s] = result[:, i * width : (i + 1) * width]
            copy = pltpu.make_async_copy(d_inter.at[s], back.at[s], back_sems.at[s])
            copy.start()
            stores.append(copy)
    for copy in stores:
        copy.wait()


def dense(fmap, received, labels, v, u, cross_bias, h, hidden_bias, out_weight, scale):
    features, batch, width = received.shape
    total_width = features * width
    rank = v.shape[1]
    units = h.shape[1]
    vmem = pl.BlockSpec(memory_space=pltpu.VMEM)
    smem = pl.BlockSpec(memory_space=pltpu.SMEM)
    hbm = pl.BlockSpec(memory_space=pltpu.HBM)
    return pl.pallas_call(
        functools.partial(dense_kernel, scale),
        name="dense",
        in_specs=[smem, hbm, vmem, hbm, hbm, vmem, hbm, vmem, vmem],
        out_specs=[hbm] * 6 + [vmem] * 3,
        out_shape=[
            jax.ShapeDtypeStruct(received.shape, BF),
            jax.ShapeDtypeStruct(received.shape, BF),
            jax.ShapeDtypeStruct(received.shape, BF),
            jax.ShapeDtypeStruct((batch, rank), BF),
            jax.ShapeDtypeStruct((batch, rank), BF),
            jax.ShapeDtypeStruct((batch, units), BF),
            jax.ShapeDtypeStruct((1, total_width), F32),
            jax.ShapeDtypeStruct((1, units), F32),
            jax.ShapeDtypeStruct((1, units), F32),
        ],
        scratch_shapes=[
            pltpu.VMEM((batch, total_width), BF),
            pltpu.VMEM((batch, total_width), BF),
            pltpu.VMEM((batch, total_width), BF),
            pltpu.VMEM((batch, total_width), F32),
            pltpu.VMEM(received.shape, BF),
            pltpu.VMEM(v.shape, BF),
            pltpu.VMEM(u.shape, BF),
            pltpu.VMEM(h.shape, BF),
            pltpu.VMEM((batch, rank), BF),
            pltpu.VMEM((batch, rank), BF),
            pltpu.VMEM((batch, units), BF),
            pltpu.VMEM((batch, units), F32),
            pltpu.VMEM((batch, rank), F32),
            pltpu.SemaphoreType.DMA((features,)),
            pltpu.SemaphoreType.DMA((3,)),
            pltpu.SemaphoreType.DMA((3,)),
            pltpu.SemaphoreType.DMA((2, features)),
            pltpu.SemaphoreType.DMA((features,)),
        ],
        compiler_params=pltpu.CompilerParams(vmem_limit_bytes=DENSE_VMEM),
    )(fmap, received, labels, v, u, cross_bias, h, hidden_bias, out_weight)


def gradients_kernel(
    order,
    place,
    fmap,
    received,
    crossed,
    proj,
    low_hbm,
    low_grad_hbm,
    d_hidden_hbm,
    cross_bias_grad,
    hidden_bias_grad,
    out_weight_grad,
    *rest,
):
    parts, chunks = len(order), len(ORDER)
    outs = rest[: 2 * parts]
    inter_in, crossed_in, proj_in, low, low_grad, d_hidden = rest[2 * parts : 2 * parts + 6]
    low_t, low_grad_t, d_hidden_t, small, keep, send = rest[2 * parts + 6 : -5]
    slot_of, small_sems, inter_sems, wide_sems, out_sems = rest[-5:]
    features = fmap.shape[0]
    width = keep.shape[-1]
    rank = low_t.shape[0]
    each = features // chunks
    pair = 2
    share = each // pair

    smalls = [
        pltpu.make_async_copy(source, target, small_sems.at[i])
        for i, (source, target) in enumerate(
            ((low_hbm, low), (low_grad_hbm, low_grad), (d_hidden_hbm, d_hidden))
        )
    ]
    for copy in smalls:
        copy.start()
    for s in range(features):
        slot_of[fmap[s]] = s
    loads = []
    for part, offset in enumerate(order):
        base = lax.rem(place[1] + offset, chunks) * each
        span = pl.ds(part * each, each)
        copies = [
            pltpu.make_async_copy(crossed.at[pl.ds(base, each)], crossed_in.at[span], wide_sems.at[0, part]),
            pltpu.make_async_copy(proj.at[pl.ds(base, each)], proj_in.at[span], wide_sems.at[1, part]),
        ]
        for i in range(each):
            n = part * each + i
            copies.append(
                pltpu.make_async_copy(
                    received.at[slot_of[base + i]], inter_in.at[n], inter_sems.at[n]
                )
            )
        loads.append(copies)
    for copy in loads[0]:
        copy.start()
    for copy in smalls:
        copy.wait()

    low_t[...] = low[...].astype(F32).T.astype(BF)
    low_grad_t[...] = low_grad[...].astype(F32).T.astype(BF)
    d_hidden_t[...] = d_hidden[...].astype(F32).T.astype(BF)
    quarters = 4
    units = hidden_bias_grad.shape[1]
    per = units // (features * quarters)
    mine = lax.broadcasted_iota(jnp.int32, (features, units), 0)
    unit = lax.broadcasted_iota(jnp.int32, (features, units), 1)
    mine = unit // (per * quarters) == mine
    unit = lax.broadcasted_iota(jnp.int32, (units, width), 0)
    lane = lax.broadcasted_iota(jnp.int32, (units, width), 1)
    within = unit % (per * quarters)
    spread = (within // per * (width // quarters) + within % per == lane).astype(F32)
    for i, grad in enumerate((hidden_bias_grad, out_weight_grad)):
        small[i] = jnp.dot(
            jnp.where(mine, grad[...], 0.0),
            spread,
            preferred_element_type=F32,
            precision=lax.Precision.HIGHEST,
        )
    line = lax.broadcasted_iota(jnp.int32, (EXTRA, width), 0)
    nothing = jnp.zeros((EXTRA, width), BF)
    first = place[0] == 0

    for part, offset in enumerate(order):
        for copy in loads[part]:
            copy.wait()
        if part + 1 < parts:
            for copy in loads[part + 1]:
                copy.start()

        @pl.loop(0, share)
        def _(k, part=part, offset=offset):
            base = lax.rem(place[1] + offset, chunks) * each + k * pair
            n = part * each + k * pair

            def product(left, right):
                both = jnp.concatenate([right[n + i] for i in range(pair)], axis=1)
                return jnp.dot(left[...], both, preferred_element_type=F32).astype(BF)

            of_v = product(low_grad_t, inter_in)
            of_u = product(low_t, proj_in)
            of_h = product(d_hidden_t, crossed_in)

            def fill(one, other):
                for i in range(pair):
                    lanes = slice(i * width, (i + 1) * width)
                    f = base + i
                    cross = cross_bias_grad[:, pl.ds(pl.multiple_of(f * width, width), width)]
                    extra = jnp.where(line == 0, cross, 0.0)
                    for j in range(2):
                        extra = jnp.where(line == j + 1, small[j, pl.ds(f, 1), :], extra)
                    one[n + i, 0, pl.ds(0, rank), :] = of_v[:, lanes]
                    one[n + i, 0, pl.ds(rank, EXTRA), :] = extra.astype(BF)
                    one[n + i, 1, pl.ds(0, rank), :] = of_u[:, lanes]
                    one[n + i, 1, pl.ds(rank, EXTRA), :] = nothing
                    other[n + i, 0, pl.ds(0, rank), :] = of_h[:rank, lanes]
                    other[n + i, 0, pl.ds(rank, EXTRA), :] = nothing
                    other[n + i, 1, pl.ds(0, rank), :] = of_h[rank:, lanes]
                    other[n + i, 1, pl.ds(rank, EXTRA), :] = nothing

            @pl.when(first)
            def _():
                fill(keep, send)

            @pl.when(jnp.logical_not(first))
            def _():
                fill(send, keep)

        span = pl.ds(part * each, each)
        pltpu.make_async_copy(send.at[span], outs[parts + part], out_sems.at[parts + part]).start()
        pltpu.make_async_copy(keep.at[span], outs[part], out_sems.at[part]).start()

    for part in range(parts):
        span = pl.ds(part * each, each)
        pltpu.make_async_copy(send.at[span], outs[parts + part], out_sems.at[parts + part]).wait()
        pltpu.make_async_copy(keep.at[span], outs[part], out_sems.at[part]).wait()


def gradients(order, place, fmap, received, crossed, proj, low, low_grad, d_hidden, *small):
    features, batch, width = received.shape
    rank, units = low.shape[1], d_hidden.shape[1]
    parts = len(order)
    held = features // len(ORDER) * parts
    part = jax.ShapeDtypeStruct((features // len(ORDER), 2, rank + EXTRA, width), BF)
    vmem = pl.BlockSpec(memory_space=pltpu.VMEM)
    smem = pl.BlockSpec(memory_space=pltpu.SMEM)
    hbm = pl.BlockSpec(memory_space=pltpu.HBM)
    outs = pl.pallas_call(
        functools.partial(gradients_kernel, order),
        name="gradients",
        in_specs=[smem, smem] + [hbm] * 6 + [vmem] * 3,
        out_specs=[hbm] * (2 * parts),
        out_shape=[part] * (2 * parts),
        scratch_shapes=[pltpu.VMEM((held, batch, width), BF)] * 3
        + [
            pltpu.VMEM((batch, rank), BF),
            pltpu.VMEM((batch, rank), BF),
            pltpu.VMEM((batch, units), BF),
            pltpu.VMEM((rank, batch), BF),
            pltpu.VMEM((rank, batch), BF),
            pltpu.VMEM((units, batch), BF),
            pltpu.VMEM((2, features, width), F32),
            pltpu.VMEM((held, 2, rank + EXTRA, width), BF),
            pltpu.VMEM((held, 2, rank + EXTRA, width), BF),
            pltpu.SMEM((features,), jnp.int32),
            pltpu.SemaphoreType.DMA((3,)),
            pltpu.SemaphoreType.DMA((held,)),
            pltpu.SemaphoreType.DMA((2, parts)),
            pltpu.SemaphoreType.DMA((2 * parts,)),
        ],
        compiler_params=pltpu.CompilerParams(vmem_limit_bytes=GRADIENTS_VMEM),
        cost_estimate=pl.CostEstimate(
            flops=2 * batch * held * width * (2 * rank + units),
            bytes_accessed=held << 19,
            transcendentals=0,
        ),
    )(place, fmap, received, crossed, proj, low, low_grad, d_hidden, *small)
    return outs[:parts], outs[parts:]


def neighbours(axis):
    size = lax.axis_size(axis)
    up = [(i, (i + 1) % size) for i in range(size)]
    down = [(i, (i - 1) % size) for i in range(size)]
    return (
        lambda value: lax.ppermute(value, axis, up),
        lambda value: lax.ppermute(value, axis, down),
    )


def add(*terms):
    total = terms[0].astype(F32)
    for term in terms[1:]:
        total = total + term.astype(F32)
    return total.astype(BF)


def ring_parts(axis, opposite, following, preceding):
    up, down = neighbours(axis)
    passed = (down(opposite[0]), up(opposite[1]))
    from_following = down(jnp.concatenate([add(preceding[0], passed[0]), preceding[1]], axis=0))
    from_preceding = up(jnp.concatenate([following[0], add(following[1], passed[1])], axis=0))
    return from_following, from_preceding


def ring_spread(axis, own):
    up, down = neighbours(axis)
    preceding, following = up(own), down(own)
    half = own.shape[0] // 2
    return own, following, down(following[:half]), up(preceding[half:]), preceding


def body(
    embedding_table,
    touched_blocks,
    bag_index,
    bag_count,
    feature_map,
    labels,
    v_weight,
    u_weight,
    cross_bias,
    hidden_weight,
    hidden_bias,
    out_weight,
):
    dp = ("x", "zh", "zl", "core")
    features = feature_map.shape[0]
    rows, width = embedding_table.shape
    samples = bag_index.shape[1]
    tile = samples // touched_blocks.shape[1]
    batch = labels.shape[0]
    rank = v_weight.shape[1]
    units = hidden_weight.shape[1]
    roles = lax.axis_size("role")
    total = roles * lax.axis_size(dp) * batch
    core = lax.axis_index("core")
    role = lax.axis_index("role")

    touched = touched_blocks[0].T
    pooled, incidence = pool(touched, embedding_table, bag_index[0].T, bag_count[0].T, tile)
    received = lax.all_to_all(
        pooled.reshape(features, batch, width), dp, split_axis=0, concat_axis=0, tiled=True
    )
    back, crossed, proj, low, low_grad, d_hidden, cross_g, hidden_g, out_g = dense(
        feature_map,
        received,
        labels.reshape(batch, 1),
        v_weight,
        u_weight,
        cross_bias.reshape(1, -1),
        hidden_weight,
        hidden_bias.reshape(1, -1),
        out_weight.reshape(1, -1),
        LOSS_SCALE / total,
    )
    returned = lax.all_to_all(back, dp, split_axis=0, concat_axis=0, tiled=True)

    quarters = 4
    share = width // quarters
    per = units // (features * quarters)

    swap = [(0, 1), (1, 0)]
    each = features // roles
    keep, send = gradients(
        ORDER,
        jnp.stack([core, role]),
        feature_map,
        received,
        crossed,
        proj,
        low,
        low_grad,
        d_hidden,
        cross_g,
        hidden_g,
        out_g,
    )
    halves = []
    for mine, sent in zip(keep, send):
        other = lax.ppermute(sent, "core", [(0, 1), (1, 0)])
        cuts = (slice(0, each // 2), slice(each // 2, each))
        halves.append([add(mine[cut], other[cut]) for cut in cuts])

    local = scatter(touched, incidence, returned.reshape(samples, width), rows, roles)
    parts = lax.all_to_all(local, "role", split_axis=0, concat_axis=0, tiled=True)
    others, parts = lax.optimization_barrier((ring_parts("role", *halves[:3]), parts))
    role_sum = add(jnp.concatenate(halves[3], axis=0), *others)
    pieces = lax.all_to_all(
        role_sum.reshape(each * 2, rank + EXTRA, width),
        ("x", "zh", "zl"),
        split_axis=0,
        concat_axis=0,
        tiled=True,
    )
    piece = jnp.sum(pieces.astype(F32), axis=0)
    shares = lax.all_to_all(piece.T, ("zl", "core"), split_axis=0, concat_axis=0, tiled=True)
    shares = shares.reshape(quarters, share, rank + EXTRA)
    grad_v = shares[0, :, :rank]
    grad_u = shares[2, :, :rank].T
    grad_h = jnp.concatenate([shares[1, :, :rank], shares[3, :, :rank]], axis=1)
    grad_cb = shares[0, :, rank]
    grad_hb = shares[0, :per, rank + 1]
    grad_ow = shares[0, :per, rank + 2]

    part = add(*parts)
    table_grad = spread_rows(role.reshape(1), ring_spread("role", part), roles)
    return (table_grad, grad_v, grad_u, grad_cb, grad_h, grad_hb, grad_ow)


def solution(mesh):
    fine = Mesh(mesh.devices.reshape(4, 4, 2, 2, 2), ("role", "x", "zh", "zl", "core"))
    dp = ("x", "zh", "zl", "core")
    everywhere = ("role",) + dp
    return jax.shard_map(
        body,
        mesh=fine,
        in_specs=(
            P(dp, None),
            P(dp, "role", None),
            P(dp, "role", None),
            P(dp, "role", None),
            P(),
            P(everywhere),
            P(),
            P(),
            P(),
            P(),
            P(),
            P(),
        ),
        out_specs=(
            P(dp, None),
            P(everywhere, None),
            P(None, everywhere),
            P(everywhere),
            P(everywhere, None),
            P(everywhere),
            P(everywhere),
        ),
        check_vma=False,
    )
```

```python
import functools

import jax
import jax.numpy as jnp
from jax import lax
from jax.experimental import pallas as pl
from jax.experimental.pallas import tpu as pltpu
from jax.sharding import Mesh
from jax.sharding import PartitionSpec as P

BLK = 8
LOSS_SCALE = 65536.0
STEP_TILES = 16
WIDE = 2048
EXTRA = 16
PAIR = 4
ORDER = (2, 1, 3, 0)
VMEM = 60 << 20
POOL_VMEM = VMEM
DENSE_VMEM = VMEM
GRADIENTS_VMEM = VMEM
SCATTER_VMEM = VMEM

BF = jnp.bfloat16
F32 = jnp.float32


def nt(left, right):
    return lax.dot_general(left, right, (((1,), (1,)), ((), ())), preferred_element_type=F32)


def pool_kernel(touched, table, index, count, pooled, incidence, *scratch):
    rows16, rows32, index_in, count_in, held, tiles_held, table_sem, in_sems, out_sems = scratch
    tiles, tile, _ = incidence.shape
    steps = tiles // STEP_TILES
    span = STEP_TILES * tile

    def loads(step):
        part = pl.ds(pl.multiple_of(step * span, span), span)
        return (
            pltpu.make_async_copy(index.at[:, part], index_in.at[:, part], in_sems.at[0, step]),
            pltpu.make_async_copy(count.at[:, part], count_in.at[:, part], in_sems.at[1, step]),
        )

    def stores(step):
        part = pl.ds(pl.multiple_of(step * span, span), span)
        some = pl.ds(step * STEP_TILES, STEP_TILES)
        return (
            pltpu.make_async_copy(held.at[part], pooled.at[part], out_sems.at[0, step]),
            pltpu.make_async_copy(tiles_held.at[some], incidence.at[some], out_sems.at[1, step]),
        )

    whole = pltpu.make_async_copy(table, rows16, table_sem)
    whole.start()
    for step in range(steps):
        for copy in loads(step):
            copy.start()
    whole.wait()
    rows32[...] = rows16[...].astype(F32)
    listed = lax.broadcasted_iota(jnp.int32, (tile, tile), 0).astype(BF)

    @pl.loop(0, steps)
    def _(step):
        for copy in loads(step):
            copy.wait()
        for i in range(STEP_TILES):
            t = step * STEP_TILES + i
            part = pl.ds(pl.multiple_of(t * tile, tile), tile)
            idx = index_in[:, part].astype(BF)
            cnt = count_in[:, part].astype(BF)
            total = jnp.zeros((tile, tile), BF)
            for j in range(index.shape[0]):
                total += jnp.where(idx[j : j + 1] == listed, cnt[j : j + 1], jnp.zeros((), BF))
            tiles_held[t] = total
            blocks = [
                rows32[pl.ds(pl.multiple_of(touched[k, t] * BLK, BLK), BLK), :]
                for k in range(touched.shape[0])
            ]
            picked = jnp.concatenate(blocks, axis=0).astype(BF)
            held[part, :] = lax.dot_general(
                total, picked, (((0,), (0,)), ((), ())), preferred_element_type=F32
            ).astype(BF)
        for copy in stores(step):
            copy.start()

    for step in range(steps):
        for copy in stores(step):
            copy.wait()


def pool(touched, table, index, count, tile):
    hot, samples = index.shape
    tiles = samples // tile
    width = table.shape[1]
    steps = tiles // STEP_TILES
    hbm = pl.BlockSpec(memory_space=pltpu.HBM)
    return pl.pallas_call(
        pool_kernel,
        name="pool",
        in_specs=[pl.BlockSpec(memory_space=pltpu.SMEM), hbm, hbm, hbm],
        out_specs=[hbm, hbm],
        out_shape=[
            jax.ShapeDtypeStruct((samples, width), BF),
            jax.ShapeDtypeStruct((tiles, tile, tile), BF),
        ],
        scratch_shapes=[
            pltpu.VMEM(table.shape, BF),
            pltpu.VMEM(table.shape, F32),
            pltpu.VMEM(index.shape, jnp.int32),
            pltpu.VMEM(count.shape, jnp.int32),
            pltpu.VMEM((samples, width), BF),
            pltpu.VMEM((tiles, tile, tile), BF),
            pltpu.SemaphoreType.DMA,
            pltpu.SemaphoreType.DMA((2, steps)),
            pltpu.SemaphoreType.DMA((2, steps)),
        ],
        compiler_params=pltpu.CompilerParams(vmem_limit_bytes=POOL_VMEM),
    )(touched, table, index, count)


def scatter_kernel(touched, incidence, grad, out, *scratch):
    sums, (tiles_in, grads_in, sems) = scratch[:-3], scratch[-3:]
    tiles, tile, _ = incidence.shape
    chunks, rows, _ = out.shape
    steps = tiles // STEP_TILES

    def loads(step):
        part = pl.ds(step * STEP_TILES, STEP_TILES)
        span = pl.ds(step * STEP_TILES * tile, STEP_TILES * tile)
        return (
            pltpu.make_async_copy(incidence.at[part], tiles_in.at[part], sems.at[0, step]),
            pltpu.make_async_copy(grad.at[span], grads_in.at[span], sems.at[1, step]),
        )

    for step in range(steps):
        for copy in loads(step):
            copy.start()
    for acc in sums:
        acc[...] = jnp.zeros_like(acc)

    @pl.loop(0, steps)
    def _(step):
        for copy in loads(step):
            copy.wait()
        for i in range(STEP_TILES):
            t = step * STEP_TILES + i
            product = jnp.dot(
                tiles_in[t], grads_in[pl.ds(t * tile, tile), :], preferred_element_type=F32
            )
            for k in range(touched.shape[0]):
                acc = sums[k % len(sums)]
                place = pl.ds(pl.multiple_of(touched[k, t] * BLK, BLK), BLK)
                acc[place, :] += product[k * BLK : (k + 1) * BLK]

    for i in range(chunks):
        place = pl.ds(i * rows, rows)
        total = sums[0][place, :]
        for acc in sums[1:]:
            total = total + acc[place, :]
        out[i] = total.astype(out.dtype)


def scatter(touched, incidence, grad, rows, chunks):
    tiles, tile, _ = incidence.shape
    width = grad.shape[1]
    steps = tiles // STEP_TILES
    smem = pl.BlockSpec(memory_space=pltpu.SMEM)
    hbm = pl.BlockSpec(memory_space=pltpu.HBM)
    vmem = pl.BlockSpec(memory_space=pltpu.VMEM)
    return pl.pallas_call(
        scatter_kernel,
        name="scatter",
        in_specs=[smem, hbm, hbm],
        out_specs=vmem,
        out_shape=jax.ShapeDtypeStruct((chunks, rows // chunks, width), BF),
        scratch_shapes=[pltpu.VMEM((rows, width), F32)] * 4
        + [
            pltpu.VMEM(incidence.shape, BF),
            pltpu.VMEM(grad.shape, BF),
            pltpu.SemaphoreType.DMA((2, steps)),
        ],
        compiler_params=pltpu.CompilerParams(vmem_limit_bytes=SCATTER_VMEM),
        cost_estimate=pl.CostEstimate(flops=1 << 33, bytes_accessed=8 << 20, transcendentals=0),
    )(touched, incidence, grad)


def spread_kernel(role, own, following, opposite_a, opposite_b, preceding, out):
    rows = own.shape[0]
    half = rows // 2
    chunks = out.shape[0] // rows

    def place(offset, size, piece):
        first = lax.rem(role[0] + offset, chunks) * rows
        out[pl.ds(pl.multiple_of(first, rows) + size, piece.shape[0]), :] = piece[...].astype(F32)

    place(0, 0, own)
    place(1, 0, following)
    place(2, 0, opposite_a)
    place(2, half, opposite_b)
    place(3, 0, preceding)


def spread_rows(role, pieces, chunks):
    rows, width = pieces[0].shape
    vmem = pl.BlockSpec(memory_space=pltpu.VMEM)
    return pl.pallas_call(
        spread_kernel,
        name="spread_rows",
        in_specs=[pl.BlockSpec(memory_space=pltpu.SMEM)] + [vmem] * 5,
        out_specs=vmem,
        out_shape=jax.ShapeDtypeStruct((chunks * rows, width), F32),
        compiler_params=pltpu.CompilerParams(vmem_limit_bytes=VMEM),
    )(role, *pieces)


def dense_kernel(
    scale,
    fmap,
    received,
    labels,
    v_hbm,
    u_hbm,
    cross_bias,
    h_hbm,
    hidden_bias,
    out_weight,
    back,
    crossed_hbm,
    proj_hbm,
    low_hbm,
    low_grad_hbm,
    d_hidden_hbm,
    cross_bias_grad,
    hidden_bias_grad,
    out_weight_grad,
    inter,
    crossed,
    proj_low,
    held,
    d_inter,
    v,
    u,
    h,
    low_out,
    low_grad_out,
    d_hidden_out,
    hidden,
    low_sum,
    slot_of,
    in_sem,
    weight_sems,
    small_sems,
    wide_sems,
):
    features, batch, width = received.shape
    total_width = features * width
    blocks = total_width // WIDE
    per_block = WIDE // width

    weights = [
        pltpu.make_async_copy(source, target, weight_sems.at[i])
        for i, (source, target) in enumerate(((v_hbm, v), (u_hbm, u), (h_hbm, h)))
    ]
    weights[0].start()
    load = pltpu.make_async_copy(received, inter, in_sem)
    load.start()
    weights[1].start()
    weights[2].start()

    def store(row, source, target, b):
        part = pl.ds(b * per_block, per_block)
        return pltpu.make_async_copy(source.at[part], target.at[part], wide_sems.at[row, b])

    def of_block(b):
        slots = [slot_of[b * per_block + i] for i in range(per_block)]
        return jnp.concatenate([inter[slot] for slot in slots], axis=1).astype(F32)

    def put(target, b, value):
        for i in range(per_block):
            target[b * per_block + i] = value[:, i * width : (i + 1) * width]

    small = [
        pltpu.make_async_copy(source, target, small_sems.at[i])
        for i, (source, target) in enumerate(
            ((low_out, low_hbm), (low_grad_out, low_grad_hbm), (d_hidden_out, d_hidden_hbm))
        )
    ]
    for s in range(features):
        slot_of[fmap[s]] = s
    low_sum[...] = jnp.zeros_like(low_sum)
    hidden[...] = jnp.broadcast_to(hidden_bias[...], hidden.shape)
    hidden_bias_grad[...] = jnp.zeros_like(hidden_bias_grad)
    out_weight_grad[...] = jnp.zeros_like(out_weight_grad)
    load.wait()
    weights[0].wait()
    for b in range(blocks):
        slots = range(b * per_block, (b + 1) * per_block)
        places = [pl.ds(pl.multiple_of(fmap[s] * width, width), width) for s in slots]
        left = jnp.concatenate([inter[s] for s in slots], axis=1)
        right = jnp.concatenate([v[place, :] for place in places], axis=0)
        low_sum[...] += jnp.dot(left, right, preferred_element_type=F32)

    low_out[...] = low_sum[...].astype(BF)
    small[0].start()
    weights[1].wait()
    weights[2].wait()

    @pl.loop(0, blocks)
    def _(b):
        cols = pl.ds(pl.multiple_of(b * WIDE, WIDE), WIDE)
        projected = (
            jnp.dot(low_out[...], u[:, cols], preferred_element_type=F32) + cross_bias[:, cols]
        )
        held[:, cols] = projected
        x = of_block(b)
        product = (x * projected + x).astype(BF)
        put(crossed, b, product)
        hidden[...] += jnp.dot(product, h[cols, :], preferred_element_type=F32)
        store(0, crossed, crossed_hbm, b).start()

    chunk = 64

    @pl.loop(0, batch // chunk)
    def _(r):
        rows = pl.ds(pl.multiple_of(r * chunk, chunk), chunk)
        pre = hidden[rows, :]
        gate = jax.nn.sigmoid(pre)
        act = (pre * gate).astype(BF).astype(F32)
        weight = out_weight[...].astype(F32)
        logit = jnp.sum(act * weight, axis=1, keepdims=True)
        d_logit = (scale * (jax.nn.sigmoid(logit) - labels[rows, :].astype(F32))).astype(BF)
        d_logit = d_logit.astype(F32)
        d_hidden = (d_logit * weight * (gate * (1.0 + pre * (1.0 - gate)))).astype(BF)
        d_hidden_out[rows, :] = d_hidden
        hidden_bias_grad[...] += jnp.sum(d_hidden.astype(F32), axis=0, keepdims=True)
        out_weight_grad[...] += jnp.sum(d_logit * act, axis=0, keepdims=True)

    small[2].start()
    low_sum[...] = jnp.zeros_like(low_sum)

    @pl.loop(0, blocks)
    def _(b):
        cols = pl.ds(pl.multiple_of(b * WIDE, WIDE), WIDE)
        d_crossed = nt(d_hidden_out[...], h[cols, :])
        d_proj = d_crossed * of_block(b)
        cross_bias_grad[:, cols] = jnp.sum(d_proj, axis=0, keepdims=True)
        rounded = d_proj.astype(BF)
        put(proj_low, b, rounded)
        low_sum[...] += nt(rounded, u[:, cols])
        held[:, cols] = d_crossed * (held[:, cols] + 1.0)
        store(1, proj_low, proj_hbm, b).start()

    low_grad_out[...] = low_sum[...].astype(BF)
    small[1].start()
    stores = list(small)
    for b in range(blocks):
        stores += [store(0, crossed, crossed_hbm, b), store(1, proj_low, proj_hbm, b)]
    for b in range(blocks):
        slots = range(b * per_block, (b + 1) * per_block)
        places = [pl.ds(pl.multiple_of(fmap[s] * width, width), width) for s in slots]
        kept = jnp.concatenate([held[:, place] for place in places], axis=1)
        right = jnp.concatenate([v[place, :] for place in places], axis=0)
        result = (kept + nt(low_grad_out[...], right)).astype(BF)
        put(d_inter, b, result)
        copy = store(2, d_inter, back, b)
        copy.start()
        stores.append(copy)
    for copy in stores:
        copy.wait()


def dense(fmap, received, labels, v, u, cross_bias, h, hidden_bias, out_weight, scale):
    features, batch, width = received.shape
    total_width = features * width
    rank = v.shape[1]
    units = h.shape[1]
    vmem = pl.BlockSpec(memory_space=pltpu.VMEM)
    smem = pl.BlockSpec(memory_space=pltpu.SMEM)
    hbm = pl.BlockSpec(memory_space=pltpu.HBM)
    return pl.pallas_call(
        functools.partial(dense_kernel, scale),
        name="dense",
        in_specs=[smem, hbm, vmem, hbm, hbm, vmem, hbm, vmem, vmem],
        out_specs=[hbm] * 6 + [vmem] * 3,
        out_shape=[
            jax.ShapeDtypeStruct(received.shape, BF),
            jax.ShapeDtypeStruct(received.shape, BF),
            jax.ShapeDtypeStruct(received.shape, BF),
            jax.ShapeDtypeStruct((batch, rank), BF),
            jax.ShapeDtypeStruct((batch, rank), BF),
            jax.ShapeDtypeStruct((batch, units), BF),
            jax.ShapeDtypeStruct((1, total_width), F32),
            jax.ShapeDtypeStruct((1, units), F32),
            jax.ShapeDtypeStruct((1, units), F32),
        ],
        scratch_shapes=[
            pltpu.VMEM(received.shape, BF),
            pltpu.VMEM(received.shape, BF),
            pltpu.VMEM(received.shape, BF),
            pltpu.VMEM((batch, total_width), F32),
            pltpu.VMEM(received.shape, BF),
            pltpu.VMEM(v.shape, BF),
            pltpu.VMEM(u.shape, BF),
            pltpu.VMEM(h.shape, BF),
            pltpu.VMEM((batch, rank), BF),
            pltpu.VMEM((batch, rank), BF),
            pltpu.VMEM((batch, units), BF),
            pltpu.VMEM((batch, units), F32),
            pltpu.VMEM((batch, rank), F32),
            pltpu.SMEM((features,), jnp.int32),
            pltpu.SemaphoreType.DMA,
            pltpu.SemaphoreType.DMA((3,)),
            pltpu.SemaphoreType.DMA((3,)),
            pltpu.SemaphoreType.DMA((3, total_width // WIDE)),
        ],
        compiler_params=pltpu.CompilerParams(vmem_limit_bytes=DENSE_VMEM),
    )(fmap, received, labels, v, u, cross_bias, h, hidden_bias, out_weight)


def gradients_kernel(
    order,
    place,
    fmap,
    received,
    crossed,
    proj,
    low_hbm,
    low_grad_hbm,
    d_hidden_hbm,
    cross_bias_grad,
    hidden_bias_grad,
    out_weight_grad,
    *rest,
):
    parts, chunks = len(order), len(ORDER)
    outs = rest[: 2 * parts]
    inter_in, crossed_in, proj_in, low, low_grad, d_hidden = rest[2 * parts : 2 * parts + 6]
    low_t, low_grad_t, d_hidden_t, small, keep, send = rest[2 * parts + 6 : -5]
    slot_of, small_sems, inter_sem, wide_sems, out_sems = rest[-5:]
    features = fmap.shape[0]
    width = keep.shape[-1]
    rank = low_t.shape[0]
    each = features // chunks
    share = each // PAIR

    smalls = [
        pltpu.make_async_copy(source, target, small_sems.at[i])
        for i, (source, target) in enumerate(
            ((low_hbm, low), (low_grad_hbm, low_grad), (d_hidden_hbm, d_hidden))
        )
    ]
    for copy in smalls:
        copy.start()
    for s in range(features):
        slot_of[fmap[s]] = s
    loads = []
    for part, offset in enumerate(order):
        base = lax.rem(place[1] + offset, chunks) * each
        span = pl.ds(part * each, each)
        copies = [
            pltpu.make_async_copy(crossed.at[pl.ds(base, each)], crossed_in.at[span], wide_sems.at[0, part]),
            pltpu.make_async_copy(proj.at[pl.ds(base, each)], proj_in.at[span], wide_sems.at[1, part]),
        ]
        loads.append(copies)
    whole = pltpu.make_async_copy(received, inter_in, inter_sem)
    whole.start()
    for copy in loads[0]:
        copy.start()
    for copy in smalls:
        copy.wait()

    low_t[...] = low[...].astype(F32).T.astype(BF)
    low_grad_t[...] = low_grad[...].astype(F32).T.astype(BF)
    d_hidden_t[...] = d_hidden[...].astype(F32).T.astype(BF)
    quarters = 4
    units = hidden_bias_grad.shape[1]
    per = units // (features * quarters)
    mine = lax.broadcasted_iota(jnp.int32, (features, units), 0)
    unit = lax.broadcasted_iota(jnp.int32, (features, units), 1)
    mine = unit // (per * quarters) == mine
    unit = lax.broadcasted_iota(jnp.int32, (units, width), 0)
    lane = lax.broadcasted_iota(jnp.int32, (units, width), 1)
    within = unit % (per * quarters)
    spread = (within // per * (width // quarters) + within % per == lane).astype(F32)
    for i, grad in enumerate((hidden_bias_grad, out_weight_grad)):
        small[i] = jnp.dot(
            jnp.where(mine, grad[...], 0.0),
            spread,
            preferred_element_type=F32,
            precision=lax.Precision.HIGHEST,
        )

    def stores(part, k):
        span, place_out = pl.ds(part * each + k * PAIR, PAIR), pl.ds(k * PAIR, PAIR)
        return [
            pltpu.make_async_copy(source.at[span], outs[i].at[place_out], out_sems.at[i, k])
            for i, source in ((parts + part, send), (part, keep))
        ]

    line = lax.broadcasted_iota(jnp.int32, (EXTRA, width), 0)
    nothing = jnp.zeros((EXTRA, width), BF)
    first = place[0] == 0

    whole.wait()
    for part, offset in enumerate(order):
        for copy in loads[part]:
            copy.wait()
        if part + 1 < parts:
            for copy in loads[part + 1]:
                copy.start()

        @pl.loop(0, share)
        def _(k, part=part, offset=offset):
            base = lax.rem(place[1] + offset, chunks) * each + k * PAIR
            n = part * each + k * PAIR

            def product(left, *right):
                both = jnp.concatenate(right, axis=1)
                return jnp.dot(left[...], both, preferred_element_type=F32).astype(BF)

            of_v = product(low_grad_t, *[inter_in[slot_of[base + i]] for i in range(PAIR)])
            of_u = product(low_t, *[proj_in[n + i] for i in range(PAIR)])
            of_h = product(d_hidden_t, *[crossed_in[n + i] for i in range(PAIR)])

            def fill(one, other):
                for i in range(PAIR):
                    lanes = slice(i * width, (i + 1) * width)
                    f = base + i
                    cross = cross_bias_grad[:, pl.ds(pl.multiple_of(f * width, width), width)]
                    extra = jnp.where(line == 0, cross, 0.0)
                    for j in range(2):
                        extra = jnp.where(line == j + 1, small[j, pl.ds(f, 1), :], extra)
                    one[n + i, 0, pl.ds(0, rank), :] = of_v[:, lanes]
                    one[n + i, 0, pl.ds(rank, EXTRA), :] = extra.astype(BF)
                    one[n + i, 1, pl.ds(0, rank), :] = of_u[:, lanes]
                    one[n + i, 1, pl.ds(rank, EXTRA), :] = nothing
                    other[n + i, 0, pl.ds(0, rank), :] = of_h[:rank, lanes]
                    other[n + i, 0, pl.ds(rank, EXTRA), :] = nothing
                    other[n + i, 1, pl.ds(0, rank), :] = of_h[rank:, lanes]
                    other[n + i, 1, pl.ds(rank, EXTRA), :] = nothing

            @pl.when(first)
            def _():
                fill(keep, send)

            @pl.when(jnp.logical_not(first))
            def _():
                fill(send, keep)

            for copy in stores(part, k):
                copy.start()

    for part in range(parts):
        for k in range(share):
            for copy in stores(part, k):
                copy.wait()


def gradients(order, place, fmap, received, crossed, proj, low, low_grad, d_hidden, *small):
    features, batch, width = received.shape
    rank, units = low.shape[1], d_hidden.shape[1]
    parts = len(order)
    held = features // len(ORDER) * parts
    part = jax.ShapeDtypeStruct((features // len(ORDER), 2, rank + EXTRA, width), BF)
    vmem = pl.BlockSpec(memory_space=pltpu.VMEM)
    smem = pl.BlockSpec(memory_space=pltpu.SMEM)
    hbm = pl.BlockSpec(memory_space=pltpu.HBM)
    outs = pl.pallas_call(
        functools.partial(gradients_kernel, order),
        name="gradients",
        in_specs=[smem, smem] + [hbm] * 6 + [vmem] * 3,
        out_specs=[hbm] * (2 * parts),
        out_shape=[part] * (2 * parts),
        scratch_shapes=[pltpu.VMEM((features, batch, width), BF)]
        + [pltpu.VMEM((held, batch, width), BF)] * 2
        + [
            pltpu.VMEM((batch, rank), BF),
            pltpu.VMEM((batch, rank), BF),
            pltpu.VMEM((batch, units), BF),
            pltpu.VMEM((rank, batch), BF),
            pltpu.VMEM((rank, batch), BF),
            pltpu.VMEM((units, batch), BF),
            pltpu.VMEM((2, features, width), F32),
            pltpu.VMEM((held, 2, rank + EXTRA, width), BF),
            pltpu.VMEM((held, 2, rank + EXTRA, width), BF),
            pltpu.SMEM((features,), jnp.int32),
            pltpu.SemaphoreType.DMA((3,)),
            pltpu.SemaphoreType.DMA,
            pltpu.SemaphoreType.DMA((2, parts)),
            pltpu.SemaphoreType.DMA((2 * parts, features // len(ORDER) // PAIR)),
        ],
        compiler_params=pltpu.CompilerParams(vmem_limit_bytes=GRADIENTS_VMEM),
        cost_estimate=pl.CostEstimate(
            flops=2 * batch * held * width * (2 * rank + units),
            bytes_accessed=held << 19,
            transcendentals=0,
        ),
    )(place, fmap, received, crossed, proj, low, low_grad, d_hidden, *small)
    return outs[:parts], outs[parts:]


def fold_kernel(own, swapped, from_following, from_preceding, out):
    features, _, lines, width = own.shape
    quarters = out.shape[0] // features
    rank = lines - EXTRA

    @pl.loop(0, features)
    def _(f):
        total = own[f].astype(F32) + swapped[f].astype(F32)
        total = total + from_following[f].astype(F32) + from_preceding[f].astype(F32)
        filler = jnp.zeros((width - EXTRA, width), F32)
        extra = jnp.concatenate([total[0, rank:], filler], axis=0)
        across = [total[0, :rank].T, total[1, :rank].T, extra.T]
        across = jnp.concatenate(across, axis=1).astype(BF)
        for j in range(quarters):
            out[f * quarters + j] = across[j * width // quarters : (j + 1) * width // quarters]


def fold(quarters, *parts):
    features, _, lines, width = parts[0].shape
    vmem = pl.BlockSpec(memory_space=pltpu.VMEM)
    shape = (features * quarters, width // quarters, 2 * (lines - EXTRA) + width)
    return pl.pallas_call(
        fold_kernel,
        name="fold",
        in_specs=[vmem] * 4,
        out_specs=vmem,
        out_shape=jax.ShapeDtypeStruct(shape, BF),
        compiler_params=pltpu.CompilerParams(vmem_limit_bytes=VMEM),
    )(*parts)


def finish_kernel(pieces, grad_v, grad_u, grad_h, cross_bias, hidden_bias, out_weight):
    sources = pieces.shape[0]
    rank = grad_v.shape[1]
    sums = []
    for core in range(2):
        total = pieces[core].astype(F32)
        for source in range(core + 2, sources, 2):
            total = total + pieces[source].astype(F32)
        sums.append(total)
    grad_v[...] = sums[0][:, :rank]
    grad_u[...] = sums[0][:, rank : 2 * rank]
    grad_h[...] = sums[1][:, : 2 * rank]
    small = sums[0][:, 2 * rank :].T
    cross_bias[...] = small[0:1]
    hidden_bias[...] = small[1:2, : hidden_bias.shape[1]]
    out_weight[...] = small[2:3, : out_weight.shape[1]]


def finish(pieces, rank, units, per):
    share = pieces.shape[1]
    vmem = pl.BlockSpec(memory_space=pltpu.VMEM)
    shapes = ((share, rank), (share, rank), (share, units), (1, share), (1, per), (1, per))
    return pl.pallas_call(
        finish_kernel,
        name="finish",
        in_specs=[vmem],
        out_specs=[vmem] * 6,
        out_shape=[jax.ShapeDtypeStruct(shape, F32) for shape in shapes],
        compiler_params=pltpu.CompilerParams(vmem_limit_bytes=VMEM),
    )(pieces)


def neighbours(axis):
    size = lax.axis_size(axis)
    up = [(i, (i + 1) % size) for i in range(size)]
    down = [(i, (i - 1) % size) for i in range(size)]
    return (
        lambda value: lax.ppermute(value, axis, up),
        lambda value: lax.ppermute(value, axis, down),
    )


def add(*terms):
    total = terms[0].astype(F32)
    for term in terms[1:]:
        total = total + term.astype(F32)
    return total.astype(BF)


def ring_parts(axis, opposite, following, preceding):
    up, down = neighbours(axis)
    passed = (down(opposite[0]), up(opposite[1]))
    from_following = down(jnp.concatenate([add(preceding[0], passed[0]), preceding[1]], axis=0))
    from_preceding = up(jnp.concatenate([following[0], add(following[1], passed[1])], axis=0))
    return from_following, from_preceding


def ring_spread(axis, own):
    up, down = neighbours(axis)
    preceding, following = up(own), down(own)
    half = own.shape[0] // 2
    return own, following, down(following[:half]), up(preceding[half:]), preceding


def body(
    embedding_table,
    touched_blocks,
    bag_index,
    bag_count,
    feature_map,
    labels,
    v_weight,
    u_weight,
    cross_bias,
    hidden_weight,
    hidden_bias,
    out_weight,
):
    dp = ("x", "zh", "zl", "core")
    features = feature_map.shape[0]
    rows, width = embedding_table.shape
    samples = bag_index.shape[1]
    tile = samples // touched_blocks.shape[1]
    batch = labels.shape[0]
    rank = v_weight.shape[1]
    units = hidden_weight.shape[1]
    roles = lax.axis_size("role")
    total = roles * lax.axis_size(dp) * batch
    core = lax.axis_index("core")
    role = lax.axis_index("role")

    touched = touched_blocks[0].T
    pooled, incidence = pool(touched, embedding_table, bag_index[0].T, bag_count[0].T, tile)
    received = lax.all_to_all(
        pooled.reshape(features, batch, width), dp, split_axis=0, concat_axis=0, tiled=True
    )
    back, crossed, proj, low, low_grad, d_hidden, cross_g, hidden_g, out_g = dense(
        feature_map,
        received,
        labels.reshape(batch, 1),
        v_weight,
        u_weight,
        cross_bias.reshape(1, -1),
        hidden_weight,
        hidden_bias.reshape(1, -1),
        out_weight.reshape(1, -1),
        LOSS_SCALE / total,
    )
    returned = lax.all_to_all(back, dp, split_axis=0, concat_axis=0, tiled=True)

    quarters = 4
    share = width // quarters
    per = units // (features * quarters)

    swap = [(0, 1), (1, 0)]
    each = features // roles
    keep, send = gradients(
        ORDER,
        jnp.stack([core, role]),
        feature_map,
        received,
        crossed,
        proj,
        low,
        low_grad,
        d_hidden,
        cross_g,
        hidden_g,
        out_g,
    )
    others = [lax.ppermute(sent, "core", [(0, 1), (1, 0)]) for sent in send]
    halves = []
    for mine, other in zip(keep[:3], others):
        cuts = (slice(0, each // 2), slice(each // 2, each))
        halves.append([add(mine[cut], other[cut]) for cut in cuts])
    local = scatter(touched, incidence, returned.reshape(samples, width), rows, roles)
    parts = lax.all_to_all(local, "role", split_axis=0, concat_axis=0, tiled=True)
    quarters = 4
    folded = fold(quarters, keep[3], others[3], *ring_parts("role", *halves))
    folded, parts = lax.optimization_barrier((folded, parts))
    pieces = lax.all_to_all(folded, dp, split_axis=0, concat_axis=0, tiled=True)
    per = units // (features * quarters)
    grad_v, grad_u, grad_h, grad_cb, grad_hb, grad_ow = finish(pieces, rank, units, per)
    part = add(*parts)
    table_grad = spread_rows(role.reshape(1), ring_spread("role", part), roles)
    return (
        table_grad,
        grad_v,
        grad_u.T,
        grad_cb.reshape(-1),
        grad_h,
        grad_hb.reshape(-1),
        grad_ow.reshape(-1),
    )


def solution(mesh):
    fine = Mesh(mesh.devices.reshape(4, 4, 2, 2, 2), ("role", "x", "zh", "zl", "core"))
    dp = ("x", "zh", "zl", "core")
    everywhere = ("role",) + dp
    return jax.shard_map(
        body,
        mesh=fine,
        in_specs=(
            P(dp, None),
            P(dp, "role", None),
            P(dp, "role", None),
            P(dp, "role", None),
            P(),
            P(everywhere),
            P(),
            P(),
            P(),
            P(),
            P(),
            P(),
        ),
        out_specs=(
            P(dp, None),
            P(everywhere, None),
            P(None, everywhere),
            P(everywhere),
            P(everywhere, None),
            P(everywhere),
            P(everywhere),
        ),
        check_vma=False,
    )
```

```python
import functools

import jax
import jax.numpy as jnp
from jax import lax
from jax.experimental import pallas as pl
from jax.experimental.pallas import tpu as pltpu
from jax.sharding import Mesh
from jax.sharding import PartitionSpec as P

BLK = 8
LOSS_SCALE = 65536.0
STEP_TILES = 16
WIDE = 2048
EXTRA = 16
PAIR = 4
ORDER = (2, 1, 3, 0)
VMEM = 60 << 20
POOL_VMEM = VMEM
DENSE_VMEM = 52 << 20
GRADIENTS_VMEM = 52 << 20
SMALL_VMEM = 40 << 20
SCATTER_VMEM = 52 << 20

BF = jnp.bfloat16
F32 = jnp.float32


def nt(left, right):
    return lax.dot_general(left, right, (((1,), (1,)), ((), ())), preferred_element_type=F32)


def pool_kernel(touched, table, index, count, pooled, incidence, *scratch):
    rows16, rows32, index_in, count_in, held, tiles_held, table_sem, in_sems, out_sems = scratch
    tiles, tile, _ = incidence.shape
    steps = tiles // STEP_TILES
    span = STEP_TILES * tile

    def loads(step):
        part = pl.ds(pl.multiple_of(step * span, span), span)
        return (
            pltpu.make_async_copy(index.at[:, part], index_in.at[:, part], in_sems.at[0, step]),
            pltpu.make_async_copy(count.at[:, part], count_in.at[:, part], in_sems.at[1, step]),
        )

    def stores(step):
        part = pl.ds(pl.multiple_of(step * span, span), span)
        some = pl.ds(step * STEP_TILES, STEP_TILES)
        return (
            pltpu.make_async_copy(held.at[part], pooled.at[part], out_sems.at[0, step]),
            pltpu.make_async_copy(tiles_held.at[some], incidence.at[some], out_sems.at[1, step]),
        )

    whole = pltpu.make_async_copy(table, rows16, table_sem)
    whole.start()
    for step in range(steps):
        for copy in loads(step):
            copy.start()
    whole.wait()
    rows32[...] = rows16[...].astype(F32)
    listed = lax.broadcasted_iota(jnp.int32, (tile, tile), 0).astype(BF)

    @pl.loop(0, steps)
    def _(step):
        for copy in loads(step):
            copy.wait()
        for i in range(STEP_TILES):
            t = step * STEP_TILES + i
            part = pl.ds(pl.multiple_of(t * tile, tile), tile)
            idx = index_in[:, part].astype(BF)
            cnt = count_in[:, part].astype(BF)
            total = jnp.zeros((tile, tile), BF)
            for j in range(index.shape[0]):
                total += jnp.where(idx[j : j + 1] == listed, cnt[j : j + 1], jnp.zeros((), BF))
            tiles_held[t] = total
            blocks = [
                rows32[pl.ds(pl.multiple_of(touched[k, t] * BLK, BLK), BLK), :]
                for k in range(touched.shape[0])
            ]
            picked = jnp.concatenate(blocks, axis=0).astype(BF)
            held[part, :] = lax.dot_general(
                total, picked, (((0,), (0,)), ((), ())), preferred_element_type=F32
            ).astype(BF)
        for copy in stores(step):
            copy.start()

    for step in range(steps):
        for copy in stores(step):
            copy.wait()


def pool(touched, table, index, count, tile):
    hot, samples = index.shape
    tiles = samples // tile
    width = table.shape[1]
    steps = tiles // STEP_TILES
    hbm = pl.BlockSpec(memory_space=pltpu.HBM)
    return pl.pallas_call(
        pool_kernel,
        name="pool",
        in_specs=[pl.BlockSpec(memory_space=pltpu.SMEM), hbm, hbm, hbm],
        out_specs=[hbm, hbm],
        out_shape=[
            jax.ShapeDtypeStruct((samples, width), BF),
            jax.ShapeDtypeStruct((tiles, tile, tile), BF),
        ],
        scratch_shapes=[
            pltpu.VMEM(table.shape, BF),
            pltpu.VMEM(table.shape, F32),
            pltpu.VMEM(index.shape, jnp.int32),
            pltpu.VMEM(count.shape, jnp.int32),
            pltpu.VMEM((samples, width), BF),
            pltpu.VMEM((tiles, tile, tile), BF),
            pltpu.SemaphoreType.DMA,
            pltpu.SemaphoreType.DMA((2, steps)),
            pltpu.SemaphoreType.DMA((2, steps)),
        ],
        compiler_params=pltpu.CompilerParams(vmem_limit_bytes=POOL_VMEM),
    )(touched, table, index, count)


def scatter_kernel(touched, incidence, grad, out, *scratch):
    sums, (tiles_in, sems) = scratch[:-2], scratch[-2:]
    tiles, tile, _ = incidence.shape
    chunks, rows, _ = out.shape
    steps = tiles // STEP_TILES

    def load(step):
        part = pl.ds(step * STEP_TILES, STEP_TILES)
        return pltpu.make_async_copy(incidence.at[part], tiles_in.at[part], sems.at[step])

    for step in range(steps):
        load(step).start()
    for acc in sums:
        acc[...] = jnp.zeros_like(acc)

    @pl.loop(0, steps)
    def _(step):
        load(step).wait()
        for i in range(STEP_TILES):
            t = step * STEP_TILES + i
            product = jnp.dot(
                tiles_in[t], grad[pl.ds(t * tile, tile), :], preferred_element_type=F32
            )
            for k in range(touched.shape[0]):
                acc = sums[k % len(sums)]
                place = pl.ds(pl.multiple_of(touched[k, t] * BLK, BLK), BLK)
                acc[place, :] += product[k * BLK : (k + 1) * BLK]

    for i in range(chunks):
        place = pl.ds(i * rows, rows)
        total = sums[0][place, :]
        for acc in sums[1:]:
            total = total + acc[place, :]
        out[i] = total.astype(out.dtype)


def scatter(touched, incidence, grad, rows, chunks):
    tiles, tile, _ = incidence.shape
    width = grad.shape[1]
    steps = tiles // STEP_TILES
    smem = pl.BlockSpec(memory_space=pltpu.SMEM)
    hbm = pl.BlockSpec(memory_space=pltpu.HBM)
    vmem = pl.BlockSpec(memory_space=pltpu.VMEM)
    return pl.pallas_call(
        scatter_kernel,
        name="scatter",
        in_specs=[smem, hbm, vmem],
        out_specs=vmem,
        out_shape=jax.ShapeDtypeStruct((chunks, rows // chunks, width), BF),
        scratch_shapes=[pltpu.VMEM((rows, width), F32)] * 4
        + [
            pltpu.VMEM(incidence.shape, BF),
            pltpu.SemaphoreType.DMA((steps,)),
        ],
        compiler_params=pltpu.CompilerParams(vmem_limit_bytes=SCATTER_VMEM),
        cost_estimate=pl.CostEstimate(flops=1 << 33, bytes_accessed=8 << 20, transcendentals=0),
    )(touched, incidence, grad)


def spread_kernel(role, own, following, opposite_a, opposite_b, preceding, out):
    rows = own.shape[0]
    half = rows // 2
    chunks = out.shape[0] // rows

    def place(offset, size, piece):
        first = lax.rem(role[0] + offset, chunks) * rows
        out[pl.ds(pl.multiple_of(first, rows) + size, piece.shape[0]), :] = piece[...].astype(F32)

    place(0, 0, own)
    place(1, 0, following)
    place(2, 0, opposite_a)
    place(2, half, opposite_b)
    place(3, 0, preceding)


def spread_rows(role, pieces, chunks):
    rows, width = pieces[0].shape
    vmem = pl.BlockSpec(memory_space=pltpu.VMEM)
    return pl.pallas_call(
        spread_kernel,
        name="spread_rows",
        in_specs=[pl.BlockSpec(memory_space=pltpu.SMEM)] + [vmem] * 5,
        out_specs=vmem,
        out_shape=jax.ShapeDtypeStruct((chunks * rows, width), F32),
        compiler_params=pltpu.CompilerParams(vmem_limit_bytes=SMALL_VMEM),
    )(role, *pieces)


def dense_kernel(
    scale,
    fmap,
    received,
    labels,
    v_hbm,
    u_hbm,
    cross_bias,
    h_hbm,
    hidden_bias,
    out_weight,
    back,
    crossed_hbm,
    proj_hbm,
    low_hbm,
    low_grad_hbm,
    d_hidden_hbm,
    cross_bias_grad,
    hidden_bias_grad,
    out_weight_grad,
    inter,
    crossed,
    proj_low,
    held,
    d_inter,
    v,
    u,
    h,
    low_out,
    low_grad_out,
    d_hidden_out,
    hidden,
    low_sum,
    slot_of,
    in_sem,
    weight_sems,
    small_sems,
    wide_sems,
):
    features, batch, width = received.shape
    total_width = features * width
    blocks = total_width // WIDE
    per_block = WIDE // width

    weights = [
        pltpu.make_async_copy(source, target, weight_sems.at[i])
        for i, (source, target) in enumerate(((v_hbm, v), (u_hbm, u), (h_hbm, h)))
    ]
    weights[0].start()
    load = pltpu.make_async_copy(received, inter, in_sem)
    load.start()
    weights[1].start()
    weights[2].start()

    def store(row, source, target, b):
        part = pl.ds(b * per_block, per_block)
        return pltpu.make_async_copy(source.at[part], target.at[part], wide_sems.at[row, b])

    def of_block(b):
        slots = [slot_of[b * per_block + i] for i in range(per_block)]
        return jnp.concatenate([inter[slot] for slot in slots], axis=1).astype(F32)

    def put(target, b, value):
        for i in range(per_block):
            target[b * per_block + i] = value[:, i * width : (i + 1) * width]

    small = [
        pltpu.make_async_copy(source, target, small_sems.at[i])
        for i, (source, target) in enumerate(
            ((low_out, low_hbm), (low_grad_out, low_grad_hbm), (d_hidden_out, d_hidden_hbm))
        )
    ]
    for s in range(features):
        slot_of[fmap[s]] = s
    low_sum[...] = jnp.zeros_like(low_sum)
    hidden[...] = jnp.broadcast_to(hidden_bias[...], hidden.shape)
    hidden_bias_grad[...] = jnp.zeros_like(hidden_bias_grad)
    out_weight_grad[...] = jnp.zeros_like(out_weight_grad)
    load.wait()
    weights[0].wait()
    for b in range(blocks):
        slots = range(b * per_block, (b + 1) * per_block)
        places = [pl.ds(pl.multiple_of(fmap[s] * width, width), width) for s in slots]
        left = jnp.concatenate([inter[s] for s in slots], axis=1)
        right = jnp.concatenate([v[place, :] for place in places], axis=0)
        low_sum[...] += jnp.dot(left, right, preferred_element_type=F32)

    low_out[...] = low_sum[...].astype(BF)
    small[0].start()
    weights[1].wait()
    weights[2].wait()

    @pl.loop(0, blocks)
    def _(b):
        cols = pl.ds(pl.multiple_of(b * WIDE, WIDE), WIDE)
        projected = (
            jnp.dot(low_out[...], u[:, cols], preferred_element_type=F32) + cross_bias[:, cols]
        )
        held[:, cols] = projected
        x = of_block(b)
        product = (x * projected + x).astype(BF)
        put(crossed, b, product)
        hidden[...] += jnp.dot(product, h[cols, :], preferred_element_type=F32)
        store(0, crossed, crossed_hbm, b).start()

    chunk = 64

    @pl.loop(0, batch // chunk)
    def _(r):
        rows = pl.ds(pl.multiple_of(r * chunk, chunk), chunk)
        pre = hidden[rows, :]
        gate = jax.nn.sigmoid(pre)
        act = (pre * gate).astype(BF).astype(F32)
        weight = out_weight[...].astype(F32)
        logit = jnp.sum(act * weight, axis=1, keepdims=True)
        d_logit = (scale * (jax.nn.sigmoid(logit) - labels[rows, :].astype(F32))).astype(BF)
        d_logit = d_logit.astype(F32)
        d_hidden = (d_logit * weight * (gate * (1.0 + pre * (1.0 - gate)))).astype(BF)
        d_hidden_out[rows, :] = d_hidden
        hidden_bias_grad[...] += jnp.sum(d_hidden.astype(F32), axis=0, keepdims=True)
        out_weight_grad[...] += jnp.sum(d_logit * act, axis=0, keepdims=True)

    small[2].start()
    low_sum[...] = jnp.zeros_like(low_sum)

    @pl.loop(0, blocks)
    def _(b):
        cols = pl.ds(pl.multiple_of(b * WIDE, WIDE), WIDE)
        d_crossed = nt(d_hidden_out[...], h[cols, :])
        d_proj = d_crossed * of_block(b)
        cross_bias_grad[:, cols] = jnp.sum(d_proj, axis=0, keepdims=True)
        rounded = d_proj.astype(BF)
        put(proj_low, b, rounded)
        low_sum[...] += nt(rounded, u[:, cols])
        held[:, cols] = d_crossed * (held[:, cols] + 1.0)
        store(1, proj_low, proj_hbm, b).start()

    low_grad_out[...] = low_sum[...].astype(BF)
    small[1].start()
    stores = list(small)
    for b in range(blocks):
        stores += [store(0, crossed, crossed_hbm, b), store(1, proj_low, proj_hbm, b)]
    for b in range(blocks):
        slots = range(b * per_block, (b + 1) * per_block)
        places = [pl.ds(pl.multiple_of(fmap[s] * width, width), width) for s in slots]
        kept = jnp.concatenate([held[:, place] for place in places], axis=1)
        right = jnp.concatenate([v[place, :] for place in places], axis=0)
        result = (kept + nt(low_grad_out[...], right)).astype(BF)
        put(d_inter, b, result)
        copy = store(2, d_inter, back, b)
        copy.start()
        stores.append(copy)
    for copy in stores:
        copy.wait()


def dense(fmap, received, labels, v, u, cross_bias, h, hidden_bias, out_weight, scale):
    features, batch, width = received.shape
    total_width = features * width
    rank = v.shape[1]
    units = h.shape[1]
    vmem = pl.BlockSpec(memory_space=pltpu.VMEM)
    smem = pl.BlockSpec(memory_space=pltpu.SMEM)
    hbm = pl.BlockSpec(memory_space=pltpu.HBM)
    return pl.pallas_call(
        functools.partial(dense_kernel, scale),
        name="dense",
        in_specs=[smem, vmem, vmem, hbm, hbm, vmem, hbm, vmem, vmem],
        out_specs=[hbm] * 6 + [vmem] * 3,
        out_shape=[
            jax.ShapeDtypeStruct(received.shape, BF),
            jax.ShapeDtypeStruct(received.shape, BF),
            jax.ShapeDtypeStruct(received.shape, BF),
            jax.ShapeDtypeStruct((batch, rank), BF),
            jax.ShapeDtypeStruct((batch, rank), BF),
            jax.ShapeDtypeStruct((batch, units), BF),
            jax.ShapeDtypeStruct((1, total_width), F32),
            jax.ShapeDtypeStruct((1, units), F32),
            jax.ShapeDtypeStruct((1, units), F32),
        ],
        scratch_shapes=[
            pltpu.VMEM(received.shape, BF),
            pltpu.VMEM(received.shape, BF),
            pltpu.VMEM(received.shape, BF),
            pltpu.VMEM((batch, total_width), F32),
            pltpu.VMEM(received.shape, BF),
            pltpu.VMEM(v.shape, BF),
            pltpu.VMEM(u.shape, BF),
            pltpu.VMEM(h.shape, BF),
            pltpu.VMEM((batch, rank), BF),
            pltpu.VMEM((batch, rank), BF),
            pltpu.VMEM((batch, units), BF),
            pltpu.VMEM((batch, units), F32),
            pltpu.VMEM((batch, rank), F32),
            pltpu.SMEM((features,), jnp.int32),
            pltpu.SemaphoreType.DMA,
            pltpu.SemaphoreType.DMA((3,)),
            pltpu.SemaphoreType.DMA((3,)),
            pltpu.SemaphoreType.DMA((3, total_width // WIDE)),
        ],
        compiler_params=pltpu.CompilerParams(vmem_limit_bytes=DENSE_VMEM),
    )(fmap, received, labels, v, u, cross_bias, h, hidden_bias, out_weight)


def gradients_kernel(
    order,
    place,
    fmap,
    received,
    crossed,
    proj,
    low_hbm,
    low_grad_hbm,
    d_hidden_hbm,
    cross_bias_grad,
    hidden_bias_grad,
    out_weight_grad,
    *rest,
):
    parts, chunks = len(order), len(ORDER)
    outs = rest[: 2 * parts]
    inter_in, crossed_in, proj_in, low, low_grad, d_hidden = rest[2 * parts : 2 * parts + 6]
    low_t, low_grad_t, d_hidden_t, small, keep, send = rest[2 * parts + 6 : -5]
    slot_of, small_sems, inter_sem, wide_sems, out_sems = rest[-5:]
    features = fmap.shape[0]
    width = keep.shape[-1]
    rank = low_t.shape[0]
    each = features // chunks
    share = each // PAIR

    smalls = [
        pltpu.make_async_copy(source, target, small_sems.at[i])
        for i, (source, target) in enumerate(
            ((low_hbm, low), (low_grad_hbm, low_grad), (d_hidden_hbm, d_hidden))
        )
    ]
    for copy in smalls:
        copy.start()
    for s in range(features):
        slot_of[fmap[s]] = s
    loads = []
    for part, offset in enumerate(order):
        base = lax.rem(place[1] + offset, chunks) * each
        span = pl.ds(part * each, each)
        copies = [
            pltpu.make_async_copy(crossed.at[pl.ds(base, each)], crossed_in.at[span], wide_sems.at[0, part]),
            pltpu.make_async_copy(proj.at[pl.ds(base, each)], proj_in.at[span], wide_sems.at[1, part]),
        ]
        loads.append(copies)
    whole = pltpu.make_async_copy(received, inter_in, inter_sem)
    whole.start()
    for copy in loads[0]:
        copy.start()
    for copy in smalls:
        copy.wait()

    low_t[...] = low[...].astype(F32).T.astype(BF)
    low_grad_t[...] = low_grad[...].astype(F32).T.astype(BF)
    d_hidden_t[...] = d_hidden[...].astype(F32).T.astype(BF)
    quarters = 4
    units = hidden_bias_grad.shape[1]
    per = units // (features * quarters)
    mine = lax.broadcasted_iota(jnp.int32, (features, units), 0)
    unit = lax.broadcasted_iota(jnp.int32, (features, units), 1)
    mine = unit // (per * quarters) == mine
    unit = lax.broadcasted_iota(jnp.int32, (units, width), 0)
    lane = lax.broadcasted_iota(jnp.int32, (units, width), 1)
    within = unit % (per * quarters)
    spread = (within // per * (width // quarters) + within % per == lane).astype(F32)
    for i, grad in enumerate((hidden_bias_grad, out_weight_grad)):
        small[i] = jnp.dot(
            jnp.where(mine, grad[...], 0.0),
            spread,
            preferred_element_type=F32,
            precision=lax.Precision.HIGHEST,
        )

    def stores(part, k):
        span, place_out = pl.ds(part * each + k * PAIR, PAIR), pl.ds(k * PAIR, PAIR)
        return [
            pltpu.make_async_copy(source.at[span], outs[i].at[place_out], out_sems.at[i, k])
            for i, source in ((parts + part, send), (part, keep))
        ]

    line = lax.broadcasted_iota(jnp.int32, (EXTRA, width), 0)
    nothing = jnp.zeros((EXTRA, width), BF)
    first = place[0] == 0

    whole.wait()
    for part, offset in enumerate(order):
        for copy in loads[part]:
            copy.wait()
        if part + 1 < parts:
            for copy in loads[part + 1]:
                copy.start()

        @pl.loop(0, share)
        def _(k, part=part, offset=offset):
            base = lax.rem(place[1] + offset, chunks) * each + k * PAIR
            n = part * each + k * PAIR

            def product(left, *right):
                both = jnp.concatenate(right, axis=1)
                return jnp.dot(left[...], both, preferred_element_type=F32).astype(BF)

            of_v = product(low_grad_t, *[inter_in[slot_of[base + i]] for i in range(PAIR)])
            of_u = product(low_t, *[proj_in[n + i] for i in range(PAIR)])
            of_h = product(d_hidden_t, *[crossed_in[n + i] for i in range(PAIR)])

            def fill(one, other):
                for i in range(PAIR):
                    lanes = slice(i * width, (i + 1) * width)
                    f = base + i
                    cross = cross_bias_grad[:, pl.ds(pl.multiple_of(f * width, width), width)]
                    extra = jnp.where(line == 0, cross, 0.0)
                    for j in range(2):
                        extra = jnp.where(line == j + 1, small[j, pl.ds(f, 1), :], extra)
                    one[n + i, 0, pl.ds(0, rank), :] = of_v[:, lanes]
                    one[n + i, 0, pl.ds(rank, EXTRA), :] = extra.astype(BF)
                    one[n + i, 1, pl.ds(0, rank), :] = of_u[:, lanes]
                    one[n + i, 1, pl.ds(rank, EXTRA), :] = nothing
                    other[n + i, 0, pl.ds(0, rank), :] = of_h[:rank, lanes]
                    other[n + i, 0, pl.ds(rank, EXTRA), :] = nothing
                    other[n + i, 1, pl.ds(0, rank), :] = of_h[rank:, lanes]
                    other[n + i, 1, pl.ds(rank, EXTRA), :] = nothing

            @pl.when(first)
            def _():
                fill(keep, send)

            @pl.when(jnp.logical_not(first))
            def _():
                fill(send, keep)

            for copy in stores(part, k):
                copy.start()

    for part in range(parts):
        for k in range(share):
            for copy in stores(part, k):
                copy.wait()


def gradients(order, place, fmap, received, crossed, proj, low, low_grad, d_hidden, *small):
    features, batch, width = received.shape
    rank, units = low.shape[1], d_hidden.shape[1]
    parts = len(order)
    held = features // len(ORDER) * parts
    part = jax.ShapeDtypeStruct((features // len(ORDER), 2, rank + EXTRA, width), BF)
    vmem = pl.BlockSpec(memory_space=pltpu.VMEM)
    smem = pl.BlockSpec(memory_space=pltpu.SMEM)
    hbm = pl.BlockSpec(memory_space=pltpu.HBM)
    outs = pl.pallas_call(
        functools.partial(gradients_kernel, order),
        name="gradients",
        in_specs=[smem, smem, vmem] + [hbm] * 5 + [vmem] * 3,
        out_specs=[hbm] * (2 * parts),
        out_shape=[part] * (2 * parts),
        scratch_shapes=[pltpu.VMEM((features, batch, width), BF)]
        + [pltpu.VMEM((held, batch, width), BF)] * 2
        + [
            pltpu.VMEM((batch, rank), BF),
            pltpu.VMEM((batch, rank), BF),
            pltpu.VMEM((batch, units), BF),
            pltpu.VMEM((rank, batch), BF),
            pltpu.VMEM((rank, batch), BF),
            pltpu.VMEM((units, batch), BF),
            pltpu.VMEM((2, features, width), F32),
            pltpu.VMEM((held, 2, rank + EXTRA, width), BF),
            pltpu.VMEM((held, 2, rank + EXTRA, width), BF),
            pltpu.SMEM((features,), jnp.int32),
            pltpu.SemaphoreType.DMA((3,)),
            pltpu.SemaphoreType.DMA,
            pltpu.SemaphoreType.DMA((2, parts)),
            pltpu.SemaphoreType.DMA((2 * parts, features // len(ORDER) // PAIR)),
        ],
        compiler_params=pltpu.CompilerParams(vmem_limit_bytes=GRADIENTS_VMEM),
        cost_estimate=pl.CostEstimate(
            flops=2 * batch * held * width * (2 * rank + units),
            bytes_accessed=held << 19,
            transcendentals=0,
        ),
    )(place, fmap, received, crossed, proj, low, low_grad, d_hidden, *small)
    return outs[:parts], outs[parts:]


def fold_kernel(own, swapped, from_following, from_preceding, out):
    features, _, lines, width = own.shape
    quarters = out.shape[0] // features
    rank = lines - EXTRA

    @pl.loop(0, features)
    def _(f):
        total = own[f].astype(F32) + swapped[f].astype(F32)
        total = total + from_following[f].astype(F32) + from_preceding[f].astype(F32)
        filler = jnp.zeros((width - EXTRA, width), F32)
        extra = jnp.concatenate([total[0, rank:], filler], axis=0)
        across = [total[0, :rank].T, total[1, :rank].T, extra.T]
        across = jnp.concatenate(across, axis=1).astype(BF)
        for j in range(quarters):
            out[f * quarters + j] = across[j * width // quarters : (j + 1) * width // quarters]


def fold(quarters, *parts):
    features, _, lines, width = parts[0].shape
    vmem = pl.BlockSpec(memory_space=pltpu.VMEM)
    shape = (features * quarters, width // quarters, 2 * (lines - EXTRA) + width)
    return pl.pallas_call(
        fold_kernel,
        name="fold",
        in_specs=[vmem] * 4,
        out_specs=vmem,
        out_shape=jax.ShapeDtypeStruct(shape, BF),
        compiler_params=pltpu.CompilerParams(vmem_limit_bytes=SMALL_VMEM),
    )(*parts)


def finish_kernel(pieces, grad_v, grad_u, grad_h, cross_bias, hidden_bias, out_weight):
    sources = pieces.shape[0]
    rank = grad_v.shape[1]
    sums = []
    for core in range(2):
        total = pieces[core].astype(F32)
        for source in range(core + 2, sources, 2):
            total = total + pieces[source].astype(F32)
        sums.append(total)
    grad_v[...] = sums[0][:, :rank]
    grad_u[...] = sums[0][:, rank : 2 * rank]
    grad_h[...] = sums[1][:, : 2 * rank]
    small = sums[0][:, 2 * rank :].T
    cross_bias[...] = small[0:1]
    hidden_bias[...] = small[1:2, : hidden_bias.shape[1]]
    out_weight[...] = small[2:3, : out_weight.shape[1]]


def finish(pieces, rank, units, per):
    share = pieces.shape[1]
    vmem = pl.BlockSpec(memory_space=pltpu.VMEM)
    shapes = ((share, rank), (share, rank), (share, units), (1, share), (1, per), (1, per))
    return pl.pallas_call(
        finish_kernel,
        name="finish",
        in_specs=[vmem],
        out_specs=[vmem] * 6,
        out_shape=[jax.ShapeDtypeStruct(shape, F32) for shape in shapes],
        compiler_params=pltpu.CompilerParams(vmem_limit_bytes=SMALL_VMEM),
    )(pieces)


def neighbours(axis):
    size = lax.axis_size(axis)
    up = [(i, (i + 1) % size) for i in range(size)]
    down = [(i, (i - 1) % size) for i in range(size)]
    return (
        lambda value: lax.ppermute(value, axis, up),
        lambda value: lax.ppermute(value, axis, down),
    )


def add(*terms):
    total = terms[0].astype(F32)
    for term in terms[1:]:
        total = total + term.astype(F32)
    return total.astype(BF)


def ring_parts(axis, opposite, following, preceding):
    up, down = neighbours(axis)
    passed = (down(opposite[0]), up(opposite[1]))
    from_following = down(jnp.concatenate([add(preceding[0], passed[0]), preceding[1]], axis=0))
    from_preceding = up(jnp.concatenate([following[0], add(following[1], passed[1])], axis=0))
    return from_following, from_preceding


def ring_spread(axis, own):
    up, down = neighbours(axis)
    preceding, following = up(own), down(own)
    half = own.shape[0] // 2
    return own, following, down(following[:half]), up(preceding[half:]), preceding


def body(
    embedding_table,
    touched_blocks,
    bag_index,
    bag_count,
    feature_map,
    labels,
    v_weight,
    u_weight,
    cross_bias,
    hidden_weight,
    hidden_bias,
    out_weight,
):
    dp = ("x", "zh", "zl", "core")
    features = feature_map.shape[0]
    rows, width = embedding_table.shape
    samples = bag_index.shape[1]
    tile = samples // touched_blocks.shape[1]
    batch = labels.shape[0]
    rank = v_weight.shape[1]
    units = hidden_weight.shape[1]
    roles = lax.axis_size("role")
    total = roles * lax.axis_size(dp) * batch
    core = lax.axis_index("core")
    role = lax.axis_index("role")

    touched = touched_blocks[0].T
    pooled, incidence = pool(touched, embedding_table, bag_index[0].T, bag_count[0].T, tile)
    received = lax.all_to_all(
        pooled.reshape(features, batch, width), dp, split_axis=0, concat_axis=0, tiled=True
    )
    back, crossed, proj, low, low_grad, d_hidden, cross_g, hidden_g, out_g = dense(
        feature_map,
        received,
        labels.reshape(batch, 1),
        v_weight,
        u_weight,
        cross_bias.reshape(1, -1),
        hidden_weight,
        hidden_bias.reshape(1, -1),
        out_weight.reshape(1, -1),
        LOSS_SCALE / total,
    )
    returned = lax.all_to_all(back, dp, split_axis=0, concat_axis=0, tiled=True)

    quarters = 4
    share = width // quarters
    per = units // (features * quarters)

    swap = [(0, 1), (1, 0)]
    each = features // roles
    keep, send = gradients(
        ORDER,
        jnp.stack([core, role]),
        feature_map,
        received,
        crossed,
        proj,
        low,
        low_grad,
        d_hidden,
        cross_g,
        hidden_g,
        out_g,
    )
    others = [lax.ppermute(sent, "core", [(0, 1), (1, 0)]) for sent in send]
    halves = []
    for mine, other in zip(keep[:3], others):
        cuts = (slice(0, each // 2), slice(each // 2, each))
        halves.append([add(mine[cut], other[cut]) for cut in cuts])
    local = scatter(touched, incidence, returned.reshape(samples, width), rows, roles)
    parts = lax.all_to_all(local, "role", split_axis=0, concat_axis=0, tiled=True)
    quarters = 4
    folded = fold(quarters, keep[3], others[3], *ring_parts("role", *halves))
    folded, parts = lax.optimization_barrier((folded, parts))
    pieces = lax.all_to_all(folded, dp, split_axis=0, concat_axis=0, tiled=True)
    per = units // (features * quarters)
    grad_v, grad_u, grad_h, grad_cb, grad_hb, grad_ow = finish(pieces, rank, units, per)
    part = add(*parts)
    table_grad = spread_rows(role.reshape(1), ring_spread("role", part), roles)
    return (
        table_grad,
        grad_v,
        grad_u.T,
        grad_cb.reshape(-1),
        grad_h,
        grad_hb.reshape(-1),
        grad_ow.reshape(-1),
    )


def solution(mesh):
    fine = Mesh(mesh.devices.reshape(4, 4, 2, 2, 2), ("role", "x", "zh", "zl", "core"))
    dp = ("x", "zh", "zl", "core")
    everywhere = ("role",) + dp
    return jax.shard_map(
        body,
        mesh=fine,
        in_specs=(
            P(dp, None),
            P(dp, "role", None),
            P(dp, "role", None),
            P(dp, "role", None),
            P(),
            P(everywhere),
            P(),
            P(),
            P(),
            P(),
            P(),
            P(),
        ),
        out_specs=(
            P(dp, None),
            P(everywhere, None),
            P(None, everywhere),
            P(everywhere),
            P(everywhere, None),
            P(everywhere),
            P(everywhere),
        ),
        check_vma=False,
    )
```

```python
import functools

import jax
import jax.numpy as jnp
from jax import lax
from jax.experimental import pallas as pl
from jax.experimental.pallas import tpu as pltpu
from jax.sharding import Mesh
from jax.sharding import PartitionSpec as P

BLK = 8
LOSS_SCALE = 65536.0
STEP_TILES = 24
WIDE = 2048
EXTRA = 16
PAIR = 4
ORDER = (2, 1, 3, 0)
VMEM = 60 << 20
POOL_VMEM = VMEM
DENSE_VMEM = 52 << 20
GRADIENTS_VMEM = 52 << 20
SMALL_VMEM = 40 << 20
SCATTER_VMEM = 52 << 20

BF = jnp.bfloat16
F32 = jnp.float32


def nt(left, right):
    return lax.dot_general(left, right, (((1,), (1,)), ((), ())), preferred_element_type=F32)


def pool_kernel(touched, table, index, count, pooled, incidence, *scratch):
    rows16, rows32, index_in, count_in, held, tiles_held, table_sem, in_sems, out_sems = scratch
    tiles, tile, _ = incidence.shape
    steps = tiles // STEP_TILES
    span = STEP_TILES * tile

    def loads(step):
        part = pl.ds(pl.multiple_of(step * span, span), span)
        return (
            pltpu.make_async_copy(index.at[:, part], index_in.at[:, part], in_sems.at[0, step]),
            pltpu.make_async_copy(count.at[:, part], count_in.at[:, part], in_sems.at[1, step]),
        )

    def stores(step):
        part = pl.ds(pl.multiple_of(step * span, span), span)
        some = pl.ds(step * STEP_TILES, STEP_TILES)
        return (
            pltpu.make_async_copy(held.at[part], pooled.at[part], out_sems.at[0, step]),
            pltpu.make_async_copy(tiles_held.at[some], incidence.at[some], out_sems.at[1, step]),
        )

    whole = pltpu.make_async_copy(table, rows16, table_sem)
    whole.start()
    for step in range(steps):
        for copy in loads(step):
            copy.start()
    whole.wait()
    rows32[...] = rows16[...].astype(F32)
    listed = lax.broadcasted_iota(jnp.int32, (tile, tile), 0).astype(BF)

    @pl.loop(0, steps)
    def _(step):
        for copy in loads(step):
            copy.wait()
        for i in range(STEP_TILES):
            t = step * STEP_TILES + i
            part = pl.ds(pl.multiple_of(t * tile, tile), tile)
            idx = index_in[:, part].astype(BF)
            cnt = count_in[:, part].astype(BF)
            total = jnp.zeros((tile, tile), BF)
            for j in range(index.shape[0]):
                total += jnp.where(idx[j : j + 1] == listed, cnt[j : j + 1], jnp.zeros((), BF))
            tiles_held[t] = total
            blocks = [
                rows32[pl.ds(pl.multiple_of(touched[k, t] * BLK, BLK), BLK), :]
                for k in range(touched.shape[0])
            ]
            picked = jnp.concatenate(blocks, axis=0).astype(BF)
            held[part, :] = lax.dot_general(
                total, picked, (((0,), (0,)), ((), ())), preferred_element_type=F32
            ).astype(BF)
        for copy in stores(step):
            copy.start()

    for step in range(steps):
        for copy in stores(step):
            copy.wait()


def pool(touched, table, index, count, tile):
    hot, samples = index.shape
    tiles = samples // tile
    width = table.shape[1]
    steps = tiles // STEP_TILES
    hbm = pl.BlockSpec(memory_space=pltpu.HBM)
    return pl.pallas_call(
        pool_kernel,
        name="pool",
        in_specs=[pl.BlockSpec(memory_space=pltpu.SMEM), hbm, hbm, hbm],
        out_specs=[hbm, hbm],
        out_shape=[
            jax.ShapeDtypeStruct((samples, width), BF),
            jax.ShapeDtypeStruct((tiles, tile, tile), BF),
        ],
        scratch_shapes=[
            pltpu.VMEM(table.shape, BF),
            pltpu.VMEM(table.shape, F32),
            pltpu.VMEM(index.shape, jnp.int32),
            pltpu.VMEM(count.shape, jnp.int32),
            pltpu.VMEM((samples, width), BF),
            pltpu.VMEM((tiles, tile, tile), BF),
            pltpu.SemaphoreType.DMA,
            pltpu.SemaphoreType.DMA((2, steps)),
            pltpu.SemaphoreType.DMA((2, steps)),
        ],
        compiler_params=pltpu.CompilerParams(vmem_limit_bytes=POOL_VMEM),
    )(touched, table, index, count)


def scatter_kernel(touched, incidence, grad, out, *scratch):
    sums, (tiles_in, sems) = scratch[:-2], scratch[-2:]
    tiles, tile, _ = incidence.shape
    chunks, rows, _ = out.shape
    steps = tiles // STEP_TILES

    def load(step):
        part = pl.ds(step * STEP_TILES, STEP_TILES)
        return pltpu.make_async_copy(incidence.at[part], tiles_in.at[part], sems.at[step])

    for step in range(steps):
        load(step).start()
    for acc in sums:
        acc[...] = jnp.zeros_like(acc)

    @pl.loop(0, steps)
    def _(step):
        load(step).wait()
        for i in range(STEP_TILES):
            t = step * STEP_TILES + i
            product = jnp.dot(
                tiles_in[t], grad[pl.ds(t * tile, tile), :], preferred_element_type=F32
            )
            for k in range(touched.shape[0]):
                acc = sums[k % len(sums)]
                place = pl.ds(pl.multiple_of(touched[k, t] * BLK, BLK), BLK)
                acc[place, :] += product[k * BLK : (k + 1) * BLK]

    for i in range(chunks):
        place = pl.ds(i * rows, rows)
        total = sums[0][place, :]
        for acc in sums[1:]:
            total = total + acc[place, :]
        out[i] = total.astype(out.dtype)


def scatter(touched, incidence, grad, rows, chunks):
    tiles, tile, _ = incidence.shape
    width = grad.shape[1]
    steps = tiles // STEP_TILES
    smem = pl.BlockSpec(memory_space=pltpu.SMEM)
    hbm = pl.BlockSpec(memory_space=pltpu.HBM)
    vmem = pl.BlockSpec(memory_space=pltpu.VMEM)
    return pl.pallas_call(
        scatter_kernel,
        name="scatter",
        in_specs=[smem, hbm, vmem],
        out_specs=vmem,
        out_shape=jax.ShapeDtypeStruct((chunks, rows // chunks, width), BF),
        scratch_shapes=[pltpu.VMEM((rows, width), F32)] * 4
        + [
            pltpu.VMEM(incidence.shape, BF),
            pltpu.SemaphoreType.DMA((steps,)),
        ],
        compiler_params=pltpu.CompilerParams(vmem_limit_bytes=SCATTER_VMEM),
        cost_estimate=pl.CostEstimate(flops=1 << 33, bytes_accessed=8 << 20, transcendentals=0),
    )(touched, incidence, grad)


def spread_kernel(role, own, following, opposite_a, opposite_b, preceding, out):
    rows = own.shape[0]
    half = rows // 2
    chunks = out.shape[0] // rows

    def place(offset, size, piece):
        first = lax.rem(role[0] + offset, chunks) * rows
        out[pl.ds(pl.multiple_of(first, rows) + size, piece.shape[0]), :] = piece[...].astype(F32)

    place(0, 0, own)
    place(1, 0, following)
    place(2, 0, opposite_a)
    place(2, half, opposite_b)
    place(3, 0, preceding)


def spread_rows(role, pieces, chunks):
    rows, width = pieces[0].shape
    vmem = pl.BlockSpec(memory_space=pltpu.VMEM)
    return pl.pallas_call(
        spread_kernel,
        name="spread_rows",
        in_specs=[pl.BlockSpec(memory_space=pltpu.SMEM)] + [vmem] * 5,
        out_specs=vmem,
        out_shape=jax.ShapeDtypeStruct((chunks * rows, width), F32),
        compiler_params=pltpu.CompilerParams(vmem_limit_bytes=SMALL_VMEM),
    )(role, *pieces)


def dense_kernel(
    scale,
    fmap,
    received,
    labels,
    v_hbm,
    u_hbm,
    cross_bias,
    h_hbm,
    hidden_bias,
    out_weight,
    back,
    crossed_hbm,
    proj_hbm,
    low_hbm,
    low_grad_hbm,
    d_hidden_hbm,
    cross_bias_grad,
    hidden_bias_grad,
    out_weight_grad,
    crossed,
    proj_low,
    held,
    d_inter,
    v,
    u,
    h,
    low_out,
    low_grad_out,
    d_hidden_out,
    hidden,
    low_sum,
    slot_of,
    weight_sems,
    small_sems,
    wide_sems,
):
    features, batch, width = received.shape
    total_width = features * width
    blocks = total_width // WIDE
    per_block = WIDE // width

    weights = [
        pltpu.make_async_copy(source, target, weight_sems.at[i])
        for i, (source, target) in enumerate(((v_hbm, v), (u_hbm, u), (h_hbm, h)))
    ]
    weights[0].start()
    weights[1].start()
    weights[2].start()

    def store(row, source, target, b):
        part = pl.ds(b * per_block, per_block)
        return pltpu.make_async_copy(source.at[part], target.at[part], wide_sems.at[row, b])

    def of_block(b):
        slots = [slot_of[b * per_block + i] for i in range(per_block)]
        return jnp.concatenate([received[slot] for slot in slots], axis=1).astype(F32)

    def put(target, b, value):
        for i in range(per_block):
            target[b * per_block + i] = value[:, i * width : (i + 1) * width]

    small = [
        pltpu.make_async_copy(source, target, small_sems.at[i])
        for i, (source, target) in enumerate(
            ((low_out, low_hbm), (low_grad_out, low_grad_hbm), (d_hidden_out, d_hidden_hbm))
        )
    ]
    for s in range(features):
        slot_of[fmap[s]] = s
    low_sum[...] = jnp.zeros_like(low_sum)
    hidden[...] = jnp.broadcast_to(hidden_bias[...], hidden.shape)
    hidden_bias_grad[...] = jnp.zeros_like(hidden_bias_grad)
    out_weight_grad[...] = jnp.zeros_like(out_weight_grad)
    weights[0].wait()
    for b in range(blocks):
        slots = range(b * per_block, (b + 1) * per_block)
        places = [pl.ds(pl.multiple_of(fmap[s] * width, width), width) for s in slots]
        left = jnp.concatenate([received[s] for s in slots], axis=1)
        right = jnp.concatenate([v[place, :] for place in places], axis=0)
        low_sum[...] += jnp.dot(left, right, preferred_element_type=F32)

    low_out[...] = low_sum[...].astype(BF)
    small[0].start()
    weights[1].wait()
    weights[2].wait()

    @pl.loop(0, blocks)
    def _(b):
        cols = pl.ds(pl.multiple_of(b * WIDE, WIDE), WIDE)
        projected = (
            jnp.dot(low_out[...], u[:, cols], preferred_element_type=F32) + cross_bias[:, cols]
        )
        held[:, cols] = projected
        x = of_block(b)
        product = (x * projected + x).astype(BF)
        put(crossed, b, product)
        hidden[...] += jnp.dot(product, h[cols, :], preferred_element_type=F32)
        store(0, crossed, crossed_hbm, b).start()

    chunk = 192

    @pl.loop(0, batch // chunk)
    def _(r):
        rows = pl.ds(pl.multiple_of(r * chunk, chunk), chunk)
        pre = hidden[rows, :]
        gate = jax.nn.sigmoid(pre)
        act = (pre * gate).astype(BF).astype(F32)
        weight = out_weight[...].astype(F32)
        logit = jnp.sum(act * weight, axis=1, keepdims=True)
        d_logit = (scale * (jax.nn.sigmoid(logit) - labels[rows, :].astype(F32))).astype(BF)
        d_logit = d_logit.astype(F32)
        d_hidden = (d_logit * weight * (gate * (1.0 + pre * (1.0 - gate)))).astype(BF)
        d_hidden_out[rows, :] = d_hidden
        hidden_bias_grad[...] += jnp.sum(d_hidden.astype(F32), axis=0, keepdims=True)
        out_weight_grad[...] += jnp.sum(d_logit * act, axis=0, keepdims=True)

    small[2].start()
    low_sum[...] = jnp.zeros_like(low_sum)

    @pl.loop(0, blocks)
    def _(b):
        cols = pl.ds(pl.multiple_of(b * WIDE, WIDE), WIDE)
        d_crossed = nt(d_hidden_out[...], h[cols, :])
        d_proj = d_crossed * of_block(b)
        cross_bias_grad[:, cols] = jnp.sum(d_proj, axis=0, keepdims=True)
        rounded = d_proj.astype(BF)
        put(proj_low, b, rounded)
        low_sum[...] += nt(rounded, u[:, cols])
        held[:, cols] = d_crossed * (held[:, cols] + 1.0)
        store(1, proj_low, proj_hbm, b).start()

    low_grad_out[...] = low_sum[...].astype(BF)
    small[1].start()
    stores = list(small)
    for b in range(blocks):
        stores += [store(0, crossed, crossed_hbm, b), store(1, proj_low, proj_hbm, b)]
    for b in range(blocks):
        slots = range(b * per_block, (b + 1) * per_block)
        places = [pl.ds(pl.multiple_of(fmap[s] * width, width), width) for s in slots]
        kept = jnp.concatenate([held[:, place] for place in places], axis=1)
        right = jnp.concatenate([v[place, :] for place in places], axis=0)
        result = (kept + nt(low_grad_out[...], right)).astype(BF)
        put(d_inter, b, result)
        copy = store(2, d_inter, back, b)
        copy.start()
        stores.append(copy)
    for copy in stores:
        copy.wait()


def dense(fmap, received, labels, v, u, cross_bias, h, hidden_bias, out_weight, scale):
    features, batch, width = received.shape
    total_width = features * width
    rank = v.shape[1]
    units = h.shape[1]
    vmem = pl.BlockSpec(memory_space=pltpu.VMEM)
    smem = pl.BlockSpec(memory_space=pltpu.SMEM)
    hbm = pl.BlockSpec(memory_space=pltpu.HBM)
    return pl.pallas_call(
        functools.partial(dense_kernel, scale),
        name="dense",
        in_specs=[smem, vmem, vmem, hbm, hbm, vmem, hbm, vmem, vmem],
        out_specs=[hbm] * 6 + [vmem] * 3,
        out_shape=[
            jax.ShapeDtypeStruct(received.shape, BF),
            jax.ShapeDtypeStruct(received.shape, BF),
            jax.ShapeDtypeStruct(received.shape, BF),
            jax.ShapeDtypeStruct((batch, rank), BF),
            jax.ShapeDtypeStruct((batch, rank), BF),
            jax.ShapeDtypeStruct((batch, units), BF),
            jax.ShapeDtypeStruct((1, total_width), F32),
            jax.ShapeDtypeStruct((1, units), F32),
            jax.ShapeDtypeStruct((1, units), F32),
        ],
        scratch_shapes=[
            pltpu.VMEM(received.shape, BF),
            pltpu.VMEM(received.shape, BF),
            pltpu.VMEM((batch, total_width), F32),
            pltpu.VMEM(received.shape, BF),
            pltpu.VMEM(v.shape, BF),
            pltpu.VMEM(u.shape, BF),
            pltpu.VMEM(h.shape, BF),
            pltpu.VMEM((batch, rank), BF),
            pltpu.VMEM((batch, rank), BF),
            pltpu.VMEM((batch, units), BF),
            pltpu.VMEM((batch, units), F32),
            pltpu.VMEM((batch, rank), F32),
            pltpu.SMEM((features,), jnp.int32),
            pltpu.SemaphoreType.DMA((3,)),
            pltpu.SemaphoreType.DMA((3,)),
            pltpu.SemaphoreType.DMA((3, total_width // WIDE)),
        ],
        compiler_params=pltpu.CompilerParams(vmem_limit_bytes=DENSE_VMEM),
    )(fmap, received, labels, v, u, cross_bias, h, hidden_bias, out_weight)


def gradients_kernel(
    order,
    place,
    fmap,
    received,
    crossed,
    proj,
    low_hbm,
    low_grad_hbm,
    d_hidden_hbm,
    cross_bias_grad,
    hidden_bias_grad,
    out_weight_grad,
    *rest,
):
    parts, chunks = len(order), len(ORDER)
    outs = rest[: 2 * parts]
    crossed_in, proj_in, low, low_grad, d_hidden = rest[2 * parts : 2 * parts + 5]
    low_t, low_grad_t, d_hidden_t, small, keep, send = rest[2 * parts + 5 : -4]
    slot_of, small_sems, wide_sems, out_sems = rest[-4:]
    features = fmap.shape[0]
    width = keep.shape[-1]
    rank = low_t.shape[0]
    each = features // chunks
    share = each // PAIR

    smalls = [
        pltpu.make_async_copy(source, target, small_sems.at[i])
        for i, (source, target) in enumerate(
            ((low_hbm, low), (low_grad_hbm, low_grad), (d_hidden_hbm, d_hidden))
        )
    ]
    for copy in smalls:
        copy.start()
    for s in range(features):
        slot_of[fmap[s]] = s
    loads = []
    for part, offset in enumerate(order):
        base = lax.rem(place[1] + offset, chunks) * each
        span = pl.ds(part * each, each)
        copies = [
            pltpu.make_async_copy(crossed.at[pl.ds(base, each)], crossed_in.at[span], wide_sems.at[0, part]),
            pltpu.make_async_copy(proj.at[pl.ds(base, each)], proj_in.at[span], wide_sems.at[1, part]),
        ]
        loads.append(copies)
    for copy in loads[0]:
        copy.start()
    for copy in smalls:
        copy.wait()

    low_t[...] = low[...].astype(F32).T.astype(BF)
    low_grad_t[...] = low_grad[...].astype(F32).T.astype(BF)
    d_hidden_t[...] = d_hidden[...].astype(F32).T.astype(BF)
    quarters = 4
    units = hidden_bias_grad.shape[1]
    per = units // (features * quarters)
    mine = lax.broadcasted_iota(jnp.int32, (features, units), 0)
    unit = lax.broadcasted_iota(jnp.int32, (features, units), 1)
    mine = unit // (per * quarters) == mine
    unit = lax.broadcasted_iota(jnp.int32, (units, width), 0)
    lane = lax.broadcasted_iota(jnp.int32, (units, width), 1)
    within = unit % (per * quarters)
    spread = (within // per * (width // quarters) + within % per == lane).astype(F32)
    for i, grad in enumerate((hidden_bias_grad, out_weight_grad)):
        small[i] = jnp.dot(
            jnp.where(mine, grad[...], 0.0),
            spread,
            preferred_element_type=F32,
            precision=lax.Precision.HIGHEST,
        )

    def stores(part, k):
        span, place_out = pl.ds(part * each + k * PAIR, PAIR), pl.ds(k * PAIR, PAIR)
        return [
            pltpu.make_async_copy(source.at[span], outs[i].at[place_out], out_sems.at[i, k])
            for i, source in ((parts + part, send), (part, keep))
        ]

    line = lax.broadcasted_iota(jnp.int32, (EXTRA, width), 0)
    nothing = jnp.zeros((EXTRA, width), BF)
    first = place[0] == 0

    for part, offset in enumerate(order):
        for copy in loads[part]:
            copy.wait()
        if part + 1 < parts:
            for copy in loads[part + 1]:
                copy.start()

        @pl.loop(0, share)
        def _(k, part=part, offset=offset):
            base = lax.rem(place[1] + offset, chunks) * each + k * PAIR
            n = part * each + k * PAIR

            def product(left, *right):
                both = jnp.concatenate(right, axis=1)
                return jnp.dot(left[...], both, preferred_element_type=F32).astype(BF)

            of_v = product(low_grad_t, *[received[slot_of[base + i]] for i in range(PAIR)])
            of_u = product(low_t, *[proj_in[n + i] for i in range(PAIR)])
            of_h = product(d_hidden_t, *[crossed_in[n + i] for i in range(PAIR)])

            def fill(one, other):
                for i in range(PAIR):
                    lanes = slice(i * width, (i + 1) * width)
                    f = base + i
                    cross = cross_bias_grad[:, pl.ds(pl.multiple_of(f * width, width), width)]
                    extra = jnp.where(line == 0, cross, 0.0)
                    for j in range(2):
                        extra = jnp.where(line == j + 1, small[j, pl.ds(f, 1), :], extra)
                    one[n + i, 0, pl.ds(0, rank), :] = of_v[:, lanes]
                    one[n + i, 0, pl.ds(rank, EXTRA), :] = extra.astype(BF)
                    one[n + i, 1, pl.ds(0, rank), :] = of_u[:, lanes]
                    one[n + i, 1, pl.ds(rank, EXTRA), :] = nothing
                    other[n + i, 0, pl.ds(0, rank), :] = of_h[:rank, lanes]
                    other[n + i, 0, pl.ds(rank, EXTRA), :] = nothing
                    other[n + i, 1, pl.ds(0, rank), :] = of_h[rank:, lanes]
                    other[n + i, 1, pl.ds(rank, EXTRA), :] = nothing

            @pl.when(first)
            def _():
                fill(keep, send)

            @pl.when(jnp.logical_not(first))
            def _():
                fill(send, keep)

            for copy in stores(part, k):
                copy.start()

    for part in range(parts):
        for k in range(share):
            for copy in stores(part, k):
                copy.wait()


def gradients(order, place, fmap, received, crossed, proj, low, low_grad, d_hidden, *small):
    features, batch, width = received.shape
    rank, units = low.shape[1], d_hidden.shape[1]
    parts = len(order)
    held = features // len(ORDER) * parts
    part = jax.ShapeDtypeStruct((features // len(ORDER), 2, rank + EXTRA, width), BF)
    vmem = pl.BlockSpec(memory_space=pltpu.VMEM)
    smem = pl.BlockSpec(memory_space=pltpu.SMEM)
    hbm = pl.BlockSpec(memory_space=pltpu.HBM)
    outs = pl.pallas_call(
        functools.partial(gradients_kernel, order),
        name="gradients",
        in_specs=[smem, smem, vmem] + [hbm] * 5 + [vmem] * 3,
        out_specs=[hbm] * (2 * parts),
        out_shape=[part] * (2 * parts),
        scratch_shapes=[pltpu.VMEM((held, batch, width), BF)] * 2
        + [
            pltpu.VMEM((batch, rank), BF),
            pltpu.VMEM((batch, rank), BF),
            pltpu.VMEM((batch, units), BF),
            pltpu.VMEM((rank, batch), BF),
            pltpu.VMEM((rank, batch), BF),
            pltpu.VMEM((units, batch), BF),
            pltpu.VMEM((2, features, width), F32),
            pltpu.VMEM((held, 2, rank + EXTRA, width), BF),
            pltpu.VMEM((held, 2, rank + EXTRA, width), BF),
            pltpu.SMEM((features,), jnp.int32),
            pltpu.SemaphoreType.DMA((3,)),
            pltpu.SemaphoreType.DMA((2, parts)),
            pltpu.SemaphoreType.DMA((2 * parts, features // len(ORDER) // PAIR)),
        ],
        compiler_params=pltpu.CompilerParams(vmem_limit_bytes=GRADIENTS_VMEM),
        cost_estimate=pl.CostEstimate(
            flops=2 * batch * held * width * (2 * rank + units),
            bytes_accessed=held << 19,
            transcendentals=0,
        ),
    )(place, fmap, received, crossed, proj, low, low_grad, d_hidden, *small)
    return outs[:parts], outs[parts:]


def fold_kernel(own, swapped, from_following, from_preceding, out):
    features, _, lines, width = own.shape
    quarters = out.shape[0] // features
    rank = lines - EXTRA

    @pl.loop(0, features)
    def _(f):
        total = own[f].astype(F32) + swapped[f].astype(F32)
        total = total + from_following[f].astype(F32) + from_preceding[f].astype(F32)
        filler = jnp.zeros((width - EXTRA, width), F32)
        extra = jnp.concatenate([total[0, rank:], filler], axis=0)
        across = [total[0, :rank].T, total[1, :rank].T, extra.T]
        across = jnp.concatenate(across, axis=1).astype(BF)
        for j in range(quarters):
            out[f * quarters + j] = across[j * width // quarters : (j + 1) * width // quarters]


def fold(quarters, *parts):
    features, _, lines, width = parts[0].shape
    vmem = pl.BlockSpec(memory_space=pltpu.VMEM)
    shape = (features * quarters, width // quarters, 2 * (lines - EXTRA) + width)
    return pl.pallas_call(
        fold_kernel,
        name="fold",
        in_specs=[vmem] * 4,
        out_specs=vmem,
        out_shape=jax.ShapeDtypeStruct(shape, BF),
        compiler_params=pltpu.CompilerParams(vmem_limit_bytes=SMALL_VMEM),
    )(*parts)


def finish_kernel(pieces, grad_v, grad_u, grad_h, cross_bias, hidden_bias, out_weight):
    sources = pieces.shape[0]
    rank = grad_v.shape[1]
    sums = []
    for core in range(2):
        total = pieces[core].astype(F32)
        for source in range(core + 2, sources, 2):
            total = total + pieces[source].astype(F32)
        sums.append(total)
    grad_v[...] = sums[0][:, :rank]
    grad_u[...] = sums[0][:, rank : 2 * rank]
    grad_h[...] = sums[1][:, : 2 * rank]
    small = sums[0][:, 2 * rank :].T
    cross_bias[...] = small[0:1]
    hidden_bias[...] = small[1:2, : hidden_bias.shape[1]]
    out_weight[...] = small[2:3, : out_weight.shape[1]]


def finish(pieces, rank, units, per):
    share = pieces.shape[1]
    vmem = pl.BlockSpec(memory_space=pltpu.VMEM)
    shapes = ((share, rank), (share, rank), (share, units), (1, share), (1, per), (1, per))
    return pl.pallas_call(
        finish_kernel,
        name="finish",
        in_specs=[vmem],
        out_specs=[vmem] * 6,
        out_shape=[jax.ShapeDtypeStruct(shape, F32) for shape in shapes],
        compiler_params=pltpu.CompilerParams(vmem_limit_bytes=SMALL_VMEM),
    )(pieces)


def neighbours(axis):
    size = lax.axis_size(axis)
    up = [(i, (i + 1) % size) for i in range(size)]
    down = [(i, (i - 1) % size) for i in range(size)]
    return (
        lambda value: lax.ppermute(value, axis, up),
        lambda value: lax.ppermute(value, axis, down),
    )


def add(*terms):
    total = terms[0].astype(F32)
    for term in terms[1:]:
        total = total + term.astype(F32)
    return total.astype(BF)


def ring_parts(axis, opposite, following, preceding):
    up, down = neighbours(axis)
    passed = (down(opposite[0]), up(opposite[1]))
    from_following = down(jnp.concatenate([add(preceding[0], passed[0]), preceding[1]], axis=0))
    from_preceding = up(jnp.concatenate([following[0], add(following[1], passed[1])], axis=0))
    return from_following, from_preceding


def ring_spread(axis, own):
    up, down = neighbours(axis)
    preceding, following = up(own), down(own)
    half = own.shape[0] // 2
    return own, following, down(following[:half]), up(preceding[half:]), preceding


def body(
    embedding_table,
    touched_blocks,
    bag_index,
    bag_count,
    feature_map,
    labels,
    v_weight,
    u_weight,
    cross_bias,
    hidden_weight,
    hidden_bias,
    out_weight,
):
    dp = ("x", "zh", "zl", "core")
    features = feature_map.shape[0]
    rows, width = embedding_table.shape
    samples = bag_index.shape[1]
    tile = samples // touched_blocks.shape[1]
    batch = labels.shape[0]
    rank = v_weight.shape[1]
    units = hidden_weight.shape[1]
    roles = lax.axis_size("role")
    total = roles * lax.axis_size(dp) * batch
    core = lax.axis_index("core")
    role = lax.axis_index("role")

    touched = touched_blocks[0].T
    pooled, incidence = pool(touched, embedding_table, bag_index[0].T, bag_count[0].T, tile)
    received = lax.all_to_all(
        pooled.reshape(features, batch, width), dp, split_axis=0, concat_axis=0, tiled=True
    )
    back, crossed, proj, low, low_grad, d_hidden, cross_g, hidden_g, out_g = dense(
        feature_map,
        received,
        labels.reshape(batch, 1),
        v_weight,
        u_weight,
        cross_bias.reshape(1, -1),
        hidden_weight,
        hidden_bias.reshape(1, -1),
        out_weight.reshape(1, -1),
        LOSS_SCALE / total,
    )
    returned = lax.all_to_all(back, dp, split_axis=0, concat_axis=0, tiled=True)

    quarters = 4
    share = width // quarters
    per = units // (features * quarters)

    swap = [(0, 1), (1, 0)]
    each = features // roles
    keep, send = gradients(
        ORDER,
        jnp.stack([core, role]),
        feature_map,
        received,
        crossed,
        proj,
        low,
        low_grad,
        d_hidden,
        cross_g,
        hidden_g,
        out_g,
    )
    others = [lax.ppermute(sent, "core", [(0, 1), (1, 0)]) for sent in send]
    halves = []
    for mine, other in zip(keep[:3], others):
        cuts = (slice(0, each // 2), slice(each // 2, each))
        halves.append([add(mine[cut], other[cut]) for cut in cuts])
    local = scatter(touched, incidence, returned.reshape(samples, width), rows, roles)
    parts = lax.all_to_all(local, "role", split_axis=0, concat_axis=0, tiled=True)
    quarters = 4
    folded = fold(quarters, keep[3], others[3], *ring_parts("role", *halves))
    folded, parts = lax.optimization_barrier((folded, parts))
    pieces = lax.all_to_all(folded, dp, split_axis=0, concat_axis=0, tiled=True)
    per = units // (features * quarters)
    grad_v, grad_u, grad_h, grad_cb, grad_hb, grad_ow = finish(pieces, rank, units, per)
    part = add(*parts)
    table_grad = spread_rows(role.reshape(1), ring_spread("role", part), roles)
    return (
        table_grad,
        grad_v,
        grad_u.T,
        grad_cb.reshape(-1),
        grad_h,
        grad_hb.reshape(-1),
        grad_ow.reshape(-1),
    )


def solution(mesh):
    fine = Mesh(mesh.devices.reshape(4, 4, 2, 2, 2), ("role", "x", "zh", "zl", "core"))
    dp = ("x", "zh", "zl", "core")
    everywhere = ("role",) + dp
    return jax.shard_map(
        body,
        mesh=fine,
        in_specs=(
            P(dp, None),
            P(dp, "role", None),
            P(dp, "role", None),
            P(dp, "role", None),
            P(),
            P(everywhere),
            P(),
            P(),
            P(),
            P(),
            P(),
            P(),
        ),
        out_specs=(
            P(dp, None),
            P(everywhere, None),
            P(None, everywhere),
            P(everywhere),
            P(everywhere, None),
            P(everywhere),
            P(everywhere),
        ),
        check_vma=False,
    )
```

```python
import functools

import jax
import jax.numpy as jnp
from jax import lax
from jax.experimental import pallas as pl
from jax.experimental.pallas import tpu as pltpu
from jax.sharding import Mesh
from jax.sharding import PartitionSpec as P

BLK = 8
LOSS_SCALE = 65536.0
STEP_TILES = 24
WIDE = 2048
EXTRA = 16
PAIR = 4
ORDER = (2, 1, 3, 0)
VMEM = 60 << 20
POOL_VMEM = VMEM
DENSE_VMEM = 52 << 20
GRADIENTS_VMEM = 52 << 20
SMALL_VMEM = 40 << 20
SCATTER_VMEM = 52 << 20

BF = jnp.bfloat16
F32 = jnp.float32


def nt(left, right):
    return lax.dot_general(left, right, (((1,), (1,)), ((), ())), preferred_element_type=F32)


def pool_kernel(touched, table, index, count, pooled, incidence, *scratch):
    rows16, rows32, index_in, count_in, held, tiles_held, table_sem, in_sems, out_sems = scratch
    tiles, tile, _ = incidence.shape
    steps = tiles // STEP_TILES
    span = STEP_TILES * tile

    def loads(step):
        part = pl.ds(pl.multiple_of(step * span, span), span)
        return (
            pltpu.make_async_copy(index.at[:, part], index_in.at[:, part], in_sems.at[0, step]),
            pltpu.make_async_copy(count.at[:, part], count_in.at[:, part], in_sems.at[1, step]),
        )

    def stores(step):
        part = pl.ds(pl.multiple_of(step * span, span), span)
        some = pl.ds(step * STEP_TILES, STEP_TILES)
        return (
            pltpu.make_async_copy(held.at[part], pooled.at[part], out_sems.at[0, step]),
            pltpu.make_async_copy(tiles_held.at[some], incidence.at[some], out_sems.at[1, step]),
        )

    whole = pltpu.make_async_copy(table, rows16, table_sem)
    whole.start()
    for step in range(steps):
        for copy in loads(step):
            copy.start()
    whole.wait()
    rows32[...] = rows16[...].astype(F32)
    listed = lax.broadcasted_iota(jnp.int32, (tile, tile), 0).astype(BF)

    @pl.loop(0, steps)
    def _(step):
        for copy in loads(step):
            copy.wait()
        for i in range(STEP_TILES):
            t = step * STEP_TILES + i
            part = pl.ds(pl.multiple_of(t * tile, tile), tile)
            idx = index_in[:, part].astype(BF)
            cnt = count_in[:, part].astype(BF)
            total = jnp.zeros((tile, tile), BF)
            for j in range(index.shape[0]):
                total += jnp.where(idx[j : j + 1] == listed, cnt[j : j + 1], jnp.zeros((), BF))
            tiles_held[t] = total
            blocks = [
                rows32[pl.ds(pl.multiple_of(touched[k, t] * BLK, BLK), BLK), :]
                for k in range(touched.shape[0])
            ]
            picked = jnp.concatenate(blocks, axis=0).astype(BF)
            held[part, :] = lax.dot_general(
                total, picked, (((0,), (0,)), ((), ())), preferred_element_type=F32
            ).astype(BF)
        for copy in stores(step):
            copy.start()

    for step in range(steps):
        for copy in stores(step):
            copy.wait()


def pool(touched, table, index, count, tile):
    hot, samples = index.shape
    tiles = samples // tile
    width = table.shape[1]
    steps = tiles // STEP_TILES
    hbm = pl.BlockSpec(memory_space=pltpu.HBM)
    return pl.pallas_call(
        pool_kernel,
        name="pool",
        in_specs=[pl.BlockSpec(memory_space=pltpu.SMEM), hbm, hbm, hbm],
        out_specs=[hbm, hbm],
        out_shape=[
            jax.ShapeDtypeStruct((samples, width), BF),
            jax.ShapeDtypeStruct((tiles, tile, tile), BF),
        ],
        scratch_shapes=[
            pltpu.VMEM(table.shape, BF),
            pltpu.VMEM(table.shape, F32),
            pltpu.VMEM(index.shape, jnp.int32),
            pltpu.VMEM(count.shape, jnp.int32),
            pltpu.VMEM((samples, width), BF),
            pltpu.VMEM((tiles, tile, tile), BF),
            pltpu.SemaphoreType.DMA,
            pltpu.SemaphoreType.DMA((2, steps)),
            pltpu.SemaphoreType.DMA((2, steps)),
        ],
        compiler_params=pltpu.CompilerParams(vmem_limit_bytes=POOL_VMEM),
    )(touched, table, index, count)


def scatter_kernel(touched, incidence, grad, out, *scratch):
    sums, (tiles_in, held, sems, out_sems) = scratch[:-4], scratch[-4:]
    tiles, tile, _ = incidence.shape
    chunks, rows, _ = out.shape
    steps = tiles // STEP_TILES

    def load(step):
        part = pl.ds(step * STEP_TILES, STEP_TILES)
        return pltpu.make_async_copy(incidence.at[part], tiles_in.at[part], sems.at[step])

    for step in range(steps):
        load(step).start()
    for acc in sums:
        acc[...] = jnp.zeros_like(acc)

    @pl.loop(0, steps)
    def _(step):
        load(step).wait()
        for i in range(STEP_TILES):
            t = step * STEP_TILES + i
            product = jnp.dot(
                tiles_in[t], grad[pl.ds(t * tile, tile), :], preferred_element_type=F32
            )
            for k in range(touched.shape[0]):
                acc = sums[k % len(sums)]
                place = pl.ds(pl.multiple_of(touched[k, t] * BLK, BLK), BLK)
                acc[place, :] += product[k * BLK : (k + 1) * BLK]

    for i in range(chunks):
        place = pl.ds(i * rows, rows)
        total = sums[0][place, :]
        for acc in sums[1:]:
            total = total + acc[place, :]
        held[i] = total.astype(out.dtype)
        pltpu.make_async_copy(held.at[i], out.at[i], out_sems.at[i]).start()
    for i in range(chunks):
        pltpu.make_async_copy(held.at[i], out.at[i], out_sems.at[i]).wait()


def scatter(touched, incidence, grad, rows, chunks):
    tiles, tile, _ = incidence.shape
    width = grad.shape[1]
    steps = tiles // STEP_TILES
    smem = pl.BlockSpec(memory_space=pltpu.SMEM)
    hbm = pl.BlockSpec(memory_space=pltpu.HBM)
    vmem = pl.BlockSpec(memory_space=pltpu.VMEM)
    return pl.pallas_call(
        scatter_kernel,
        name="scatter",
        in_specs=[smem, hbm, vmem],
        out_specs=hbm,
        out_shape=jax.ShapeDtypeStruct((chunks, rows // chunks, width), BF),
        scratch_shapes=[pltpu.VMEM((rows, width), F32)] * 4
        + [
            pltpu.VMEM(incidence.shape, BF),
            pltpu.VMEM((chunks, rows // chunks, width), BF),
            pltpu.SemaphoreType.DMA((steps,)),
            pltpu.SemaphoreType.DMA((chunks,)),
        ],
        compiler_params=pltpu.CompilerParams(vmem_limit_bytes=SCATTER_VMEM),
        cost_estimate=pl.CostEstimate(flops=1 << 33, bytes_accessed=8 << 20, transcendentals=0),
    )(touched, incidence, grad)


def spread_kernel(role, own, following, opposite_a, opposite_b, preceding, out):
    rows = own.shape[0]
    half = rows // 2
    chunks = out.shape[0] // rows

    def place(offset, size, piece):
        first = lax.rem(role[0] + offset, chunks) * rows
        out[pl.ds(pl.multiple_of(first, rows) + size, piece.shape[0]), :] = piece[...].astype(F32)

    place(0, 0, own)
    place(1, 0, following)
    place(2, 0, opposite_a)
    place(2, half, opposite_b)
    place(3, 0, preceding)


def spread_rows(role, pieces, chunks):
    rows, width = pieces[0].shape
    vmem = pl.BlockSpec(memory_space=pltpu.VMEM)
    return pl.pallas_call(
        spread_kernel,
        name="spread_rows",
        in_specs=[pl.BlockSpec(memory_space=pltpu.SMEM)] + [vmem] * 5,
        out_specs=vmem,
        out_shape=jax.ShapeDtypeStruct((chunks * rows, width), F32),
        compiler_params=pltpu.CompilerParams(vmem_limit_bytes=SMALL_VMEM),
    )(role, *pieces)


def dense_kernel(
    scale,
    fmap,
    received,
    labels,
    v_hbm,
    u_hbm,
    cross_bias,
    h_hbm,
    hidden_bias,
    out_weight,
    back,
    crossed_hbm,
    proj_hbm,
    low_hbm,
    low_grad_hbm,
    d_hidden_hbm,
    cross_bias_grad,
    hidden_bias_grad,
    out_weight_grad,
    crossed,
    proj_low,
    held,
    d_inter,
    v,
    u,
    h,
    low_out,
    low_grad_out,
    d_hidden_out,
    hidden,
    low_sum,
    slot_of,
    weight_sems,
    small_sems,
    wide_sems,
):
    features, batch, width = received.shape
    total_width = features * width
    blocks = total_width // WIDE
    per_block = WIDE // width

    weights = [
        pltpu.make_async_copy(source, target, weight_sems.at[i])
        for i, (source, target) in enumerate(((v_hbm, v), (u_hbm, u), (h_hbm, h)))
    ]
    weights[0].start()
    weights[1].start()
    weights[2].start()

    def store(row, source, target, b):
        part = pl.ds(b * per_block, per_block)
        return pltpu.make_async_copy(source.at[part], target.at[part], wide_sems.at[row, b])

    def of_block(b):
        slots = [slot_of[b * per_block + i] for i in range(per_block)]
        return jnp.concatenate([received[slot] for slot in slots], axis=1).astype(F32)

    def put(target, b, value):
        for i in range(per_block):
            target[b * per_block + i] = value[:, i * width : (i + 1) * width]

    small = [
        pltpu.make_async_copy(source, target, small_sems.at[i])
        for i, (source, target) in enumerate(
            ((low_out, low_hbm), (low_grad_out, low_grad_hbm), (d_hidden_out, d_hidden_hbm))
        )
    ]
    for s in range(features):
        slot_of[fmap[s]] = s
    low_sum[...] = jnp.zeros_like(low_sum)
    hidden[...] = jnp.broadcast_to(hidden_bias[...], hidden.shape)
    hidden_bias_grad[...] = jnp.zeros_like(hidden_bias_grad)
    out_weight_grad[...] = jnp.zeros_like(out_weight_grad)
    weights[0].wait()
    for b in range(blocks):
        slots = range(b * per_block, (b + 1) * per_block)
        places = [pl.ds(pl.multiple_of(fmap[s] * width, width), width) for s in slots]
        left = jnp.concatenate([received[s] for s in slots], axis=1)
        right = jnp.concatenate([v[place, :] for place in places], axis=0)
        low_sum[...] += jnp.dot(left, right, preferred_element_type=F32)

    low_out[...] = low_sum[...].astype(BF)
    small[0].start()
    weights[1].wait()
    weights[2].wait()

    @pl.loop(0, blocks)
    def _(b):
        cols = pl.ds(pl.multiple_of(b * WIDE, WIDE), WIDE)
        projected = (
            jnp.dot(low_out[...], u[:, cols], preferred_element_type=F32) + cross_bias[:, cols]
        )
        held[:, cols] = projected
        x = of_block(b)
        product = (x * projected + x).astype(BF)
        put(crossed, b, product)
        hidden[...] += jnp.dot(product, h[cols, :], preferred_element_type=F32)
        store(0, crossed, crossed_hbm, b).start()

    chunk = 192

    @pl.loop(0, batch // chunk)
    def _(r):
        rows = pl.ds(pl.multiple_of(r * chunk, chunk), chunk)
        pre = hidden[rows, :]
        gate = jax.nn.sigmoid(pre)
        act = (pre * gate).astype(BF).astype(F32)
        weight = out_weight[...].astype(F32)
        logit = jnp.sum(act * weight, axis=1, keepdims=True)
        d_logit = (scale * (jax.nn.sigmoid(logit) - labels[rows, :].astype(F32))).astype(BF)
        d_logit = d_logit.astype(F32)
        d_hidden = (d_logit * weight * (gate * (1.0 + pre * (1.0 - gate)))).astype(BF)
        d_hidden_out[rows, :] = d_hidden
        hidden_bias_grad[...] += jnp.sum(d_hidden.astype(F32), axis=0, keepdims=True)
        out_weight_grad[...] += jnp.sum(d_logit * act, axis=0, keepdims=True)

    small[2].start()
    low_sum[...] = jnp.zeros_like(low_sum)

    @pl.loop(0, blocks)
    def _(b):
        cols = pl.ds(pl.multiple_of(b * WIDE, WIDE), WIDE)
        d_crossed = nt(d_hidden_out[...], h[cols, :])
        d_proj = d_crossed * of_block(b)
        cross_bias_grad[:, cols] = jnp.sum(d_proj, axis=0, keepdims=True)
        rounded = d_proj.astype(BF)
        put(proj_low, b, rounded)
        low_sum[...] += nt(rounded, u[:, cols])
        held[:, cols] = d_crossed * (held[:, cols] + 1.0)
        store(1, proj_low, proj_hbm, b).start()

    low_grad_out[...] = low_sum[...].astype(BF)
    small[1].start()
    stores = list(small)
    for b in range(blocks):
        stores += [store(0, crossed, crossed_hbm, b), store(1, proj_low, proj_hbm, b)]
    for b in range(blocks):
        slots = range(b * per_block, (b + 1) * per_block)
        places = [pl.ds(pl.multiple_of(fmap[s] * width, width), width) for s in slots]
        kept = jnp.concatenate([held[:, place] for place in places], axis=1)
        right = jnp.concatenate([v[place, :] for place in places], axis=0)
        result = (kept + nt(low_grad_out[...], right)).astype(BF)
        put(d_inter, b, result)
        copy = store(2, d_inter, back, b)
        copy.start()
        stores.append(copy)
    for copy in stores:
        copy.wait()


def dense(fmap, received, labels, v, u, cross_bias, h, hidden_bias, out_weight, scale):
    features, batch, width = received.shape
    total_width = features * width
    rank = v.shape[1]
    units = h.shape[1]
    vmem = pl.BlockSpec(memory_space=pltpu.VMEM)
    smem = pl.BlockSpec(memory_space=pltpu.SMEM)
    hbm = pl.BlockSpec(memory_space=pltpu.HBM)
    return pl.pallas_call(
        functools.partial(dense_kernel, scale),
        name="dense",
        in_specs=[smem, vmem, vmem, hbm, hbm, vmem, hbm, vmem, vmem],
        out_specs=[hbm] * 6 + [vmem] * 3,
        out_shape=[
            jax.ShapeDtypeStruct(received.shape, BF),
            jax.ShapeDtypeStruct(received.shape, BF),
            jax.ShapeDtypeStruct(received.shape, BF),
            jax.ShapeDtypeStruct((batch, rank), BF),
            jax.ShapeDtypeStruct((batch, rank), BF),
            jax.ShapeDtypeStruct((batch, units), BF),
            jax.ShapeDtypeStruct((1, total_width), F32),
            jax.ShapeDtypeStruct((1, units), F32),
            jax.ShapeDtypeStruct((1, units), F32),
        ],
        scratch_shapes=[
            pltpu.VMEM(received.shape, BF),
            pltpu.VMEM(received.shape, BF),
            pltpu.VMEM((batch, total_width), F32),
            pltpu.VMEM(received.shape, BF),
            pltpu.VMEM(v.shape, BF),
            pltpu.VMEM(u.shape, BF),
            pltpu.VMEM(h.shape, BF),
            pltpu.VMEM((batch, rank), BF),
            pltpu.VMEM((batch, rank), BF),
            pltpu.VMEM((batch, units), BF),
            pltpu.VMEM((batch, units), F32),
            pltpu.VMEM((batch, rank), F32),
            pltpu.SMEM((features,), jnp.int32),
            pltpu.SemaphoreType.DMA((3,)),
            pltpu.SemaphoreType.DMA((3,)),
            pltpu.SemaphoreType.DMA((3, total_width // WIDE)),
        ],
        compiler_params=pltpu.CompilerParams(vmem_limit_bytes=DENSE_VMEM),
    )(fmap, received, labels, v, u, cross_bias, h, hidden_bias, out_weight)


def gradients_kernel(
    order,
    place,
    fmap,
    received,
    crossed,
    proj,
    low_hbm,
    low_grad_hbm,
    d_hidden_hbm,
    cross_bias_grad,
    hidden_bias_grad,
    out_weight_grad,
    *rest,
):
    parts, chunks = len(order), len(ORDER)
    outs = rest[: 2 * parts]
    crossed_in, proj_in, low, low_grad, d_hidden = rest[2 * parts : 2 * parts + 5]
    low_t, low_grad_t, d_hidden_t, small, keep, send = rest[2 * parts + 5 : -4]
    slot_of, small_sems, wide_sems, out_sems = rest[-4:]
    features = fmap.shape[0]
    width = keep.shape[-1]
    rank = low_t.shape[0]
    each = features // chunks
    share = each // PAIR

    smalls = [
        pltpu.make_async_copy(source, target, small_sems.at[i])
        for i, (source, target) in enumerate(
            ((low_hbm, low), (low_grad_hbm, low_grad), (d_hidden_hbm, d_hidden))
        )
    ]
    for copy in smalls:
        copy.start()
    for s in range(features):
        slot_of[fmap[s]] = s
    loads = []
    for part, offset in enumerate(order):
        base = lax.rem(place[1] + offset, chunks) * each
        span = pl.ds(part * each, each)
        copies = [
            pltpu.make_async_copy(crossed.at[pl.ds(base, each)], crossed_in.at[span], wide_sems.at[0, part]),
            pltpu.make_async_copy(proj.at[pl.ds(base, each)], proj_in.at[span], wide_sems.at[1, part]),
        ]
        loads.append(copies)
    for copy in loads[0]:
        copy.start()
    for copy in smalls:
        copy.wait()

    low_t[...] = low[...].astype(F32).T.astype(BF)
    low_grad_t[...] = low_grad[...].astype(F32).T.astype(BF)
    d_hidden_t[...] = d_hidden[...].astype(F32).T.astype(BF)
    quarters = 4
    units = hidden_bias_grad.shape[1]
    per = units // (features * quarters)
    mine = lax.broadcasted_iota(jnp.int32, (features, units), 0)
    unit = lax.broadcasted_iota(jnp.int32, (features, units), 1)
    mine = unit // (per * quarters) == mine
    unit = lax.broadcasted_iota(jnp.int32, (units, width), 0)
    lane = lax.broadcasted_iota(jnp.int32, (units, width), 1)
    within = unit % (per * quarters)
    spread = (within // per * (width // quarters) + within % per == lane).astype(F32)
    for i, grad in enumerate((hidden_bias_grad, out_weight_grad)):
        small[i] = jnp.dot(
            jnp.where(mine, grad[...], 0.0),
            spread,
            preferred_element_type=F32,
            precision=lax.Precision.HIGHEST,
        )

    def stores(part, k):
        span, place_out = pl.ds(part * each + k * PAIR, PAIR), pl.ds(k * PAIR, PAIR)
        return [
            pltpu.make_async_copy(source.at[span], outs[i].at[place_out], out_sems.at[i, k])
            for i, source in ((parts + part, send), (part, keep))
        ]

    line = lax.broadcasted_iota(jnp.int32, (EXTRA, width), 0)
    nothing = jnp.zeros((EXTRA, width), BF)
    first = place[0] == 0

    for part, offset in enumerate(order):
        for copy in loads[part]:
            copy.wait()
        if part + 1 < parts:
            for copy in loads[part + 1]:
                copy.start()

        @pl.loop(0, share)
        def _(k, part=part, offset=offset):
            base = lax.rem(place[1] + offset, chunks) * each + k * PAIR
            n = part * each + k * PAIR

            def product(left, *right):
                both = jnp.concatenate(right, axis=1)
                return jnp.dot(left[...], both, preferred_element_type=F32).astype(BF)

            of_v = product(low_grad_t, *[received[slot_of[base + i]] for i in range(PAIR)])
            of_u = product(low_t, *[proj_in[n + i] for i in range(PAIR)])
            of_h = product(d_hidden_t, *[crossed_in[n + i] for i in range(PAIR)])

            def fill(one, other):
                for i in range(PAIR):
                    lanes = slice(i * width, (i + 1) * width)
                    f = base + i
                    cross = cross_bias_grad[:, pl.ds(pl.multiple_of(f * width, width), width)]
                    extra = jnp.where(line == 0, cross, 0.0)
                    for j in range(2):
                        extra = jnp.where(line == j + 1, small[j, pl.ds(f, 1), :], extra)
                    one[n + i, 0, pl.ds(0, rank), :] = of_v[:, lanes]
                    one[n + i, 0, pl.ds(rank, EXTRA), :] = extra.astype(BF)
                    one[n + i, 1, pl.ds(0, rank), :] = of_u[:, lanes]
                    one[n + i, 1, pl.ds(rank, EXTRA), :] = nothing
                    other[n + i, 0, pl.ds(0, rank), :] = of_h[:rank, lanes]
                    other[n + i, 0, pl.ds(rank, EXTRA), :] = nothing
                    other[n + i, 1, pl.ds(0, rank), :] = of_h[rank:, lanes]
                    other[n + i, 1, pl.ds(rank, EXTRA), :] = nothing

            @pl.when(first)
            def _():
                fill(keep, send)

            @pl.when(jnp.logical_not(first))
            def _():
                fill(send, keep)

            for copy in stores(part, k):
                copy.start()

    for part in range(parts):
        for k in range(share):
            for copy in stores(part, k):
                copy.wait()


def gradients(order, place, fmap, received, crossed, proj, low, low_grad, d_hidden, *small):
    features, batch, width = received.shape
    rank, units = low.shape[1], d_hidden.shape[1]
    parts = len(order)
    held = features // len(ORDER) * parts
    part = jax.ShapeDtypeStruct((features // len(ORDER), 2, rank + EXTRA, width), BF)
    vmem = pl.BlockSpec(memory_space=pltpu.VMEM)
    smem = pl.BlockSpec(memory_space=pltpu.SMEM)
    hbm = pl.BlockSpec(memory_space=pltpu.HBM)
    outs = pl.pallas_call(
        functools.partial(gradients_kernel, order),
        name="gradients",
        in_specs=[smem, smem, vmem] + [hbm] * 5 + [vmem] * 3,
        out_specs=[hbm] * (2 * parts),
        out_shape=[part] * (2 * parts),
        scratch_shapes=[pltpu.VMEM((held, batch, width), BF)] * 2
        + [
            pltpu.VMEM((batch, rank), BF),
            pltpu.VMEM((batch, rank), BF),
            pltpu.VMEM((batch, units), BF),
            pltpu.VMEM((rank, batch), BF),
            pltpu.VMEM((rank, batch), BF),
            pltpu.VMEM((units, batch), BF),
            pltpu.VMEM((2, features, width), F32),
            pltpu.VMEM((held, 2, rank + EXTRA, width), BF),
            pltpu.VMEM((held, 2, rank + EXTRA, width), BF),
            pltpu.SMEM((features,), jnp.int32),
            pltpu.SemaphoreType.DMA((3,)),
            pltpu.SemaphoreType.DMA((2, parts)),
            pltpu.SemaphoreType.DMA((2 * parts, features // len(ORDER) // PAIR)),
        ],
        compiler_params=pltpu.CompilerParams(vmem_limit_bytes=GRADIENTS_VMEM),
        cost_estimate=pl.CostEstimate(
            flops=2 * batch * held * width * (2 * rank + units),
            bytes_accessed=held << 19,
            transcendentals=0,
        ),
    )(place, fmap, received, crossed, proj, low, low_grad, d_hidden, *small)
    return outs[:parts], outs[parts:]


def fold_kernel(own, swapped, from_following, from_preceding, out):
    features, _, lines, width = own.shape
    quarters = out.shape[0] // features
    rank = lines - EXTRA

    @pl.loop(0, features)
    def _(f):
        total = own[f].astype(F32) + swapped[f].astype(F32)
        total = total + from_following[f].astype(F32) + from_preceding[f].astype(F32)
        filler = jnp.zeros((width - EXTRA, width), F32)
        extra = jnp.concatenate([total[0, rank:], filler], axis=0)
        across = [total[0, :rank].T, total[1, :rank].T, extra.T]
        across = jnp.concatenate(across, axis=1).astype(BF)
        for j in range(quarters):
            out[f * quarters + j] = across[j * width // quarters : (j + 1) * width // quarters]


def fold(quarters, *parts):
    features, _, lines, width = parts[0].shape
    vmem = pl.BlockSpec(memory_space=pltpu.VMEM)
    shape = (features * quarters, width // quarters, 2 * (lines - EXTRA) + width)
    return pl.pallas_call(
        fold_kernel,
        name="fold",
        in_specs=[vmem] * 4,
        out_specs=vmem,
        out_shape=jax.ShapeDtypeStruct(shape, BF),
        compiler_params=pltpu.CompilerParams(vmem_limit_bytes=SMALL_VMEM),
    )(*parts)


def finish_kernel(pieces, grad_v, grad_u, grad_h, cross_bias, hidden_bias, out_weight):
    sources = pieces.shape[0]
    rank = grad_v.shape[1]
    sums = []
    for core in range(2):
        total = pieces[core].astype(F32)
        for source in range(core + 2, sources, 2):
            total = total + pieces[source].astype(F32)
        sums.append(total)
    grad_v[...] = sums[0][:, :rank]
    grad_u[...] = sums[0][:, rank : 2 * rank]
    grad_h[...] = sums[1][:, : 2 * rank]
    small = sums[0][:, 2 * rank :].T
    cross_bias[...] = small[0:1]
    hidden_bias[...] = small[1:2, : hidden_bias.shape[1]]
    out_weight[...] = small[2:3, : out_weight.shape[1]]


def finish(pieces, rank, units, per):
    share = pieces.shape[1]
    vmem = pl.BlockSpec(memory_space=pltpu.VMEM)
    shapes = ((share, rank), (share, rank), (share, units), (1, share), (1, per), (1, per))
    return pl.pallas_call(
        finish_kernel,
        name="finish",
        in_specs=[vmem],
        out_specs=[vmem] * 6,
        out_shape=[jax.ShapeDtypeStruct(shape, F32) for shape in shapes],
        compiler_params=pltpu.CompilerParams(vmem_limit_bytes=SMALL_VMEM),
    )(pieces)


def neighbours(axis):
    size = lax.axis_size(axis)
    up = [(i, (i + 1) % size) for i in range(size)]
    down = [(i, (i - 1) % size) for i in range(size)]
    return (
        lambda value: lax.ppermute(value, axis, up),
        lambda value: lax.ppermute(value, axis, down),
    )


def add(*terms):
    total = terms[0].astype(F32)
    for term in terms[1:]:
        total = total + term.astype(F32)
    return total.astype(BF)


def ring_parts(axis, opposite, following, preceding):
    up, down = neighbours(axis)
    passed = (down(opposite[0]), up(opposite[1]))
    from_following = down(jnp.concatenate([add(preceding[0], passed[0]), preceding[1]], axis=0))
    from_preceding = up(jnp.concatenate([following[0], add(following[1], passed[1])], axis=0))
    return from_following, from_preceding


def ring_spread(axis, own):
    up, down = neighbours(axis)
    preceding, following = up(own), down(own)
    half = own.shape[0] // 2
    return own, following, down(following[:half]), up(preceding[half:]), preceding


def body(
    embedding_table,
    touched_blocks,
    bag_index,
    bag_count,
    feature_map,
    labels,
    v_weight,
    u_weight,
    cross_bias,
    hidden_weight,
    hidden_bias,
    out_weight,
):
    dp = ("x", "zh", "zl", "core")
    features = feature_map.shape[0]
    rows, width = embedding_table.shape
    samples = bag_index.shape[1]
    tile = samples // touched_blocks.shape[1]
    batch = labels.shape[0]
    rank = v_weight.shape[1]
    units = hidden_weight.shape[1]
    roles = lax.axis_size("role")
    total = roles * lax.axis_size(dp) * batch
    core = lax.axis_index("core")
    role = lax.axis_index("role")

    touched = touched_blocks[0].T
    pooled, incidence = pool(touched, embedding_table, bag_index[0].T, bag_count[0].T, tile)
    received = lax.all_to_all(
        pooled.reshape(features, batch, width), dp, split_axis=0, concat_axis=0, tiled=True
    )
    back, crossed, proj, low, low_grad, d_hidden, cross_g, hidden_g, out_g = dense(
        feature_map,
        received,
        labels.reshape(batch, 1),
        v_weight,
        u_weight,
        cross_bias.reshape(1, -1),
        hidden_weight,
        hidden_bias.reshape(1, -1),
        out_weight.reshape(1, -1),
        LOSS_SCALE / total,
    )
    returned = lax.all_to_all(back, dp, split_axis=0, concat_axis=0, tiled=True)

    quarters = 4
    share = width // quarters
    per = units // (features * quarters)

    swap = [(0, 1), (1, 0)]
    each = features // roles
    keep, send = gradients(
        ORDER,
        jnp.stack([core, role]),
        feature_map,
        received,
        crossed,
        proj,
        low,
        low_grad,
        d_hidden,
        cross_g,
        hidden_g,
        out_g,
    )
    others = [lax.ppermute(sent, "core", [(0, 1), (1, 0)]) for sent in send]
    halves = []
    for mine, other in zip(keep[:3], others):
        cuts = (slice(0, each // 2), slice(each // 2, each))
        halves.append([add(mine[cut], other[cut]) for cut in cuts])
    local = scatter(touched, incidence, returned.reshape(samples, width), rows, roles)
    parts = lax.all_to_all(local, "role", split_axis=0, concat_axis=0, tiled=True)
    quarters = 4
    folded = fold(quarters, keep[3], others[3], *ring_parts("role", *halves))
    folded, parts = lax.optimization_barrier((folded, parts))
    pieces = lax.all_to_all(folded, dp, split_axis=0, concat_axis=0, tiled=True)
    per = units // (features * quarters)
    grad_v, grad_u, grad_h, grad_cb, grad_hb, grad_ow = finish(pieces, rank, units, per)
    part = add(*parts)
    table_grad = spread_rows(role.reshape(1), ring_spread("role", part), roles)
    return (
        table_grad,
        grad_v,
        grad_u.T,
        grad_cb.reshape(-1),
        grad_h,
        grad_hb.reshape(-1),
        grad_ow.reshape(-1),
    )


def solution(mesh):
    fine = Mesh(mesh.devices.reshape(4, 4, 2, 2, 2), ("role", "x", "zh", "zl", "core"))
    dp = ("x", "zh", "zl", "core")
    everywhere = ("role",) + dp
    return jax.shard_map(
        body,
        mesh=fine,
        in_specs=(
            P(dp, None),
            P(dp, "role", None),
            P(dp, "role", None),
            P(dp, "role", None),
            P(),
            P(everywhere),
            P(),
            P(),
            P(),
            P(),
            P(),
            P(),
        ),
        out_specs=(
            P(dp, None),
            P(everywhere, None),
            P(None, everywhere),
            P(everywhere),
            P(everywhere, None),
            P(everywhere),
            P(everywhere),
        ),
        check_vma=False,
    )
```
